32 devices in a mesh: section: 2 (over y), sx: 8 (over z, core), sy: 2 (over x).
Axes of the slice: x: 2, y: 2, z: 4, core: 2. Of those that a mesh axis runs over, the one named last changes fastest.
Arguments:
- previous: float32 [16, 128, 256], P(None, 'sx', 'sy'), may hold values from -3 to 3
- sections: float32 [4, 16, 128, 256], P('section', None, 'sx', 'sy'), may hold values from -3 to 3
- diffusivity: float32 [16, 128, 256], P(None, 'sx', 'sy'), may hold values from 0.3 to 3
- reaction: float32 [16, 128, 256], P(None, 'sx', 'sy'), may hold values from 0.2 to 2
Outputs:
- updated: float32 [4, 16, 128, 256], P('section', None, 'sx', 'sy')
The draws below stay inside these ranges and needn't reach their ends.
All inputs are finite; a program needn't handle non-finite values.
Results may differ from the reference program's by a relative error of at most 0.0003.
Values sent between devices are 32-bit elements; how exact they have to be, the bound alone decides.
A program may use at most 64 MiB of HBM per device.

```python
import math
import jax
import jax.numpy as jnp

NZ = 16
SECTIONS = 4
ITERS = 4
NX = 128
NY = 256


def level_of(rng, shape, split, least, high):
    factor_of, own = 1.0, jax.random.fold_in(rng, 6)
    for axis_at, shards_of in split:
        draws = jnp.exp(jax.random.uniform(jax.random.fold_in(own, axis_at), (shards_of,), jnp.float32, least / len(split), high / len(split)))
        factor_of = factor_of * jnp.repeat(draws, shape[axis_at] // shards_of).reshape([-1 if axis == axis_at else 1 for axis in range(len(shape))])
    return factor_of


def scatter_about(own_key, extent, scale, most, pieces=(), held_as=jnp.bfloat16):
    entries = jax.random.normal(own_key, extent, jnp.float32) * scale
    if len(pieces) > 0:
        entries = level_of(own_key, extent, pieces, -0.22, 0.18) * entries
    return jnp.clip(entries, min=-most, max=most).astype(held_as)


def setup_inputs(seed: int = 0) -> dict:
    key_of = jax.random.split(jax.random.key(seed), 5)
    previous = scatter_about(key_of[0], (NZ, NX, NY), 0.8, 3.0, ((1, 8), (2, 2)), jnp.float32)
    sections = scatter_about(key_of[1], (SECTIONS, NZ, NX, NY), 1.0, 3.0, ((0, 2), (2, 8), (3, 2)), jnp.float32)
    diffusivity = jnp.clip(jnp.exp(math.log(3.0) - 2.3025851 * jax.random.uniform(key_of[2], (NZ, NX, NY), jnp.float32) ** level_of(key_of[2], (NZ, NX, NY), ((1, 8), (2, 2)), -0.2, 0.2)), 0.3, 3.0)
    reaction = jnp.clip(jnp.exp(math.log(2.0) - 2.3025851 * jax.random.uniform(key_of[3], (NZ, NX, NY), jnp.float32) ** level_of(key_of[3], (NZ, NX, NY), ((1, 8), (2, 2)), -0.2, 0.2)), 0.2, 2.0)
    return dict(previous=previous, sections=sections, diffusivity=diffusivity, reaction=reaction)


step_size = 1.0
tiny_value = 1e-6


def invert_table(matrix):
    order_n = len(matrix)
    augmented = [list(matrix[r]) + [1.0 if c == r else 0.0 for c in range(order_n)] for r in range(order_n)]
    for col in range(order_n):
        pivot_row = max(range(col, order_n), key=lambda r: abs(augmented[r][col]))
        augmented[col], augmented[pivot_row] = augmented[pivot_row], augmented[col]
        leading = augmented[col][col]
        augmented[col] = [v / leading for v in augmented[col]]
        for r in range(order_n):
            if r != col:
                factor = augmented[r][col]
                augmented[r] = [a - factor * b for a, b in zip(augmented[r], augmented[col])]
    return [row_values[order_n:] for row_values in augmented]


def table_product(left, right):
    return [[sum(left[i][k] * right[k][j] for k in range(len(right))) for j in range(len(right[0]))] for i in range(len(left))]


def pair_add(first, second):
    return (first[0] + second[0], first[1] + second[1])


def pair_sub(first, second):
    return (first[0] - second[0], first[1] - second[1])


def pair_mul(first, second):
    return (first[0] * second[0] - first[1] * second[1], first[0] * second[1] + first[1] * second[0])


def pair_div(first, second):
    scale_sq = second[0] * second[0] + second[1] * second[1]
    return ((first[0] * second[0] + first[1] * second[1]) / scale_sq, (first[1] * second[0] - first[0] * second[1]) / scale_sq)


def quartic_value(point):
    return (((210.0 * point - 480.0) * point + 360.0) * point - 96.0) * point + 6.0


def bisect_root(lower, upper):
    for count in range(200):
        middle = 0.5 * (lower + upper)
        if (quartic_value(lower) < 0.0) == (quartic_value(middle) < 0.0):
            lower = middle
        else:
            upper = middle
    return 0.5 * (lower + upper)


def radau_tables():
    abscissae = []
    grid_steps = 4000
    for m in range(grid_steps):
        lower = 0.999 * m / grid_steps
        upper = 0.999 * (m + 1) / grid_steps
        if (quartic_value(lower) < 0.0) != (quartic_value(upper) < 0.0):
            abscissae.append(bisect_root(lower, upper))
    abscissae.append(1.0)
    vander = [[abscissae[j] ** k for k in range(4)] for j in range(4)]
    moments = [[abscissae[i] ** (k + 1) / (k + 1) for k in range(4)] for i in range(4)]
    tableau = table_product(moments, invert_table(vander))
    inverse = invert_table(tableau)
    running = [list(row_values) for row_values in inverse]
    coeffs = []
    for k in range(1, 5):
        trace_value = sum(running[i][i] for i in range(4))
        coeffs.append(-trace_value / k)
        shifted_table = [[running[i][j] + (coeffs[-1] if i == j else 0.0) for j in range(4)] for i in range(4)]
        running = table_product(inverse, shifted_table)
    start_point = (0.4, 0.9)
    estimates = [(1.0, 0.0)]
    for k in range(3):
        estimates.append(pair_mul(estimates[-1], start_point))
    for count in range(500):
        for i in range(4):
            value = (1.0, 0.0)
            for coef_value in coeffs:
                value = pair_add(pair_mul(value, estimates[i]), (coef_value, 0.0))
            denom = (1.0, 0.0)
            for j in range(4):
                if j != i:
                    denom = pair_mul(denom, pair_sub(estimates[i], estimates[j]))
            estimates[i] = pair_sub(estimates[i], pair_div(value, denom))
    chosen = [m for m in range(4) if estimates[m][1] > 0.0]
    ranking = sorted(chosen, key=lambda m: -estimates[m][1])
    columns = []
    pairs = []
    for m in ranking:
        eigen_pair = estimates[m]
        system = [[(inverse[i][j] - (eigen_pair[0] if i == j else 0.0), -(eigen_pair[1] if i == j else 0.0)) for j in range(4)] for i in range(3)]
        rows_left = [[system[i][j] for j in range(3)] + [(-system[i][3][0], -system[i][3][1])] for i in range(3)]
        for col in range(3):
            pivot_row = max(range(col, 3), key=lambda r: rows_left[r][col][0] ** 2 + rows_left[r][col][1] ** 2)
            rows_left[col], rows_left[pivot_row] = rows_left[pivot_row], rows_left[col]
            leading = rows_left[col][col]
            rows_left[col] = [pair_div(v, leading) for v in rows_left[col]]
            for r in range(3):
                if r != col:
                    factor = rows_left[r][col]
                    rows_left[r] = [pair_sub(a, pair_mul(factor, b)) for a, b in zip(rows_left[r], rows_left[col])]
        vector = [rows_left[i][3] for i in range(3)] + [(1.0, 0.0)]
        columns.append([v[0] for v in vector])
        columns.append([v[1] for v in vector])
        pairs.append((eigen_pair[0], eigen_pair[1]))
    eigen_basis = [[columns[j][i] for j in range(4)] for i in range(4)]
    basis_inverse = invert_table(eigen_basis)
    return tableau, inverse, eigen_basis, basis_inverse, pairs


def center(padded):
    return padded[..., 1:-1, 1:-1, 1:-1]


def shifted(padded, member):
    if member == 0:
        return padded[..., 2:, 1:-1, 1:-1]
    if member == 1:
        return padded[..., :-2, 1:-1, 1:-1]
    if member == 2:
        return padded[..., 1:-1, 2:, 1:-1]
    if member == 3:
        return padded[..., 1:-1, :-2, 1:-1]
    if member == 4:
        return padded[..., 1:-1, 1:-1, 2:]
    return padded[..., 1:-1, 1:-1, :-2]


def face_terms(padded):
    middle = center(padded)
    return [0.5 * (middle + shifted(padded, m)) for m in range(6)]


def face_total(faces):
    total = faces[0]
    for m in range(1, 6):
        total = total + faces[m]
    return total


def neighbour_sum(faces, padded):
    total = faces[0] * shifted(padded, 0)
    for m in range(1, 6):
        total = total + faces[m] * shifted(padded, m)
    return total


def pad_cells(field, width):
    return jnp.pad(field, [(0, 0)] * (field.ndim - 3) + [(width, width)] * 3)


def apply_inverse(diag_real, coupling, determinant, vector):
    first = (diag_real * vector[0] - coupling * vector[1]) / determinant
    second = (coupling * vector[0] + diag_real * vector[1]) / determinant
    return jnp.stack([first, second])


def apply_block(diag_real, coupling, vector):
    return jnp.stack([diag_real * vector[0] + coupling * vector[1], diag_real * vector[1] - coupling * vector[0]])


def combine(coef, fields):
    total = coef[:, 0][:, None, None, None] * fields[0][None]
    for column in range(1, fields.shape[0]):
        total = total + coef[:, column][:, None, None, None] * fields[column][None]
    return total


def reference(previous, sections, diffusivity, reaction):
    tableau, inverse, eigen_basis, basis_inverse, pairs = radau_tables()
    flux_rows = jnp.asarray(basis_inverse, jnp.float32)
    shift_table = table_product(basis_inverse, inverse)
    shift_rows = jnp.asarray([[v / step_size for v in row_values] for row_values in shift_table], jnp.float32)
    section_coef = diffusivity * (1.0 + 0.5 * jnp.tanh(sections))
    section_faces = face_terms(pad_cells(section_coef, 1))
    section_flux = neighbour_sum(section_faces, pad_cells(sections, 1)) - face_total(section_faces) * sections
    section_flux = section_flux + reaction * sections * (1.0 - sections * sections)
    increment = sections - previous
    rhs = combine(flux_rows, section_flux) - combine(shift_rows, increment)
    frozen_coef = diffusivity * (1.0 + 0.5 * jnp.tanh(previous))
    faces = face_terms(pad_cells(frozen_coef, 1))
    react_slope = reaction * (1.0 - 3.0 * previous * previous)
    base_diag = face_total(faces) - react_slope
    solutions = []
    for eigen_block in range(2):
        real_part, imag_part = pairs[eigen_block]
        diag_real = real_part / step_size + base_diag
        coupling = imag_part / step_size
        determinant = diag_real * diag_real + coupling * coupling
        residue = rhs[2 * eigen_block:2 * eigen_block + 2]
        correction = jnp.zeros_like(residue)
        for sweep in range(ITERS):
            scaled = apply_inverse(diag_real, coupling, determinant, residue)
            search = scaled + apply_inverse(diag_real, coupling, determinant, neighbour_sum(faces, pad_cells(scaled, 1)))
            image = apply_block(diag_real, coupling, search) - neighbour_sum(faces, pad_cells(search, 1))
            step_length = jnp.sum(image * residue) / (jnp.sum(image * image) + tiny_value)
            correction = correction + step_length * search
            residue = residue - step_length * image
        solutions.append(correction)
    gathered = jnp.concatenate(solutions, 0)
    return sections + combine(jnp.asarray(eigen_basis, jnp.float32), gathered)
```

```python
import functools

import jax
import jax.numpy as jnp
from jax import lax
from jax.experimental import pallas as pl
from jax.experimental.pallas import tpu as pltpu
from jax.sharding import PartitionSpec as P

ITERS = 4
DEPTH = 2 * ITERS
MESH = pl.DeviceIdType.MESH

step_size = 1.0
tiny_value = 1e-06


def invert_table(matrix):
    order_n = len(matrix)
    augmented = [
        list(matrix[r]) + [1.0 if c == r else 0.0 for c in range(order_n)] for r in range(order_n)
    ]
    for col in range(order_n):
        pivot_row = max(range(col, order_n), key=lambda r: abs(augmented[r][col]))
        augmented[col], augmented[pivot_row] = (augmented[pivot_row], augmented[col])
        leading = augmented[col][col]
        augmented[col] = [v / leading for v in augmented[col]]
        for r in range(order_n):
            if r != col:
                factor = augmented[r][col]
                augmented[r] = [a - factor * b for a, b in zip(augmented[r], augmented[col])]
    return [row_values[order_n:] for row_values in augmented]


def table_product(left, right):
    return [
        [sum((left[i][k] * right[k][j] for k in range(len(right)))) for j in range(len(right[0]))]
        for i in range(len(left))
    ]


def pair_add(first, second):
    return (first[0] + second[0], first[1] + second[1])


def pair_sub(first, second):
    return (first[0] - second[0], first[1] - second[1])


def pair_mul(first, second):
    return (
        first[0] * second[0] - first[1] * second[1],
        first[0] * second[1] + first[1] * second[0],
    )


def pair_div(first, second):
    scale_sq = second[0] * second[0] + second[1] * second[1]
    return (
        (first[0] * second[0] + first[1] * second[1]) / scale_sq,
        (first[1] * second[0] - first[0] * second[1]) / scale_sq,
    )


def quartic_value(point):
    return (((210.0 * point - 480.0) * point + 360.0) * point - 96.0) * point + 6.0


def bisect_root(lower, upper):
    for count in range(200):
        middle = 0.5 * (lower + upper)
        if (quartic_value(lower) < 0.0) == (quartic_value(middle) < 0.0):
            lower = middle
        else:
            upper = middle
    return 0.5 * (lower + upper)


def radau_tables():
    abscissae = []
    grid_steps = 4000
    for m in range(grid_steps):
        lower = 0.999 * m / grid_steps
        upper = 0.999 * (m + 1) / grid_steps
        if (quartic_value(lower) < 0.0) != (quartic_value(upper) < 0.0):
            abscissae.append(bisect_root(lower, upper))
    abscissae.append(1.0)
    vander = [[abscissae[j] ** k for k in range(4)] for j in range(4)]
    moments = [[abscissae[i] ** (k + 1) / (k + 1) for k in range(4)] for i in range(4)]
    tableau = table_product(moments, invert_table(vander))
    inverse = invert_table(tableau)
    running = [list(row_values) for row_values in inverse]
    coeffs = []
    for k in range(1, 5):
        trace_value = sum((running[i][i] for i in range(4)))
        coeffs.append(-trace_value / k)
        shifted_table = [
            [running[i][j] + (coeffs[-1] if i == j else 0.0) for j in range(4)] for i in range(4)
        ]
        running = table_product(inverse, shifted_table)
    start_point = (0.4, 0.9)
    estimates = [(1.0, 0.0)]
    for k in range(3):
        estimates.append(pair_mul(estimates[-1], start_point))
    for count in range(500):
        for i in range(4):
            value = (1.0, 0.0)
            for coef_value in coeffs:
                value = pair_add(pair_mul(value, estimates[i]), (coef_value, 0.0))
            denom = (1.0, 0.0)
            for j in range(4):
                if j != i:
                    denom = pair_mul(denom, pair_sub(estimates[i], estimates[j]))
            estimates[i] = pair_sub(estimates[i], pair_div(value, denom))
    chosen = [m for m in range(4) if estimates[m][1] > 0.0]
    ranking = sorted(chosen, key=lambda m: -estimates[m][1])
    columns = []
    pairs = []
    for m in ranking:
        eigen_pair = estimates[m]
        system = [
            [
                (
                    inverse[i][j] - (eigen_pair[0] if i == j else 0.0),
                    -(eigen_pair[1] if i == j else 0.0),
                )
                for j in range(4)
            ]
            for i in range(3)
        ]
        rows_left = [
            [system[i][j] for j in range(3)] + [(-system[i][3][0], -system[i][3][1])]
            for i in range(3)
        ]
        for col in range(3):
            pivot_row = max(
                range(col, 3), key=lambda r: rows_left[r][col][0] ** 2 + rows_left[r][col][1] ** 2
            )
            rows_left[col], rows_left[pivot_row] = (rows_left[pivot_row], rows_left[col])
            leading = rows_left[col][col]
            rows_left[col] = [pair_div(v, leading) for v in rows_left[col]]
            for r in range(3):
                if r != col:
                    factor = rows_left[r][col]
                    rows_left[r] = [
                        pair_sub(a, pair_mul(factor, b))
                        for a, b in zip(rows_left[r], rows_left[col])
                    ]
        vector = [rows_left[i][3] for i in range(3)] + [(1.0, 0.0)]
        columns.append([v[0] for v in vector])
        columns.append([v[1] for v in vector])
        pairs.append((eigen_pair[0], eigen_pair[1]))
    eigen_basis = [[columns[j][i] for j in range(4)] for i in range(4)]
    basis_inverse = invert_table(eigen_basis)
    return (tableau, inverse, eigen_basis, basis_inverse, pairs)


def near(plane, member):
    if member == 0:
        return pltpu.roll(plane, plane.shape[0] - 1, 0)
    if member == 1:
        return pltpu.roll(plane, 1, 0)
    if member == 2:
        return pltpu.roll(plane, plane.shape[1] - 1, 1)
    return pltpu.roll(plane, 1, 1)


def kernel(
    sx_count, sy_count, tables,
    prev_ref, sec_ref, diff_ref, react_ref, out_ref,
    ext_a, coef_a, ext_b, faces, face_z, alpha, beta, hist, basis,
    part, part_out, part_in, corr_out, corr_in,
    pack_a, got_a, pack_b, got_b, pack_c, got_c, gram, send_sem, recv_sem, gram_send, gram_recv,
):
    depth_z, rows, lanes = prev_ref.shape
    top = DEPTH + rows
    wide = rows + 2 * DEPTH
    group = lanes // DEPTH
    sx, sy, half = lax.axis_index("sx"), lax.axis_index("sy"), lax.axis_index("section")
    q_table, c_table, p_table, pairs = tables

    def pick(first, second):
        return jnp.where(half == 0, jnp.float32(first), jnp.float32(second))

    barrier = pltpu.get_barrier_semaphore()
    members = sx_count * sy_count
    me = sx * sy_count + sy

    def member_at(offset):
        other = lax.rem(me + offset, members)
        return {"sx": other // sy_count, "sy": lax.rem(other, sy_count)}

    ext_a[...] = jnp.zeros_like(ext_a)
    ext_b[...] = jnp.zeros_like(ext_b)
    got_a[...] = jnp.zeros_like(got_a)
    got_b[...] = jnp.zeros_like(got_b)
    got_c[...] = jnp.zeros_like(got_c)
    for field in range(2):
        hist[0, field] = jnp.zeros(hist.shape[2:], jnp.float32)

    def greet(offset, carry):
        pl.semaphore_signal(barrier, inc=1, device_id=member_at(offset), device_id_type=MESH)
        return carry

    lax.fori_loop(1, members, greet, 0)
    pl.semaphore_signal(barrier, inc=1, device_id={"section": 1 - half}, device_id_type=MESH)

    lane_group = lax.broadcasted_iota(jnp.int32, (rows, lanes), 1) // DEPTH

    def pack(plane_of, low, high):
        down = jnp.zeros((rows, lanes), jnp.float32)
        up = jnp.zeros((rows, lanes), jnp.float32)
        for z in range(depth_z):
            plane = plane_of(z)
            if z > 0:
                plane = pltpu.roll(plane, DEPTH * z, 1)
            down = jnp.where(lane_group == z, plane, down)
            up = jnp.where(lane_group == (z + group - 1) % group, plane, up)
        low[...] = down
        high[...] = up

    def unpack(from_high, from_low, store):
        count = from_high.shape[0]
        groups = lax.broadcasted_iota(jnp.int32, (count, lanes), 1) // DEPTH
        zero = jnp.zeros((count, lanes), jnp.float32)
        for z in range(depth_z):
            mixed = jnp.where(
                groups == z,
                from_high,
                jnp.where(groups == (z + group - 1) % group, from_low, zero),
            )
            if z > 0:
                mixed = pltpu.roll(mixed, lanes - DEPTH * z, 1)
            store(z, mixed)

    for j in range(2):
        pack(lambda z: sec_ref[j, z], pack_a.at[0, j], pack_a.at[1, j])
        ext_a[j, 1 : depth_z + 1, DEPTH:top, 0:lanes] = sec_ref[j]
    pack(lambda z: diff_ref[z], pack_a.at[0, 2], pack_a.at[1, 2])
    ext_a[2, 1 : depth_z + 1, DEPTH:top, 0:lanes] = diff_ref[...]

    def frozen(z, carry):
        before = prev_ref[z]
        ext_b[0, z + 1, DEPTH:top, 0:lanes] = diff_ref[z] * (1.0 + 0.5 * jnp.tanh(before))
        ext_b[1, z + 1, DEPTH:top, 0:lanes] = react_ref[z] * (1.0 - 3.0 * before * before)
        return carry

    lax.fori_loop(0, depth_z, frozen, 0)
    for j in range(2):
        pack(lambda z: ext_b[j, z + 1, DEPTH:top, 0:lanes], pack_b.at[0, j], pack_b.at[1, j])

    pl.semaphore_wait(barrier, members)

    used = [0]

    def copy(source, target, device):
        at = used[0]
        used[0] += 1
        return pltpu.make_async_remote_copy(
            src_ref=source,
            dst_ref=target,
            send_sem=send_sem.at[at],
            recv_sem=recv_sem.at[at],
            device_id=device,
            device_id_type=MESH,
        )

    left, right = lax.rem(sx + sx_count - 1, sx_count), lax.rem(sx + 1, sx_count)
    below, above = lax.rem(sy + sy_count - 1, sy_count), lax.rem(sy + 1, sy_count)
    has_left, has_right = sx > 0, sx < sx_count - 1
    has_below, has_above = sy > 0, sy < sy_count - 1
    body_z = pl.ds(1, depth_z)
    own = pl.ds(0, lanes)
    low_rows, high_rows = pl.ds(0, DEPTH), pl.ds(top, DEPTH)

    def slabs(low_source, high_source, target):
        return [
            (has_left, has_right, copy(low_source, target(high_rows), {"sx": left})),
            (has_right, has_left, copy(high_source, target(low_rows), {"sx": right})),
        ]

    def strips(packed, got, corners):
        result = []
        for side, device, out_ok, in_ok in (
            (0, below, has_below, has_above),
            (1, above, has_above, has_below),
        ):
            middle = got.at[side, :, pl.ds(DEPTH, rows), :] if corners else got.at[side]
            result.append((out_ok, in_ok, copy(packed.at[side], middle, {"sy": device})))
            if corners:
                result.append((
                    out_ok & has_left,
                    in_ok & has_right,
                    copy(
                        packed.at[side, :, pl.ds(0, DEPTH), :],
                        got.at[side, :, high_rows, :],
                        {"sx": left, "sy": device},
                    ),
                ))
                result.append((
                    out_ok & has_right,
                    in_ok & has_left,
                    copy(
                        packed.at[side, :, pl.ds(rows - DEPTH, DEPTH), :],
                        got.at[side, :, low_rows, :],
                        {"sx": right, "sy": device},
                    ),
                ))
        return result

    def start(copies):
        for out_ok, in_ok, one in copies:
            pl.when(out_ok)(one.start)

    def receive(copies):
        for out_ok, in_ok, one in copies:
            pl.when(in_ok)(one.wait_recv)

    def release(copies):
        for out_ok, in_ok, one in copies:
            pl.when(out_ok)(one.wait_send)

    copies_a = strips(pack_a, got_a, False)
    copies_a += slabs(
        diff_ref.at[:, pl.ds(0, DEPTH), :],
        diff_ref.at[:, pl.ds(rows - DEPTH, DEPTH), :],
        lambda where: ext_a.at[2, body_z, where, own],
    )
    copies_a += slabs(
        sec_ref.at[:, :, pl.ds(0, DEPTH), :],
        sec_ref.at[:, :, pl.ds(rows - DEPTH, DEPTH), :],
        lambda where: ext_a.at[pl.ds(0, 2), body_z, where, own],
    )
    start(copies_a)
    copies_b = strips(pack_b, got_b, True)
    copies_b += slabs(
        ext_b.at[:, body_z, pl.ds(DEPTH, DEPTH), own],
        ext_b.at[:, body_z, pl.ds(top - DEPTH, DEPTH), own],
        lambda where: ext_b.at[:, body_z, where, own],
    )
    start(copies_b)

    receive(copies_a)

    for j in range(3):
        def put_a(z, plane):
            ext_a[j, z + 1, DEPTH:top, lanes : 2 * lanes] = plane

        unpack(got_a[0, j], got_a[1, j], put_a)

    def section_coefs(z, carry):
        for j in range(2):
            coef_a[j, z] = ext_a[2, z] * (1.0 + 0.5 * jnp.tanh(ext_a[j, z]))
        return carry

    lax.fori_loop(0, depth_z + 2, section_coefs, 0)

    q_own = [[pick(q_table[m][j], q_table[2 + m][2 + j]) for j in range(2)] for m in range(2)]
    q_far = [[pick(q_table[2 + m][j], q_table[m][2 + j]) for j in range(2)] for m in range(2)]
    c_own = [[pick(c_table[m][j], c_table[2 + m][2 + j]) for j in range(2)] for m in range(2)]
    c_far = [[pick(c_table[2 + m][j], c_table[m][2 + j]) for j in range(2)] for m in range(2)]

    def middle(plane):
        return plane[DEPTH:top, 0:lanes]

    def fluxes(z, carry):
        flux, increment = [], []
        for j in range(2):
            cells, coefs = ext_a[j, z + 1], coef_a[j, z + 1]
            here, coef_here = middle(cells), middle(coefs)
            total = jnp.zeros_like(here)
            for member in range(4):
                face = 0.5 * (coef_here + middle(near(coefs, member)))
                total = total + face * (middle(near(cells, member)) - here)
            for level in (z, z + 2):
                face = 0.5 * (coef_here + middle(coef_a[j, level]))
                total = total + face * (middle(ext_a[j, level]) - here)
            flux.append(total + react_ref[z] * here * (1.0 - here * here))
            increment.append(here - prev_ref[z])
        for m in range(2):
            part[m, z] = (
                q_own[m][0] * flux[0] + q_own[m][1] * flux[1]
                - c_own[m][0] * increment[0] - c_own[m][1] * increment[1]
            )
            part_out[m, z] = (
                q_far[m][0] * flux[0] + q_far[m][1] * flux[1]
                - c_far[m][0] * increment[0] - c_far[m][1] * increment[1]
            )
        return carry

    chunk = depth_z // 4
    swap = []
    for at in range(4):
        lax.fori_loop(at * chunk, (at + 1) * chunk, fluxes, 0)
        piece = pl.ds(at * chunk, chunk)
        one = copy(part_out.at[:, piece], part_in.at[:, piece], {"section": 1 - half})
        one.start()
        swap.append(one)

    receive(copies_b)

    for j in range(2):
        def put_b(z, plane):
            ext_b[j, z + 1, :, lanes : 2 * lanes] = plane

        unpack(got_b[0, j], got_b[1, j], put_b)

    real_part = pick(pairs[0][0] / step_size, pairs[1][0] / step_size)
    coupling = pick(pairs[0][1] / step_size, pairs[1][1] / step_size)
    row_at = lax.broadcasted_iota(jnp.int32, (wide, 2 * lanes), 0)
    lane_at = lax.broadcasted_iota(jnp.int32, (wide, 2 * lanes), 1)
    inside = ((row_at >= DEPTH) | has_left) & ((row_at < top) | has_right)
    inside = inside & (
        (lane_at < lanes)
        | ((lane_at < lanes + DEPTH) & has_above)
        | ((lane_at >= 2 * lanes - DEPTH) & has_below)
    )
    keep = inside.astype(jnp.float32)

    def depth_faces(z, carry):
        face_z[z] = 0.5 * (ext_b[0, z] + ext_b[0, z + 1])
        return carry

    lax.fori_loop(0, depth_z + 1, depth_faces, 0)

    def operator(z, carry):
        coefs = ext_b[0, z + 1]
        diag = real_part - ext_b[1, z + 1] + face_z[z] + face_z[z + 1]
        for member in range(4):
            face = 0.5 * (coefs + near(coefs, member))
            faces[member, z] = face
            diag = diag + face
        scale = keep / (diag * diag + coupling * coupling)
        alpha[z] = diag * scale
        beta[z] = coupling * scale
        return carry

    lax.fori_loop(0, depth_z, operator, 0)

    for m in range(1, DEPTH):
        for field in range(2):
            hist[m, field, 0] = jnp.zeros((wide, 2 * lanes), jnp.float32)
            hist[m, field, depth_z + 1] = jnp.zeros((wide, 2 * lanes), jnp.float32)

    for one in swap:
        one.wait_recv()

    def first_scaled(z, carry):
        rhs = [part[m, z] + part_in[m, z] for m in range(2)]
        a, b = middle(alpha[z]), middle(beta[z])
        for m in range(2):
            basis[0, m, z] = rhs[m]
        hist[0, 0, z + 1, DEPTH:top, 0:lanes] = a * rhs[0] - b * rhs[1]
        hist[0, 1, z + 1, DEPTH:top, 0:lanes] = b * rhs[0] + a * rhs[1]
        return carry

    lax.fori_loop(0, depth_z, first_scaled, 0)
    copies_c = slabs(
        hist.at[0, :, body_z, pl.ds(DEPTH, DEPTH), own],
        hist.at[0, :, body_z, pl.ds(top - DEPTH, DEPTH), own],
        lambda where: hist.at[0, :, body_z, where, own],
    )
    start(copies_c)
    for j in range(2):
        pack(lambda z: hist[0, j, z + 1, DEPTH:top, 0:lanes], pack_c.at[0, j], pack_c.at[1, j])
    more_c = strips(pack_c, got_c, True)
    start(more_c)
    copies_c = copies_c + more_c
    receive(copies_c)

    for j in range(2):
        def put_c(z, plane):
            hist[0, j, z + 1, :, lanes : 2 * lanes] = plane

        unpack(got_c[0, j], got_c[1, j], put_c)

    for m in range(DEPTH - 1):
        def apply(z, carry):
            around = []
            for field in range(2):
                cells = hist[m, field, z + 1]
                total = face_z[z] * hist[m, field, z] + face_z[z + 1] * hist[m, field, z + 2]
                for member in range(4):
                    total = total + faces[member, z] * near(cells, member)
                around.append(total)
            if m % 2 == 1:
                for field in range(2):
                    basis[(m + 1) // 2, field, z] = middle(around[field])
            a, b = alpha[z], beta[z]
            hist[m + 1, 0, z + 1] = a * around[0] - b * around[1]
            hist[m + 1, 1, z + 1] = b * around[0] + a * around[1]
            return carry

        lax.fori_loop(0, depth_z, apply, 0)

    index = [(i, j) for i in range(ITERS + 1) for j in range(i, ITERS + 1)]

    def last_apply(z, carry):
        totals = list(carry)
        for field in range(2):
            cells = hist[DEPTH - 1, field, z + 1]
            total = middle(face_z[z]) * middle(hist[DEPTH - 1, field, z])
            total = total + middle(face_z[z + 1]) * middle(hist[DEPTH - 1, field, z + 2])
            for member in range(4):
                total = total + middle(faces[member, z]) * middle(near(cells, member))
            members_of = [basis[k, field, z] for k in range(ITERS)] + [total]
            for at, (i, j) in enumerate(index):
                product = members_of[i] * members_of[j]
                for r in range(0, rows, 8):
                    totals[at] = totals[at] + product[r : r + 8]
        return tuple(totals)

    zeros = tuple(jnp.zeros((8, lanes), jnp.float32) for pair in index)
    sums = lax.fori_loop(0, depth_z, last_apply, zeros)
    gram[0, len(index) : 16] = jnp.zeros((16 - len(index), lanes), jnp.float32)
    for at, total in enumerate(sums):
        gram[0, at : at + 1] = jnp.sum(total, axis=0, keepdims=True)

    def gram_copy(offset):
        return pltpu.make_async_remote_copy(
            src_ref=gram.at[0],
            dst_ref=gram.at[offset],
            send_sem=gram_send.at[offset],
            recv_sem=gram_recv.at[offset],
            device_id=member_at(offset),
            device_id_type=MESH,
        )

    def gram_start(offset, carry):
        gram_copy(offset).start()
        return carry

    def gram_take(offset, carry):
        gram_copy(offset).wait_recv()
        return carry

    def gram_release(offset, carry):
        gram_copy(offset).wait_send()
        return carry

    lax.fori_loop(1, members, gram_start, 0)
    release(copies_a)
    release(copies_b)
    release(copies_c)
    for one in swap:
        one.wait_send()
    lax.fori_loop(1, members, gram_take, 0)
    table = gram[0]
    turn = [lax.rem(me - place + members, members) for place in range(members)]
    table = gram[turn[0]]
    for place in range(1, members):
        table = table + gram[turn[place]]
    table = jnp.sum(table, axis=1, keepdims=True)
    entry = {}
    for at, (i, j) in enumerate(index):
        entry[i, j] = entry[j, i] = table[at : at + 1, :]

    weights = {0: jnp.ones((1, 1), jnp.float32)}
    gains = {}
    for sweep in range(ITERS):
        image = {}
        for j in range(sweep + 2):
            if j in weights and j - 1 in weights:
                image[j] = weights[j] - weights[j - 1]
            elif j in weights:
                image[j] = weights[j]
            else:
                image[j] = -weights[j - 1]
        against = {
            j: functools.reduce(jnp.add, [image[i] * entry[i, j] for i in image]) for j in image
        }
        numerator = functools.reduce(jnp.add, [against[j] * weights[j] for j in weights])
        denominator = functools.reduce(jnp.add, [against[j] * image[j] for j in image])
        step = numerator / (denominator + tiny_value)
        for j in weights:
            gains[j] = gains[j] + step * weights[j] if j in gains else step * weights[j]
        weights = {
            j: (weights[j] - step * image[j]) if j in weights else -step * image[j] for j in image
        }

    p_own = [[pick(p_table[j][m], p_table[2 + j][2 + m]) for m in range(2)] for j in range(2)]
    p_far = [[pick(p_table[2 + j][m], p_table[j][2 + m]) for m in range(2)] for j in range(2)]
    gain_at = [jnp.broadcast_to(gains[k], (rows, lanes)) for k in range(ITERS)]

    def correct(z, carry):
        fix = []
        for field in range(2):
            total = None
            for k in range(ITERS):
                search = middle(hist[2 * k, field, z + 1]) + middle(hist[2 * k + 1, field, z + 1])
                total = gain_at[k] * search if total is None else total + gain_at[k] * search
            fix.append(total)
        for j in range(2):
            corr_out[j, z] = p_far[j][0] * fix[0] + p_far[j][1] * fix[1]
            part[j, z] = sec_ref[j, z] + p_own[j][0] * fix[0] + p_own[j][1] * fix[1]
        return carry

    final = []
    for at in range(4):
        lax.fori_loop(at * chunk, (at + 1) * chunk, correct, 0)
        piece = pl.ds(at * chunk, chunk)
        one = copy(corr_out.at[:, piece], corr_in.at[:, piece], {"section": 1 - half})
        one.start()
        final.append(one)
    for at in range(4):
        final[at].wait_recv()

        def finish(z, carry):
            for j in range(2):
                out_ref[j, z] = part[j, z] + corr_in[j, z]
            return carry

        lax.fori_loop(at * chunk, (at + 1) * chunk, finish, 0)
    for one in final:
        one.wait_send()
    lax.fori_loop(1, members, gram_release, 0)


def solution(mesh):
    sx_count, sy_count = mesh.shape["sx"], mesh.shape["sy"]
    tableau, inverse, eigen_basis, basis_inverse, pairs = radau_tables()
    shift_table = table_product(basis_inverse, inverse)
    shift_table = [[v / step_size for v in row_values] for row_values in shift_table]
    tables = (basis_inverse, shift_table, eigen_basis, pairs)

    def body(previous, sections, diffusivity, reaction):
        depth_z, rows, lanes = previous.shape
        wide = rows + 2 * DEPTH
        f32 = jnp.float32
        vmem = pltpu.VMEM
        ext = (depth_z + 2, wide, 2 * lanes)
        flat = (depth_z, wide, 2 * lanes)
        block = (2, depth_z, rows, lanes)
        members = sx_count * sy_count
        return pl.pallas_call(
            functools.partial(kernel, sx_count, sy_count, tables),
            out_shape=jax.ShapeDtypeStruct(sections.shape, f32),
            in_specs=[pl.BlockSpec(memory_space=pltpu.VMEM)] * 4,
            out_specs=pl.BlockSpec(memory_space=pltpu.VMEM),
            scratch_shapes=[
                vmem((3,) + ext, f32),
                vmem((2,) + ext, f32),
                vmem((2,) + ext, f32),
                vmem((4,) + flat, f32),
                vmem((depth_z + 1, wide, 2 * lanes), f32),
                vmem(flat, f32),
                vmem(flat, f32),
                vmem((DEPTH, 2) + ext, f32),
                vmem((ITERS,) + block, f32),
                vmem(block, f32),
                vmem(block, f32),
                vmem(block, f32),
                vmem(block, f32),
                vmem(block, f32),
                vmem((2, 3, rows, lanes), f32),
                vmem((2, 3, rows, lanes), f32),
                vmem((2, 2, rows, lanes), f32),
                vmem((2, 2, wide, lanes), f32),
                vmem((2, 2, rows, lanes), f32),
                vmem((2, 2, wide, lanes), f32),
                vmem((members, 16, lanes), f32),
                pltpu.SemaphoreType.DMA((32,)),
                pltpu.SemaphoreType.DMA((32,)),
                pltpu.SemaphoreType.DMA((members,)),
                pltpu.SemaphoreType.DMA((members,)),
            ],
            compiler_params=pltpu.CompilerParams(
                collective_id=0, has_side_effects=True, vmem_limit_bytes=48 * 1024 * 1024
            ),
        )(previous, sections, diffusivity, reaction)

    in_specs = (
        P(None, "sx", "sy"),
        P("section", None, "sx", "sy"),
        P(None, "sx", "sy"),
        P(None, "sx", "sy"),
    )
    out_specs = P("section", None, "sx", "sy")
    return jax.shard_map(body, mesh=mesh, in_specs=in_specs, out_specs=out_specs, check_vma=False)
```

```python
import functools

import jax
import jax.numpy as jnp
from jax import lax
from jax.experimental import pallas as pl
from jax.experimental.pallas import tpu as pltpu
from jax.sharding import PartitionSpec as P

ITERS = 4
DEPTH = 2 * ITERS
MESH = pl.DeviceIdType.MESH

step_size = 1.0
tiny_value = 1e-06


def invert_table(matrix):
    order_n = len(matrix)
    augmented = [
        list(matrix[r]) + [1.0 if c == r else 0.0 for c in range(order_n)] for r in range(order_n)
    ]
    for col in range(order_n):
        pivot_row = max(range(col, order_n), key=lambda r: abs(augmented[r][col]))
        augmented[col], augmented[pivot_row] = (augmented[pivot_row], augmented[col])
        leading = augmented[col][col]
        augmented[col] = [v / leading for v in augmented[col]]
        for r in range(order_n):
            if r != col:
                factor = augmented[r][col]
                augmented[r] = [a - factor * b for a, b in zip(augmented[r], augmented[col])]
    return [row_values[order_n:] for row_values in augmented]


def table_product(left, right):
    return [
        [sum((left[i][k] * right[k][j] for k in range(len(right)))) for j in range(len(right[0]))]
        for i in range(len(left))
    ]


def pair_add(first, second):
    return (first[0] + second[0], first[1] + second[1])


def pair_sub(first, second):
    return (first[0] - second[0], first[1] - second[1])


def pair_mul(first, second):
    return (
        first[0] * second[0] - first[1] * second[1],
        first[0] * second[1] + first[1] * second[0],
    )


def pair_div(first, second):
    scale_sq = second[0] * second[0] + second[1] * second[1]
    return (
        (first[0] * second[0] + first[1] * second[1]) / scale_sq,
        (first[1] * second[0] - first[0] * second[1]) / scale_sq,
    )


def quartic_value(point):
    return (((210.0 * point - 480.0) * point + 360.0) * point - 96.0) * point + 6.0


def bisect_root(lower, upper):
    for count in range(200):
        middle = 0.5 * (lower + upper)
        if (quartic_value(lower) < 0.0) == (quartic_value(middle) < 0.0):
            lower = middle
        else:
            upper = middle
    return 0.5 * (lower + upper)


def radau_tables():
    abscissae = []
    grid_steps = 4000
    for m in range(grid_steps):
        lower = 0.999 * m / grid_steps
        upper = 0.999 * (m + 1) / grid_steps
        if (quartic_value(lower) < 0.0) != (quartic_value(upper) < 0.0):
            abscissae.append(bisect_root(lower, upper))
    abscissae.append(1.0)
    vander = [[abscissae[j] ** k for k in range(4)] for j in range(4)]
    moments = [[abscissae[i] ** (k + 1) / (k + 1) for k in range(4)] for i in range(4)]
    tableau = table_product(moments, invert_table(vander))
    inverse = invert_table(tableau)
    running = [list(row_values) for row_values in inverse]
    coeffs = []
    for k in range(1, 5):
        trace_value = sum((running[i][i] for i in range(4)))
        coeffs.append(-trace_value / k)
        shifted_table = [
            [running[i][j] + (coeffs[-1] if i == j else 0.0) for j in range(4)] for i in range(4)
        ]
        running = table_product(inverse, shifted_table)
    start_point = (0.4, 0.9)
    estimates = [(1.0, 0.0)]
    for k in range(3):
        estimates.append(pair_mul(estimates[-1], start_point))
    for count in range(500):
        for i in range(4):
            value = (1.0, 0.0)
            for coef_value in coeffs:
                value = pair_add(pair_mul(value, estimates[i]), (coef_value, 0.0))
            denom = (1.0, 0.0)
            for j in range(4):
                if j != i:
                    denom = pair_mul(denom, pair_sub(estimates[i], estimates[j]))
            estimates[i] = pair_sub(estimates[i], pair_div(value, denom))
    chosen = [m for m in range(4) if estimates[m][1] > 0.0]
    ranking = sorted(chosen, key=lambda m: -estimates[m][1])
    columns = []
    pairs = []
    for m in ranking:
        eigen_pair = estimates[m]
        system = [
            [
                (
                    inverse[i][j] - (eigen_pair[0] if i == j else 0.0),
                    -(eigen_pair[1] if i == j else 0.0),
                )
                for j in range(4)
            ]
            for i in range(3)
        ]
        rows_left = [
            [system[i][j] for j in range(3)] + [(-system[i][3][0], -system[i][3][1])]
            for i in range(3)
        ]
        for col in range(3):
            pivot_row = max(
                range(col, 3), key=lambda r: rows_left[r][col][0] ** 2 + rows_left[r][col][1] ** 2
            )
            rows_left[col], rows_left[pivot_row] = (rows_left[pivot_row], rows_left[col])
            leading = rows_left[col][col]
            rows_left[col] = [pair_div(v, leading) for v in rows_left[col]]
            for r in range(3):
                if r != col:
                    factor = rows_left[r][col]
                    rows_left[r] = [
                        pair_sub(a, pair_mul(factor, b))
                        for a, b in zip(rows_left[r], rows_left[col])
                    ]
        vector = [rows_left[i][3] for i in range(3)] + [(1.0, 0.0)]
        columns.append([v[0] for v in vector])
        columns.append([v[1] for v in vector])
        pairs.append((eigen_pair[0], eigen_pair[1]))
    eigen_basis = [[columns[j][i] for j in range(4)] for i in range(4)]
    basis_inverse = invert_table(eigen_basis)
    return (tableau, inverse, eigen_basis, basis_inverse, pairs)


def near(plane, member):
    if member == 0:
        return pltpu.roll(plane, plane.shape[0] - 1, 0)
    if member == 1:
        return pltpu.roll(plane, 1, 0)
    if member == 2:
        return pltpu.roll(plane, plane.shape[1] - 1, 1)
    return pltpu.roll(plane, 1, 1)


def kernel(
    sx_count, sy_count, tables,
    prev_any, sec_any, diff_any, react_any, out_ref,
    prev_ref, sec_ref, diff_ref, react_ref,
    ext_a, ext_b, faces, face_z, alpha, beta, *rest,
):
    hist, rest = rest[:DEPTH], rest[DEPTH:]
    (
    basis, part, part_out, part_in, corr_out, corr_in,
    pack_a, got_a, pack_b, got_b, pack_c, got_c, gram, load_sem,
    send_sem, recv_sem, gram_send, gram_recv,
    ) = rest
    depth_z, rows, lanes = prev_ref.shape
    top = DEPTH + rows
    wide = rows + 2 * DEPTH
    group = lanes // DEPTH
    sx, sy, half = lax.axis_index("sx"), lax.axis_index("sy"), lax.axis_index("section")
    q_table, c_table, p_table, pairs = tables

    def pick(first, second):
        return jnp.where(half == 0, jnp.float32(first), jnp.float32(second))

    barrier = pltpu.get_barrier_semaphore()
    members = sx_count * sy_count
    me = sx * sy_count + sy

    def member_at(offset):
        other = lax.rem(me + offset, members)
        return {"sx": other // sy_count, "sy": lax.rem(other, sy_count)}

    loads = [
        pltpu.make_async_copy(source, target, load_sem.at[at])
        for at, (source, target) in enumerate((
            (sec_any, sec_ref), (diff_any, diff_ref), (prev_any, prev_ref), (react_any, react_ref),
        ))
    ]
    for one in loads:
        one.start()
    ext_a[...] = jnp.zeros_like(ext_a)
    ext_b[...] = jnp.zeros_like(ext_b)
    got_a[...] = jnp.zeros_like(got_a)
    got_b[...] = jnp.zeros_like(got_b)
    got_c[...] = jnp.zeros_like(got_c)
    for field in range(2):
        hist[0][field] = jnp.zeros(hist[0].shape[1:], jnp.float32)

    def greet(offset, carry):
        pl.semaphore_signal(barrier, inc=1, device_id=member_at(offset), device_id_type=MESH)
        return carry

    lax.fori_loop(1, members, greet, 0)
    pl.semaphore_signal(barrier, inc=1, device_id={"section": 1 - half}, device_id_type=MESH)

    lane_group = lax.broadcasted_iota(jnp.int32, (rows, lanes), 1) // DEPTH

    def pack(plane_of, low, high):
        down = jnp.zeros((rows, lanes), jnp.float32)
        up = jnp.zeros((rows, lanes), jnp.float32)
        for z in range(depth_z):
            plane = plane_of(z)
            if z > 0:
                plane = pltpu.roll(plane, DEPTH * z, 1)
            down = jnp.where(lane_group == z, plane, down)
            up = jnp.where(lane_group == (z + group - 1) % group, plane, up)
        low[...] = down
        high[...] = up

    def unpack(from_high, from_low, store):
        count = from_high.shape[0]
        groups = lax.broadcasted_iota(jnp.int32, (count, lanes), 1) // DEPTH
        zero = jnp.zeros((count, lanes), jnp.float32)
        for z in range(depth_z):
            mixed = jnp.where(
                groups == z,
                from_high,
                jnp.where(groups == (z + group - 1) % group, from_low, zero),
            )
            if z > 0:
                mixed = pltpu.roll(mixed, lanes - DEPTH * z, 1)
            store(z, mixed)

    for one in loads:
        one.wait()

    def planes(fn, least, most, batch):
        def several(at, carry):
            stores = []
            for step in range(batch):
                stores.append(fn(least + at * batch + step))
            for store in stores:
                store()
            return carry

        lax.fori_loop(0, (most - least) // batch, several, 0)

    def own_coefs(z):
        before, diffusivity = prev_ref[z], diff_ref[z]
        cells = [sec_ref[j, z] for j in range(2)]
        coefs = [diffusivity * (1.0 + 0.5 * jnp.tanh(cells[j])) for j in range(2)]
        coef = diffusivity * (1.0 + 0.5 * jnp.tanh(before))
        slope = react_ref[z] * (1.0 - 3.0 * before * before)

        def store():
            for j in range(2):
                ext_a[j, z + 1, DEPTH:top, 0:lanes] = cells[j]
                ext_a[2 + j, z + 1, DEPTH:top, 0:lanes] = coefs[j]
            ext_b[0, z + 1, DEPTH:top, 0:lanes] = coef
            ext_b[1, z + 1, DEPTH:top, 0:lanes] = slope

        return store

    planes(own_coefs, 0, depth_z, 2)
    for j in range(4):
        pack(lambda z: ext_a[j, z + 1, DEPTH:top, 0:lanes], pack_a.at[0, j], pack_a.at[1, j])
    for j in range(2):
        pack(lambda z: ext_b[j, z + 1, DEPTH:top, 0:lanes], pack_b.at[0, j], pack_b.at[1, j])

    pl.semaphore_wait(barrier, members)

    used = [0]

    def copy(source, target, device):
        at = used[0]
        used[0] += 1
        return pltpu.make_async_remote_copy(
            src_ref=source,
            dst_ref=target,
            send_sem=send_sem.at[at],
            recv_sem=recv_sem.at[at],
            device_id=device,
            device_id_type=MESH,
        )

    left, right = lax.rem(sx + sx_count - 1, sx_count), lax.rem(sx + 1, sx_count)
    below, above = lax.rem(sy + sy_count - 1, sy_count), lax.rem(sy + 1, sy_count)
    has_left, has_right = sx > 0, sx < sx_count - 1
    has_below, has_above = sy > 0, sy < sy_count - 1
    body_z = pl.ds(1, depth_z)
    own = pl.ds(0, lanes)
    low_rows, high_rows = pl.ds(0, DEPTH), pl.ds(top, DEPTH)

    def slabs(low_source, high_source, target):
        return [
            (has_left, has_right, copy(low_source, target(high_rows), {"sx": left})),
            (has_right, has_left, copy(high_source, target(low_rows), {"sx": right})),
        ]

    def strips(packed, got, corners):
        result = []
        for side, device, out_ok, in_ok in (
            (0, below, has_below, has_above),
            (1, above, has_above, has_below),
        ):
            middle = got.at[side, :, pl.ds(DEPTH, rows), :] if corners else got.at[side]
            result.append((out_ok, in_ok, copy(packed.at[side], middle, {"sy": device})))
            if corners:
                result.append((
                    out_ok & has_left,
                    in_ok & has_right,
                    copy(
                        packed.at[side, :, pl.ds(0, DEPTH), :],
                        got.at[side, :, high_rows, :],
                        {"sx": left, "sy": device},
                    ),
                ))
                result.append((
                    out_ok & has_right,
                    in_ok & has_left,
                    copy(
                        packed.at[side, :, pl.ds(rows - DEPTH, DEPTH), :],
                        got.at[side, :, low_rows, :],
                        {"sx": right, "sy": device},
                    ),
                ))
        return result

    def start(copies):
        for out_ok, in_ok, one in copies:
            pl.when(out_ok)(one.start)

    def receive(copies):
        for out_ok, in_ok, one in copies:
            pl.when(in_ok)(one.wait_recv)

    def release(copies):
        for out_ok, in_ok, one in copies:
            pl.when(out_ok)(one.wait_send)

    copies_a = strips(pack_a, got_a, False)
    edge = pl.ds(top, 1), pl.ds(DEPTH - 1, 1)
    copies_a.append((
        has_left,
        has_right,
        copy(
            ext_a.at[:, body_z, pl.ds(DEPTH, 1), own],
            ext_a.at[:, body_z, edge[0], own],
            {"sx": left},
        ),
    ))
    copies_a.append((
        has_right,
        has_left,
        copy(
            ext_a.at[:, body_z, pl.ds(top - 1, 1), own],
            ext_a.at[:, body_z, edge[1], own],
            {"sx": right},
        ),
    ))
    start(copies_a)
    copies_b = strips(pack_b, got_b, True)
    copies_b += slabs(
        ext_b.at[:, body_z, pl.ds(DEPTH, DEPTH), own],
        ext_b.at[:, body_z, pl.ds(top - DEPTH, DEPTH), own],
        lambda where: ext_b.at[:, body_z, where, own],
    )
    start(copies_b)

    receive(copies_a)

    for j in range(4):
        def put_a(z, plane):
            ext_a[j, z + 1, DEPTH:top, lanes : 2 * lanes] = plane

        unpack(got_a[0, j], got_a[1, j], put_a)

    q_own = [[pick(q_table[m][j], q_table[2 + m][2 + j]) for j in range(2)] for m in range(2)]
    q_far = [[pick(q_table[2 + m][j], q_table[m][2 + j]) for j in range(2)] for m in range(2)]
    c_own = [[pick(c_table[m][j], c_table[2 + m][2 + j]) for j in range(2)] for m in range(2)]
    c_far = [[pick(c_table[2 + m][j], c_table[m][2 + j]) for j in range(2)] for m in range(2)]

    def middle(plane):
        return plane[DEPTH:top, 0:lanes]

    def fluxes(z):
        flux, increment = [], []
        for j in range(2):
            cells, coefs = ext_a[j, z + 1], ext_a[2 + j, z + 1]
            here, coef_here = middle(cells), middle(coefs)
            total = jnp.zeros_like(here)
            for member in range(4):
                face = 0.5 * (coef_here + middle(near(coefs, member)))
                total = total + face * (middle(near(cells, member)) - here)
            for level in (z, z + 2):
                face = 0.5 * (coef_here + middle(ext_a[2 + j, level]))
                total = total + face * (middle(ext_a[j, level]) - here)
            flux.append(total + react_ref[z] * here * (1.0 - here * here))
            increment.append(here - prev_ref[z])
        near_part = [
            q_own[m][0] * flux[0] + q_own[m][1] * flux[1]
            - c_own[m][0] * increment[0] - c_own[m][1] * increment[1]
            for m in range(2)
        ]
        far_part = [
            q_far[m][0] * flux[0] + q_far[m][1] * flux[1]
            - c_far[m][0] * increment[0] - c_far[m][1] * increment[1]
            for m in range(2)
        ]

        def store():
            for m in range(2):
                part[m, z] = near_part[m]
                part_out[m, z] = far_part[m]

        return store

    chunk = depth_z // 4
    swap = []
    for at in range(4):
        planes(fluxes, at * chunk, (at + 1) * chunk, 2)
        piece = pl.ds(at * chunk, chunk)
        one = copy(part_out.at[:, piece], part_in.at[:, piece], {"section": 1 - half})
        one.start()
        swap.append(one)

    receive(copies_b)

    for j in range(2):
        def put_b(z, plane):
            ext_b[j, z + 1, :, lanes : 2 * lanes] = plane

        unpack(got_b[0, j], got_b[1, j], put_b)

    real_part = pick(pairs[0][0] / step_size, pairs[1][0] / step_size)
    coupling = pick(pairs[0][1] / step_size, pairs[1][1] / step_size)
    row_at = lax.broadcasted_iota(jnp.int32, (wide, 2 * lanes), 0)
    lane_at = lax.broadcasted_iota(jnp.int32, (wide, 2 * lanes), 1)
    inside = ((row_at >= DEPTH) | has_left) & ((row_at < top) | has_right)
    inside = inside & (
        (lane_at < lanes)
        | ((lane_at < lanes + DEPTH) & has_above)
        | ((lane_at >= 2 * lanes - DEPTH) & has_below)
    )
    keep = inside.astype(jnp.float32)

    def depth_faces(z, carry):
        face_z[z] = 0.5 * (ext_b[0, z] + ext_b[0, z + 1])
        return carry

    lax.fori_loop(0, depth_z + 1, depth_faces, 0)

    def operator(z):
        coefs = ext_b[0, z + 1]
        diag = real_part - ext_b[1, z + 1] + face_z[z] + face_z[z + 1]
        sides = [0.5 * (coefs + near(coefs, member)) for member in range(4)]
        for face in sides:
            diag = diag + face
        scale = keep / (diag * diag + coupling * coupling)

        def store():
            for member in range(4):
                faces[member, z] = sides[member]
            alpha[z] = diag * scale
            beta[z] = coupling * scale

        return store

    planes(operator, 0, depth_z, 2)

    for m in range(1, DEPTH):
        for field in range(2):
            hist[m][field, 0] = jnp.zeros((wide, 2 * lanes), jnp.float32)
            hist[m][field, depth_z + 1] = jnp.zeros((wide, 2 * lanes), jnp.float32)

    for one in swap:
        one.wait_recv()

    def first_scaled(z):
        rhs = [part[m, z] + part_in[m, z] for m in range(2)]
        a, b = middle(alpha[z]), middle(beta[z])

        def store():
            for m in range(2):
                basis[0, m, z] = rhs[m]
            hist[0][0, z + 1, DEPTH:top, 0:lanes] = a * rhs[0] - b * rhs[1]
            hist[0][1, z + 1, DEPTH:top, 0:lanes] = b * rhs[0] + a * rhs[1]

        return store

    planes(first_scaled, 0, depth_z, 4)
    copies_c = slabs(
        hist[0].at[:, body_z, pl.ds(DEPTH, DEPTH), own],
        hist[0].at[:, body_z, pl.ds(top - DEPTH, DEPTH), own],
        lambda where: hist[0].at[:, body_z, where, own],
    )
    start(copies_c)
    for j in range(2):
        pack(lambda z: hist[0][j, z + 1, DEPTH:top, 0:lanes], pack_c.at[0, j], pack_c.at[1, j])
    more_c = strips(pack_c, got_c, True)
    start(more_c)
    copies_c = copies_c + more_c
    receive(copies_c)

    for j in range(2):
        def put_c(z, plane):
            hist[0][j, z + 1, :, lanes : 2 * lanes] = plane

        unpack(got_c[0, j], got_c[1, j], put_c)

    for m in range(DEPTH - 1):
        def apply(z):
            around = []
            for field in range(2):
                cells = hist[m][field, z + 1]
                total = face_z[z] * hist[m][field, z] + face_z[z + 1] * hist[m][field, z + 2]
                for member in range(4):
                    total = total + faces[member, z] * near(cells, member)
                around.append(total)
            a, b = alpha[z], beta[z]
            scaled = [a * around[0] - b * around[1], b * around[0] + a * around[1]]

            def store():
                for field in range(2):
                    if m % 2 == 1:
                        basis[(m + 1) // 2, field, z] = middle(around[field])
                    hist[m + 1][field, z + 1] = scaled[field]

            return store

        planes(apply, 0, depth_z, 2)

    index = [(i, j) for i in range(ITERS + 1) for j in range(i, ITERS + 1)]

    def last_apply(z, carry):
        totals = list(carry)
        for field in range(2):
            cells = hist[DEPTH - 1][field, z + 1]
            total = middle(face_z[z]) * middle(hist[DEPTH - 1][field, z])
            total = total + middle(face_z[z + 1]) * middle(hist[DEPTH - 1][field, z + 2])
            for member in range(4):
                total = total + middle(faces[member, z]) * middle(near(cells, member))
            members_of = [basis[k, field, z] for k in range(ITERS)] + [total]
            for at, (i, j) in enumerate(index):
                product = members_of[i] * members_of[j]
                for r in range(0, rows, 8):
                    totals[at] = totals[at] + product[r : r + 8]
        return tuple(totals)

    zeros = tuple(jnp.zeros((8, lanes), jnp.float32) for pair in index)
    sums = lax.fori_loop(0, depth_z, last_apply, zeros)
    square = jnp.concatenate(
        [jnp.sum(total, axis=0, keepdims=True) for total in sums]
        + [jnp.zeros((16 - len(index), lanes), jnp.float32)],
        axis=0,
    )
    diagonal = lax.broadcasted_iota(jnp.int32, (16, lanes), 0) == lax.broadcasted_iota(
        jnp.int32, (16, lanes), 1
    )
    square = jnp.where(diagonal, jnp.sum(square, axis=1, keepdims=True), 0.0)
    gram[0] = jnp.sum(square, axis=0, keepdims=True)

    def gram_copy(offset):
        return pltpu.make_async_remote_copy(
            src_ref=gram.at[0],
            dst_ref=gram.at[offset],
            send_sem=gram_send.at[offset],
            recv_sem=gram_recv.at[offset],
            device_id=member_at(offset),
            device_id_type=MESH,
        )

    def gram_start(offset, carry):
        gram_copy(offset).start()
        return carry

    def gram_take(offset, carry):
        gram_copy(offset).wait_recv()
        return carry

    def gram_release(offset, carry):
        gram_copy(offset).wait_send()
        return carry

    lax.fori_loop(1, members, gram_start, 0)
    release(copies_a)
    release(copies_b)
    release(copies_c)
    for one in swap:
        one.wait_send()
    lax.fori_loop(1, members, gram_take, 0)
    turn = [lax.rem(me - place + members, members) for place in range(members)]
    table = gram[turn[0]]
    for place in range(1, members):
        table = table + gram[turn[place]]
    table = jnp.where(diagonal, jnp.broadcast_to(table, (16, lanes)), 0.0)
    table = jnp.sum(table, axis=1, keepdims=True)
    entry = {}
    for at, (i, j) in enumerate(index):
        entry[i, j] = entry[j, i] = table[at : at + 1, :]

    weights = {0: jnp.ones((1, 1), jnp.float32)}
    gains = {}
    for sweep in range(ITERS):
        image = {}
        for j in range(sweep + 2):
            if j in weights and j - 1 in weights:
                image[j] = weights[j] - weights[j - 1]
            elif j in weights:
                image[j] = weights[j]
            else:
                image[j] = -weights[j - 1]
        against = {
            j: functools.reduce(jnp.add, [image[i] * entry[i, j] for i in image]) for j in image
        }
        numerator = functools.reduce(jnp.add, [against[j] * weights[j] for j in weights])
        denominator = functools.reduce(jnp.add, [against[j] * image[j] for j in image])
        step = numerator / (denominator + tiny_value)
        for j in weights:
            gains[j] = gains[j] + step * weights[j] if j in gains else step * weights[j]
        weights = {
            j: (weights[j] - step * image[j]) if j in weights else -step * image[j] for j in image
        }

    p_own = [[pick(p_table[j][m], p_table[2 + j][2 + m]) for m in range(2)] for j in range(2)]
    p_far = [[pick(p_table[2 + j][m], p_table[j][2 + m]) for m in range(2)] for j in range(2)]
    gain_at = [jnp.broadcast_to(gains[k], (rows, lanes)) for k in range(ITERS)]

    def correct(z):
        fix = []
        for field in range(2):
            total = None
            for k in range(ITERS):
                search = middle(hist[2 * k][field, z + 1]) + middle(hist[2 * k + 1][field, z + 1])
                total = gain_at[k] * search if total is None else total + gain_at[k] * search
            fix.append(total)

        def store():
            for j in range(2):
                corr_out[j, z] = p_far[j][0] * fix[0] + p_far[j][1] * fix[1]
                part[j, z] = sec_ref[j, z] + p_own[j][0] * fix[0] + p_own[j][1] * fix[1]

        return store

    final = []
    for at in range(4):
        planes(correct, at * chunk, (at + 1) * chunk, 4)
        piece = pl.ds(at * chunk, chunk)
        one = copy(corr_out.at[:, piece], corr_in.at[:, piece], {"section": 1 - half})
        one.start()
        final.append(one)
    for at in range(4):
        final[at].wait_recv()

        piece = pl.ds(at * chunk, chunk)
        out_ref[:, piece] = part[:, piece] + corr_in[:, piece]
    for one in final:
        one.wait_send()
    lax.fori_loop(1, members, gram_release, 0)


def solution(mesh):
    sx_count, sy_count = mesh.shape["sx"], mesh.shape["sy"]
    tableau, inverse, eigen_basis, basis_inverse, pairs = radau_tables()
    shift_table = table_product(basis_inverse, inverse)
    shift_table = [[v / step_size for v in row_values] for row_values in shift_table]
    tables = (basis_inverse, shift_table, eigen_basis, pairs)

    def body(previous, sections, diffusivity, reaction):
        depth_z, rows, lanes = previous.shape
        wide = rows + 2 * DEPTH
        f32 = jnp.float32
        vmem = pltpu.VMEM
        ext = (depth_z + 2, wide, 2 * lanes)
        flat = (depth_z, wide, 2 * lanes)
        block = (2, depth_z, rows, lanes)
        members = sx_count * sy_count
        return pl.pallas_call(
            functools.partial(kernel, sx_count, sy_count, tables),
            out_shape=jax.ShapeDtypeStruct(sections.shape, f32),
            in_specs=[pl.BlockSpec(memory_space=pl.ANY)] * 4,
            out_specs=pl.BlockSpec(memory_space=pltpu.VMEM),
            scratch_shapes=[
                vmem((depth_z, rows, lanes), f32),
                vmem(block, f32),
                vmem((depth_z, rows, lanes), f32),
                vmem((depth_z, rows, lanes), f32),
                vmem((4,) + ext, f32),
                vmem((2,) + ext, f32),
                vmem((4,) + flat, f32),
                vmem((depth_z + 1, wide, 2 * lanes), f32),
                vmem(flat, f32),
                vmem(flat, f32),
                *[vmem((2,) + ext, f32) for m in range(DEPTH)],
                vmem((ITERS,) + block, f32),
                vmem(block, f32),
                vmem(block, f32),
                vmem(block, f32),
                vmem(block, f32),
                vmem(block, f32),
                vmem((2, 4, rows, lanes), f32),
                vmem((2, 4, rows, lanes), f32),
                vmem((2, 2, rows, lanes), f32),
                vmem((2, 2, wide, lanes), f32),
                vmem((2, 2, rows, lanes), f32),
                vmem((2, 2, wide, lanes), f32),
                vmem((members, 1, lanes), f32),
                pltpu.SemaphoreType.DMA((4,)),
                pltpu.SemaphoreType.DMA((32,)),
                pltpu.SemaphoreType.DMA((32,)),
                pltpu.SemaphoreType.DMA((members,)),
                pltpu.SemaphoreType.DMA((members,)),
            ],
            compiler_params=pltpu.CompilerParams(
                collective_id=0, has_side_effects=True, vmem_limit_bytes=48 * 1024 * 1024
            ),
        )(previous, sections, diffusivity, reaction)

    in_specs = (
        P(None, "sx", "sy"),
        P("section", None, "sx", "sy"),
        P(None, "sx", "sy"),
        P(None, "sx", "sy"),
    )
    out_specs = P("section", None, "sx", "sy")
    return jax.shard_map(body, mesh=mesh, in_specs=in_specs, out_specs=out_specs, check_vma=False)
```

```python
import functools

import jax
import jax.numpy as jnp
from jax import lax
from jax.experimental import pallas as pl
from jax.experimental.pallas import tpu as pltpu
from jax.sharding import PartitionSpec as P

ITERS = 4
DEPTH = 2 * ITERS
MESH = pl.DeviceIdType.MESH

step_size = 1.0
tiny_value = 1e-06


def invert_table(matrix):
    order_n = len(matrix)
    augmented = [
        list(matrix[r]) + [1.0 if c == r else 0.0 for c in range(order_n)] for r in range(order_n)
    ]
    for col in range(order_n):
        pivot_row = max(range(col, order_n), key=lambda r: abs(augmented[r][col]))
        augmented[col], augmented[pivot_row] = (augmented[pivot_row], augmented[col])
        leading = augmented[col][col]
        augmented[col] = [v / leading for v in augmented[col]]
        for r in range(order_n):
            if r != col:
                factor = augmented[r][col]
                augmented[r] = [a - factor * b for a, b in zip(augmented[r], augmented[col])]
    return [row_values[order_n:] for row_values in augmented]


def table_product(left, right):
    return [
        [sum((left[i][k] * right[k][j] for k in range(len(right)))) for j in range(len(right[0]))]
        for i in range(len(left))
    ]


def pair_add(first, second):
    return (first[0] + second[0], first[1] + second[1])


def pair_sub(first, second):
    return (first[0] - second[0], first[1] - second[1])


def pair_mul(first, second):
    return (
        first[0] * second[0] - first[1] * second[1],
        first[0] * second[1] + first[1] * second[0],
    )


def pair_div(first, second):
    scale_sq = second[0] * second[0] + second[1] * second[1]
    return (
        (first[0] * second[0] + first[1] * second[1]) / scale_sq,
        (first[1] * second[0] - first[0] * second[1]) / scale_sq,
    )


def quartic_value(point):
    return (((210.0 * point - 480.0) * point + 360.0) * point - 96.0) * point + 6.0


def bisect_root(lower, upper):
    for count in range(200):
        middle = 0.5 * (lower + upper)
        if (quartic_value(lower) < 0.0) == (quartic_value(middle) < 0.0):
            lower = middle
        else:
            upper = middle
    return 0.5 * (lower + upper)


def radau_tables():
    abscissae = []
    grid_steps = 4000
    for m in range(grid_steps):
        lower = 0.999 * m / grid_steps
        upper = 0.999 * (m + 1) / grid_steps
        if (quartic_value(lower) < 0.0) != (quartic_value(upper) < 0.0):
            abscissae.append(bisect_root(lower, upper))
    abscissae.append(1.0)
    vander = [[abscissae[j] ** k for k in range(4)] for j in range(4)]
    moments = [[abscissae[i] ** (k + 1) / (k + 1) for k in range(4)] for i in range(4)]
    tableau = table_product(moments, invert_table(vander))
    inverse = invert_table(tableau)
    running = [list(row_values) for row_values in inverse]
    coeffs = []
    for k in range(1, 5):
        trace_value = sum((running[i][i] for i in range(4)))
        coeffs.append(-trace_value / k)
        shifted_table = [
            [running[i][j] + (coeffs[-1] if i == j else 0.0) for j in range(4)] for i in range(4)
        ]
        running = table_product(inverse, shifted_table)
    start_point = (0.4, 0.9)
    estimates = [(1.0, 0.0)]
    for k in range(3):
        estimates.append(pair_mul(estimates[-1], start_point))
    for count in range(500):
        for i in range(4):
            value = (1.0, 0.0)
            for coef_value in coeffs:
                value = pair_add(pair_mul(value, estimates[i]), (coef_value, 0.0))
            denom = (1.0, 0.0)
            for j in range(4):
                if j != i:
                    denom = pair_mul(denom, pair_sub(estimates[i], estimates[j]))
            estimates[i] = pair_sub(estimates[i], pair_div(value, denom))
    chosen = [m for m in range(4) if estimates[m][1] > 0.0]
    ranking = sorted(chosen, key=lambda m: -estimates[m][1])
    columns = []
    pairs = []
    for m in ranking:
        eigen_pair = estimates[m]
        system = [
            [
                (
                    inverse[i][j] - (eigen_pair[0] if i == j else 0.0),
                    -(eigen_pair[1] if i == j else 0.0),
                )
                for j in range(4)
            ]
            for i in range(3)
        ]
        rows_left = [
            [system[i][j] for j in range(3)] + [(-system[i][3][0], -system[i][3][1])]
            for i in range(3)
        ]
        for col in range(3):
            pivot_row = max(
                range(col, 3), key=lambda r: rows_left[r][col][0] ** 2 + rows_left[r][col][1] ** 2
            )
            rows_left[col], rows_left[pivot_row] = (rows_left[pivot_row], rows_left[col])
            leading = rows_left[col][col]
            rows_left[col] = [pair_div(v, leading) for v in rows_left[col]]
            for r in range(3):
                if r != col:
                    factor = rows_left[r][col]
                    rows_left[r] = [
                        pair_sub(a, pair_mul(factor, b))
                        for a, b in zip(rows_left[r], rows_left[col])
                    ]
        vector = [rows_left[i][3] for i in range(3)] + [(1.0, 0.0)]
        columns.append([v[0] for v in vector])
        columns.append([v[1] for v in vector])
        pairs.append((eigen_pair[0], eigen_pair[1]))
    eigen_basis = [[columns[j][i] for j in range(4)] for i in range(4)]
    basis_inverse = invert_table(eigen_basis)
    return (tableau, inverse, eigen_basis, basis_inverse, pairs)


def near(plane, member):
    if member == 0:
        return pltpu.roll(plane, plane.shape[0] - 1, 0)
    if member == 1:
        return pltpu.roll(plane, 1, 0)
    if member == 2:
        return pltpu.roll(plane, plane.shape[1] - 1, 1)
    return pltpu.roll(plane, 1, 1)


def kernel(
    sx_count, sy_count, tables,
    prev_any, sec_any, diff_any, react_any, out_ref,
    prev_ref, sec_ref, diff_ref, react_ref,
    ext_a, ext_b, faces, face_x, alpha, beta, *rest,
):
    hist, rest = rest[:DEPTH], rest[DEPTH:]
    powers, rest = rest[: ITERS - 1], rest[ITERS - 1 :]
    (
    basis, part, part_out, part_in, corr_out, corr_in,
    pack_a, got_a, pack_b, got_b, pack_c, got_c, gram, load_sem,
    send_sem, recv_sem, gram_send, gram_recv,
    ) = rest
    depth_z, lanes = ext_a.shape[2], prev_ref.shape[1]
    rows = prev_ref.shape[0] // depth_z
    top = DEPTH + rows
    group = rows
    sx, sy, half = lax.axis_index("sx"), lax.axis_index("sy"), lax.axis_index("section")
    q_table, c_table, p_table, pairs = tables

    def pick(first, second):
        return jnp.where(half == 0, jnp.float32(first), jnp.float32(second))

    barrier = pltpu.get_barrier_semaphore()
    members = sx_count * sy_count
    me = sx * sy_count + sy

    def member_at(offset):
        other = lax.rem(me + offset, members)
        return {"sx": other // sy_count, "sy": lax.rem(other, sy_count)}

    loads = [
        pltpu.make_async_copy(source, target, load_sem.at[at])
        for at, (source, target) in enumerate((
            (sec_any, sec_ref), (diff_any, diff_ref), (prev_any, prev_ref), (react_any, react_ref),
        ))
    ]
    for one in loads:
        one.start()
    ext_a[...] = jnp.zeros_like(ext_a)
    ext_b[...] = jnp.zeros_like(ext_b)
    got_a[...] = jnp.zeros_like(got_a)
    got_b[...] = jnp.zeros_like(got_b)
    got_c[...] = jnp.zeros_like(got_c)
    for field in range(2):
        hist[0][field] = jnp.zeros(hist[0].shape[1:], jnp.float32)

    def greet(offset, carry):
        pl.semaphore_signal(barrier, inc=1, device_id=member_at(offset), device_id_type=MESH)
        return carry

    lax.fori_loop(1, members, greet, 0)
    pl.semaphore_signal(barrier, inc=1, device_id={"section": 1 - half}, device_id_type=MESH)

    lane_group = lax.broadcasted_iota(jnp.int32, (depth_z, lanes), 1) // DEPTH

    def pack(plane_of, low, high):
        down = jnp.zeros((depth_z, lanes), jnp.float32)
        up = jnp.zeros((depth_z, lanes), jnp.float32)
        for x in range(rows):
            plane = plane_of(x)
            if x > 0:
                plane = pltpu.roll(plane, DEPTH * x, 1)
            down = jnp.where(lane_group == x, plane, down)
            up = jnp.where(lane_group == (x + group - 1) % group, plane, up)
        low[...] = down
        high[...] = up

    def unpack(from_high, from_low, members_x, store):
        for x in members_x:
            mixed = jnp.where(
                lane_group == x,
                from_high,
                jnp.where(lane_group == (x + group - 1) % group, from_low, 0.0),
            )
            if x > 0:
                mixed = pltpu.roll(mixed, lanes - DEPTH * x, 1)
            store(x, mixed)

    def unpack_wide(got, j, target):
        for place, members_x in ((0, range(rows - DEPTH, rows)), (1, range(rows)), (2, range(DEPTH))):
            first = (DEPTH - rows, DEPTH, top)[place]

            def store(x, plane):
                target[j, first + x, :, lanes : 2 * lanes] = plane

            unpack(got[0, place, j], got[1, place, j], members_x, store)

    def column(ref, x):
        return ref[pl.ds(x, depth_z, stride=rows), :]

    for one in loads:
        one.wait()

    def planes(fn, least, most, batch):
        def several(at, carry):
            stores = []
            for step in range(batch):
                stores.append(fn(least + at * batch + step))
            for store in stores:
                store()
            return carry

        lax.fori_loop(0, (most - least) // batch, several, 0)

    def own_coefs(x):
        before, diffusivity = column(prev_ref, x), column(diff_ref, x)
        cells = [column(sec_ref.at[j], x) for j in range(2)]
        coefs = [diffusivity * (1.0 + 0.5 * jnp.tanh(cells[j])) for j in range(2)]
        coef = diffusivity * (1.0 + 0.5 * jnp.tanh(before))
        slope = column(react_ref, x) * (1.0 - 3.0 * before * before)

        def store():
            for j in range(2):
                ext_a[j, x + DEPTH, :, 0:lanes] = cells[j]
                ext_a[2 + j, x + DEPTH, :, 0:lanes] = coefs[j]
            ext_b[0, x + DEPTH, :, 0:lanes] = coef
            ext_b[1, x + DEPTH, :, 0:lanes] = slope

        return store

    planes(own_coefs, 0, rows, 2)
    for j in range(4):
        pack(lambda x: ext_a[j, x + DEPTH, :, 0:lanes], pack_a.at[0, j], pack_a.at[1, j])
    for j in range(2):
        pack(lambda x: ext_b[j, x + DEPTH, :, 0:lanes], pack_b.at[0, j], pack_b.at[1, j])

    pl.semaphore_wait(barrier, members)

    used = [0]

    def copy(source, target, device):
        at = used[0]
        used[0] += 1
        return pltpu.make_async_remote_copy(
            src_ref=source,
            dst_ref=target,
            send_sem=send_sem.at[at],
            recv_sem=recv_sem.at[at],
            device_id=device,
            device_id_type=MESH,
        )

    wide = rows + 2 * DEPTH
    left, right = lax.rem(sx + sx_count - 1, sx_count), lax.rem(sx + 1, sx_count)
    below, above = lax.rem(sy + sy_count - 1, sy_count), lax.rem(sy + 1, sy_count)
    has_left, has_right = sx > 0, sx < sx_count - 1
    has_below, has_above = sy > 0, sy < sy_count - 1
    own = pl.ds(0, lanes)
    low_rows, high_rows = pl.ds(0, DEPTH), pl.ds(top, DEPTH)

    def slabs(low_source, high_source, target):
        return [
            (has_left, has_right, copy(low_source, target(high_rows), {"sx": left})),
            (has_right, has_left, copy(high_source, target(low_rows), {"sx": right})),
        ]

    def strips(packed, got, corners):
        result = []
        for side, device, out_ok, in_ok in (
            (0, below, has_below, has_above),
            (1, above, has_above, has_below),
        ):
            middle = got.at[side, 1] if corners else got.at[side]
            result.append((out_ok, in_ok, copy(packed.at[side], middle, {"sy": device})))
            if corners:
                result.append((
                    out_ok & has_left,
                    in_ok & has_right,
                    copy(
                        packed.at[side],
                        got.at[side, 2],
                        {"sx": left, "sy": device},
                    ),
                ))
                result.append((
                    out_ok & has_right,
                    in_ok & has_left,
                    copy(
                        packed.at[side],
                        got.at[side, 0],
                        {"sx": right, "sy": device},
                    ),
                ))
        return result

    def start(copies):
        for out_ok, in_ok, one in copies:
            pl.when(out_ok)(one.start)

    def receive(copies):
        for out_ok, in_ok, one in copies:
            pl.when(in_ok)(one.wait_recv)

    def release(copies):
        for out_ok, in_ok, one in copies:
            pl.when(out_ok)(one.wait_send)

    copies_a = strips(pack_a, got_a, False)
    edge = pl.ds(top, 1), pl.ds(DEPTH - 1, 1)
    copies_a.append((
        has_left,
        has_right,
        copy(
            ext_a.at[:, pl.ds(DEPTH, 1), :, own],
            ext_a.at[:, edge[0], :, own],
            {"sx": left},
        ),
    ))
    copies_a.append((
        has_right,
        has_left,
        copy(
            ext_a.at[:, pl.ds(top - 1, 1), :, own],
            ext_a.at[:, edge[1], :, own],
            {"sx": right},
        ),
    ))
    start(copies_a)
    copies_b = strips(pack_b, got_b, True)
    copies_b += slabs(
        ext_b.at[:, pl.ds(DEPTH, DEPTH), :, own],
        ext_b.at[:, pl.ds(top - DEPTH, DEPTH), :, own],
        lambda where: ext_b.at[:, where, :, own],
    )
    start(copies_b)

    receive(copies_a)

    for j in range(4):
        def put_a(x, plane):
            ext_a[j, x + DEPTH, :, lanes : 2 * lanes] = plane

        unpack(got_a[0, j], got_a[1, j], range(rows), put_a)

    q_own = [[pick(q_table[m][j], q_table[2 + m][2 + j]) for j in range(2)] for m in range(2)]
    q_far = [[pick(q_table[2 + m][j], q_table[m][2 + j]) for j in range(2)] for m in range(2)]
    c_own = [[pick(c_table[m][j], c_table[2 + m][2 + j]) for j in range(2)] for m in range(2)]
    c_far = [[pick(c_table[2 + m][j], c_table[m][2 + j]) for j in range(2)] for m in range(2)]

    def middle(plane):
        return plane[:, 0:lanes]

    z_at = lax.broadcasted_iota(jnp.int32, (depth_z, 2 * lanes), 0)
    has_next = (z_at < depth_z - 1, z_at > 0)

    def around_z(plane, member):
        mask = has_next[member][:, 0 : plane.shape[1]]
        return jnp.where(mask, near(plane, member), 0.0)

    def fluxes(x):
        flux, increment = [], []
        for j in range(2):
            cells, coefs = ext_a[j, x + DEPTH], ext_a[2 + j, x + DEPTH]
            here, coef_here = middle(cells), middle(coefs)
            total = jnp.zeros_like(here)
            for member in range(2):
                face = 0.5 * (coef_here + around_z(coef_here, member))
                total = total + face * (around_z(here, member) - here)
            for member in (2, 3):
                face = 0.5 * (coef_here + middle(near(coefs, member)))
                total = total + face * (middle(near(cells, member)) - here)
            for place in (x + DEPTH - 1, x + DEPTH + 1):
                face = 0.5 * (coef_here + ext_a[2 + j, place, :, 0:lanes])
                total = total + face * (ext_a[j, place, :, 0:lanes] - here)
            flux.append(total + column(react_ref, x) * here * (1.0 - here * here))
            increment.append(here - column(prev_ref, x))
        near_part = [
            q_own[m][0] * flux[0] + q_own[m][1] * flux[1]
            - c_own[m][0] * increment[0] - c_own[m][1] * increment[1]
            for m in range(2)
        ]
        far_part = [
            q_far[m][0] * flux[0] + q_far[m][1] * flux[1]
            - c_far[m][0] * increment[0] - c_far[m][1] * increment[1]
            for m in range(2)
        ]

        def store():
            for m in range(2):
                part[m, x] = near_part[m]
                part_out[m, x] = far_part[m]

        return store

    chunk = rows // 4
    swap = []
    for at in range(4):
        planes(fluxes, at * chunk, (at + 1) * chunk, 2)
        piece = pl.ds(at * chunk, chunk)
        one = copy(part_out.at[:, piece], part_in.at[:, piece], {"section": 1 - half})
        one.start()
        swap.append(one)

    receive(copies_b)

    for j in range(2):
        unpack_wide(got_b, j, ext_b)

    real_part = pick(pairs[0][0] / step_size, pairs[1][0] / step_size)
    coupling = pick(pairs[0][1] / step_size, pairs[1][1] / step_size)
    lane_at = lax.broadcasted_iota(jnp.int32, (depth_z, 2 * lanes), 1)
    inside = (
        (lane_at < lanes)
        | ((lane_at < lanes + DEPTH) & has_above)
        | ((lane_at >= 2 * lanes - DEPTH) & has_below)
    )
    keep = inside.astype(jnp.float32)

    def x_faces(x):
        face = 0.5 * (ext_b[0, x] + ext_b[0, x + 1])

        def store():
            face_x[x] = face

        return store

    planes(x_faces, 0, wide - 1, 1)

    def operator(x):
        coefs = ext_b[0, x]
        diag = real_part - ext_b[1, x] + face_x[x - 1] + face_x[x]
        sides = []
        for member in range(2):
            face = 0.5 * (coefs + around_z(coefs, member))
            diag = diag + face
            sides.append(jnp.where(has_next[member], face, 0.0))
        for member in (2, 3):
            face = 0.5 * (coefs + near(coefs, member))
            diag = diag + face
            sides.append(face)
        inside_x = ((x >= DEPTH) | has_left) & ((x < top) | has_right)
        scale = keep / (diag * diag + coupling * coupling)
        scale = jnp.where(inside_x, scale, 0.0)

        def store():
            for member in range(4):
                faces[member, x] = sides[member]
            alpha[x] = diag * scale
            beta[x] = coupling * scale

        return store

    planes(operator, 1, wide - 1, 2)

    def first_scaled(x):
        rhs = [part[m, x] + part_in[m, x] for m in range(2)]
        a, b = middle(alpha[x + DEPTH]), middle(beta[x + DEPTH])

        def store():
            for m in range(2):
                basis[0, m, x] = rhs[m]
            hist[0][0, x + DEPTH, :, 0:lanes] = a * rhs[0] - b * rhs[1]
            hist[0][1, x + DEPTH, :, 0:lanes] = b * rhs[0] + a * rhs[1]

        return store

    copies_c = slabs(
        hist[0].at[:, pl.ds(DEPTH, DEPTH), :, own],
        hist[0].at[:, pl.ds(top - DEPTH, DEPTH), :, own],
        lambda where: hist[0].at[:, where, :, own],
    )
    for at in range(4):
        swap[at].wait_recv()
        planes(first_scaled, at * chunk, (at + 1) * chunk, chunk)
        if (at + 1) * chunk == DEPTH:
            start(copies_c[0:1])
        if (at + 1) * chunk == rows:
            start(copies_c[1:2])
    for j in range(2):
        pack(lambda x: hist[0][j, x + DEPTH, :, 0:lanes], pack_c.at[0, j], pack_c.at[1, j])
    more_c = strips(pack_c, got_c, True)
    start(more_c)
    copies_c = copies_c + more_c
    receive(copies_c)
    for j in range(2):
        unpack_wide(got_c, j, hist[0])

    for m in range(DEPTH - 1):
        def apply(x):
            around = []
            for field in range(2):
                cells = hist[m][field, x]
                total = face_x[x - 1] * hist[m][field, x - 1] + face_x[x] * hist[m][field, x + 1]
                for member in range(4):
                    total = total + faces[member, x] * near(cells, member)
                around.append(total)
            a, b = alpha[x], beta[x]
            scaled = [a * around[0] - b * around[1], b * around[0] + a * around[1]]

            def store():
                for field in range(2):
                    if m % 2 == 1:
                        powers[(m - 1) // 2][field, x] = middle(around[field])
                    hist[m + 1][field, x] = scaled[field]

            return store

        planes(apply, m + 1, wide - 1 - m, 2)

    index = [(i, j) for i in range(ITERS + 1) for j in range(i, ITERS + 1)]

    def last_apply(x, carry):
        totals = list(carry)
        for field in range(2):
            at_x = x + DEPTH
            cells = hist[DEPTH - 1][field, at_x]
            total = middle(face_x[at_x - 1]) * hist[DEPTH - 1][field, at_x - 1, :, 0:lanes]
            total = total + middle(face_x[at_x]) * hist[DEPTH - 1][field, at_x + 1, :, 0:lanes]
            for member in range(2):
                total = total + middle(faces[member, at_x]) * near(middle(cells), member)
            for member in (2, 3):
                total = total + middle(faces[member, at_x]) * middle(near(cells, member))
            members_of = [basis[0, field, x]]
            members_of += [powers[k][field, at_x] for k in range(ITERS - 1)] + [total]
            for at, (i, j) in enumerate(index):
                product = members_of[i] * members_of[j]
                for r in range(0, depth_z, 8):
                    totals[at] = totals[at] + product[r : r + 8]
        return tuple(totals)

    zeros = tuple(jnp.zeros((8, lanes), jnp.float32) for pair in index)
    sums = lax.fori_loop(0, rows, last_apply, zeros)
    square = jnp.concatenate(
        [jnp.sum(total, axis=0, keepdims=True) for total in sums]
        + [jnp.zeros((16 - len(index), lanes), jnp.float32)],
        axis=0,
    )
    diagonal = lax.broadcasted_iota(jnp.int32, (16, lanes), 0) == lax.broadcasted_iota(
        jnp.int32, (16, lanes), 1
    )
    square = jnp.where(diagonal, jnp.sum(square, axis=1, keepdims=True), 0.0)
    gram[0] = jnp.sum(square, axis=0, keepdims=True)

    def gram_copy(offset):
        return pltpu.make_async_remote_copy(
            src_ref=gram.at[0],
            dst_ref=gram.at[offset],
            send_sem=gram_send.at[offset],
            recv_sem=gram_recv.at[offset],
            device_id=member_at(offset),
            device_id_type=MESH,
        )

    def gram_start(offset, carry):
        gram_copy(offset).start()
        return carry

    def gram_take(offset, carry):
        gram_copy(offset).wait_recv()
        return carry

    def gram_release(offset, carry):
        gram_copy(offset).wait_send()
        return carry

    lax.fori_loop(1, members, gram_start, 0)
    release(copies_a)
    release(copies_b)
    release(copies_c)
    for one in swap:
        one.wait_send()
    lax.fori_loop(1, members, gram_take, 0)
    turn = [lax.rem(me - place + members, members) for place in range(members)]
    table = gram[turn[0]]
    for place in range(1, members):
        table = table + gram[turn[place]]
    table = jnp.where(diagonal, jnp.broadcast_to(table, (16, lanes)), 0.0)
    table = jnp.sum(table, axis=1, keepdims=True)
    entry = {}
    for at, (i, j) in enumerate(index):
        entry[i, j] = entry[j, i] = table[at : at + 1, :]

    weights = {0: jnp.ones((1, 1), jnp.float32)}
    gains = {}
    for sweep in range(ITERS):
        image = {}
        for j in range(sweep + 2):
            if j in weights and j - 1 in weights:
                image[j] = weights[j] - weights[j - 1]
            elif j in weights:
                image[j] = weights[j]
            else:
                image[j] = -weights[j - 1]
        against = {
            j: functools.reduce(jnp.add, [image[i] * entry[i, j] for i in image]) for j in image
        }
        numerator = functools.reduce(jnp.add, [against[j] * weights[j] for j in weights])
        denominator = functools.reduce(jnp.add, [against[j] * image[j] for j in image])
        step = numerator / (denominator + tiny_value)
        for j in weights:
            gains[j] = gains[j] + step * weights[j] if j in gains else step * weights[j]
        weights = {
            j: (weights[j] - step * image[j]) if j in weights else -step * image[j] for j in image
        }

    p_own = [[pick(p_table[j][m], p_table[2 + j][2 + m]) for m in range(2)] for j in range(2)]
    p_far = [[pick(p_table[2 + j][m], p_table[j][2 + m]) for m in range(2)] for j in range(2)]
    gain_at = [jnp.broadcast_to(gains[k], (depth_z, lanes)) for k in range(ITERS)]

    def correct(x):
        fix = []
        for field in range(2):
            total = None
            for k in range(ITERS):
                search = (
                    hist[2 * k][field, x + DEPTH, :, 0:lanes]
                    + hist[2 * k + 1][field, x + DEPTH, :, 0:lanes]
                )
                total = gain_at[k] * search if total is None else total + gain_at[k] * search
            fix.append(total)
        base = [ext_a[j, x + DEPTH, :, 0:lanes] for j in range(2)]

        def store():
            for j in range(2):
                corr_out[j, x] = p_far[j][0] * fix[0] + p_far[j][1] * fix[1]
                part[j, x] = base[j] + p_own[j][0] * fix[0] + p_own[j][1] * fix[1]

        return store

    final = []
    for at in range(4):
        planes(correct, at * chunk, (at + 1) * chunk, 4)
        piece = pl.ds(at * chunk, chunk)
        one = copy(corr_out.at[:, piece], corr_in.at[:, piece], {"section": 1 - half})
        one.start()
        final.append(one)
    for at in range(4):
        final[at].wait_recv()

        for x in range(at * chunk, (at + 1) * chunk):
            for j in range(2):
                out_ref[j, pl.ds(x, depth_z, stride=rows), :] = part[j, x] + corr_in[j, x]
    for one in final:
        one.wait_send()
    lax.fori_loop(1, members, gram_release, 0)


def solution(mesh):
    sx_count, sy_count = mesh.shape["sx"], mesh.shape["sy"]
    tableau, inverse, eigen_basis, basis_inverse, pairs = radau_tables()
    shift_table = table_product(basis_inverse, inverse)
    shift_table = [[v / step_size for v in row_values] for row_values in shift_table]
    tables = (basis_inverse, shift_table, eigen_basis, pairs)

    def body(previous, sections, diffusivity, reaction):
        depth_z, rows, lanes = previous.shape
        wide = rows + 2 * DEPTH
        f32 = jnp.float32
        vmem = pltpu.VMEM
        ext = (wide, depth_z, 2 * lanes)
        block = (2, rows, depth_z, lanes)
        flat = (depth_z * rows, lanes)
        members = sx_count * sy_count
        return pl.pallas_call(
            functools.partial(kernel, sx_count, sy_count, tables),
            out_shape=jax.ShapeDtypeStruct((2,) + flat, f32),
            in_specs=[pl.BlockSpec(memory_space=pltpu.HBM)] * 4,
            out_specs=pl.BlockSpec(memory_space=pltpu.VMEM),
            scratch_shapes=[
                vmem(flat, f32),
                vmem((2,) + flat, f32),
                vmem(flat, f32),
                vmem(flat, f32),
                vmem((4,) + ext, f32),
                vmem((2,) + ext, f32),
                vmem((4,) + ext, f32),
                vmem(ext, f32),
                vmem(ext, f32),
                vmem(ext, f32),
                *[vmem((2,) + ext, f32) for m in range(DEPTH)],
                *[vmem((2, wide, depth_z, lanes), f32) for m in range(ITERS - 1)],
                vmem((1,) + block, f32),
                vmem(block, f32),
                vmem(block, f32),
                vmem(block, f32),
                vmem(block, f32),
                vmem(block, f32),
                vmem((2, 4, depth_z, lanes), f32),
                vmem((2, 4, depth_z, lanes), f32),
                vmem((2, 2, depth_z, lanes), f32),
                vmem((2, 3, 2, depth_z, lanes), f32),
                vmem((2, 2, depth_z, lanes), f32),
                vmem((2, 3, 2, depth_z, lanes), f32),
                vmem((members, 1, lanes), f32),
                pltpu.SemaphoreType.DMA((4,)),
                pltpu.SemaphoreType.DMA((32,)),
                pltpu.SemaphoreType.DMA((32,)),
                pltpu.SemaphoreType.DMA((members,)),
                pltpu.SemaphoreType.DMA((members,)),
            ],
            compiler_params=pltpu.CompilerParams(
                collective_id=0, has_side_effects=True, vmem_limit_bytes=48 * 1024 * 1024
            ),
        )(
            previous.reshape(flat),
            sections.reshape((2,) + flat),
            diffusivity.reshape(flat),
            reaction.reshape(flat),
        ).reshape(sections.shape)

    in_specs = (
        P(None, "sx", "sy"),
        P("section", None, "sx", "sy"),
        P(None, "sx", "sy"),
        P(None, "sx", "sy"),
    )
    out_specs = P("section", None, "sx", "sy")
    return jax.shard_map(body, mesh=mesh, in_specs=in_specs, out_specs=out_specs, check_vma=False)
```

```python
import functools

import jax
import jax.numpy as jnp
from jax import lax
from jax.experimental import pallas as pl
from jax.experimental.pallas import tpu as pltpu
from jax.sharding import PartitionSpec as P

ITERS = 4
DEPTH = 2 * ITERS
MESH = pl.DeviceIdType.MESH

step_size = 1.0
tiny_value = 1e-06


def invert_table(matrix):
    order_n = len(matrix)
    augmented = [
        list(matrix[r]) + [1.0 if c == r else 0.0 for c in range(order_n)] for r in range(order_n)
    ]
    for col in range(order_n):
        pivot_row = max(range(col, order_n), key=lambda r: abs(augmented[r][col]))
        augmented[col], augmented[pivot_row] = (augmented[pivot_row], augmented[col])
        leading = augmented[col][col]
        augmented[col] = [v / leading for v in augmented[col]]
        for r in range(order_n):
            if r != col:
                factor = augmented[r][col]
                augmented[r] = [a - factor * b for a, b in zip(augmented[r], augmented[col])]
    return [row_values[order_n:] for row_values in augmented]


def table_product(left, right):
    return [
        [sum((left[i][k] * right[k][j] for k in range(len(right)))) for j in range(len(right[0]))]
        for i in range(len(left))
    ]


def pair_add(first, second):
    return (first[0] + second[0], first[1] + second[1])


def pair_sub(first, second):
    return (first[0] - second[0], first[1] - second[1])


def pair_mul(first, second):
    return (
        first[0] * second[0] - first[1] * second[1],
        first[0] * second[1] + first[1] * second[0],
    )


def pair_div(first, second):
    scale_sq = second[0] * second[0] + second[1] * second[1]
    return (
        (first[0] * second[0] + first[1] * second[1]) / scale_sq,
        (first[1] * second[0] - first[0] * second[1]) / scale_sq,
    )


def quartic_value(point):
    return (((210.0 * point - 480.0) * point + 360.0) * point - 96.0) * point + 6.0


def bisect_root(lower, upper):
    for count in range(200):
        middle = 0.5 * (lower + upper)
        if (quartic_value(lower) < 0.0) == (quartic_value(middle) < 0.0):
            lower = middle
        else:
            upper = middle
    return 0.5 * (lower + upper)


def radau_tables():
    abscissae = []
    grid_steps = 4000
    for m in range(grid_steps):
        lower = 0.999 * m / grid_steps
        upper = 0.999 * (m + 1) / grid_steps
        if (quartic_value(lower) < 0.0) != (quartic_value(upper) < 0.0):
            abscissae.append(bisect_root(lower, upper))
    abscissae.append(1.0)
    vander = [[abscissae[j] ** k for k in range(4)] for j in range(4)]
    moments = [[abscissae[i] ** (k + 1) / (k + 1) for k in range(4)] for i in range(4)]
    tableau = table_product(moments, invert_table(vander))
    inverse = invert_table(tableau)
    running = [list(row_values) for row_values in inverse]
    coeffs = []
    for k in range(1, 5):
        trace_value = sum((running[i][i] for i in range(4)))
        coeffs.append(-trace_value / k)
        shifted_table = [
            [running[i][j] + (coeffs[-1] if i == j else 0.0) for j in range(4)] for i in range(4)
        ]
        running = table_product(inverse, shifted_table)
    start_point = (0.4, 0.9)
    estimates = [(1.0, 0.0)]
    for k in range(3):
        estimates.append(pair_mul(estimates[-1], start_point))
    for count in range(500):
        for i in range(4):
            value = (1.0, 0.0)
            for coef_value in coeffs:
                value = pair_add(pair_mul(value, estimates[i]), (coef_value, 0.0))
            denom = (1.0, 0.0)
            for j in range(4):
                if j != i:
                    denom = pair_mul(denom, pair_sub(estimates[i], estimates[j]))
            estimates[i] = pair_sub(estimates[i], pair_div(value, denom))
    chosen = [m for m in range(4) if estimates[m][1] > 0.0]
    ranking = sorted(chosen, key=lambda m: -estimates[m][1])
    columns = []
    pairs = []
    for m in ranking:
        eigen_pair = estimates[m]
        system = [
            [
                (
                    inverse[i][j] - (eigen_pair[0] if i == j else 0.0),
                    -(eigen_pair[1] if i == j else 0.0),
                )
                for j in range(4)
            ]
            for i in range(3)
        ]
        rows_left = [
            [system[i][j] for j in range(3)] + [(-system[i][3][0], -system[i][3][1])]
            for i in range(3)
        ]
        for col in range(3):
            pivot_row = max(
                range(col, 3), key=lambda r: rows_left[r][col][0] ** 2 + rows_left[r][col][1] ** 2
            )
            rows_left[col], rows_left[pivot_row] = (rows_left[pivot_row], rows_left[col])
            leading = rows_left[col][col]
            rows_left[col] = [pair_div(v, leading) for v in rows_left[col]]
            for r in range(3):
                if r != col:
                    factor = rows_left[r][col]
                    rows_left[r] = [
                        pair_sub(a, pair_mul(factor, b))
                        for a, b in zip(rows_left[r], rows_left[col])
                    ]
        vector = [rows_left[i][3] for i in range(3)] + [(1.0, 0.0)]
        columns.append([v[0] for v in vector])
        columns.append([v[1] for v in vector])
        pairs.append((eigen_pair[0], eigen_pair[1]))
    eigen_basis = [[columns[j][i] for j in range(4)] for i in range(4)]
    basis_inverse = invert_table(eigen_basis)
    return (tableau, inverse, eigen_basis, basis_inverse, pairs)


def near(plane, member):
    if member == 0:
        return pltpu.roll(plane, plane.shape[0] - 1, 0)
    if member == 1:
        return pltpu.roll(plane, 1, 0)
    if member == 2:
        return pltpu.roll(plane, plane.shape[1] - 1, 1)
    return pltpu.roll(plane, 1, 1)


def kernel(
    sx_count, sy_count, tables,
    prev_any, sec_any, diff_any, react_any, out_ref,
    prev_ref, sec_ref, diff_ref, react_ref,
    ext_a, ext_b, faces, face_x, alpha, beta, *rest,
):
    hist, rest = rest[:DEPTH], rest[DEPTH:]
    powers, rest = rest[: ITERS - 1], rest[ITERS - 1 :]
    (
    basis, part, part_out, part_in, corr_out, corr_in,
    pack_a, got_a, pack_b, got_b, pack_c, got_c, gram, load_sem,
    send_sem, recv_sem, gram_send, gram_recv,
    ) = rest
    depth_z, lanes = ext_a.shape[2], prev_ref.shape[1]
    rows = prev_ref.shape[0] // depth_z
    top = DEPTH + rows
    group = rows
    sx, sy, half = lax.axis_index("sx"), lax.axis_index("sy"), lax.axis_index("section")
    q_table, c_table, p_table, pairs = tables

    def pick(first, second):
        return jnp.where(half == 0, jnp.float32(first), jnp.float32(second))

    barrier = pltpu.get_barrier_semaphore()
    members = sx_count * sy_count
    me = sx * sy_count + sy

    def member_at(offset):
        other = lax.rem(me + offset, members)
        return {"sx": other // sy_count, "sy": lax.rem(other, sy_count)}

    loads = [
        pltpu.make_async_copy(source, target, load_sem.at[at])
        for at, (source, target) in enumerate((
            (sec_any, sec_ref), (diff_any, diff_ref), (prev_any, prev_ref), (react_any, react_ref),
        ))
    ]
    for one in loads:
        one.start()
    ext_a[...] = jnp.zeros_like(ext_a)
    ext_b[...] = jnp.zeros_like(ext_b)
    got_a[...] = jnp.zeros_like(got_a)
    got_b[...] = jnp.zeros_like(got_b)
    got_c[...] = jnp.zeros_like(got_c)
    for field in range(2):
        hist[0][field] = jnp.zeros(hist[0].shape[1:], jnp.float32)

    def greet(offset, carry):
        pl.semaphore_signal(barrier, inc=1, device_id=member_at(offset), device_id_type=MESH)
        return carry

    lax.fori_loop(1, members, greet, 0)
    pl.semaphore_signal(barrier, inc=1, device_id={"section": 1 - half}, device_id_type=MESH)

    lane_group = lax.broadcasted_iota(jnp.int32, (depth_z, lanes), 1) // DEPTH

    def pack(plane_of, low, high):
        down = jnp.zeros((depth_z, lanes), jnp.float32)
        up = jnp.zeros((depth_z, lanes), jnp.float32)
        for x in range(rows):
            plane = plane_of(x)
            if x > 0:
                plane = pltpu.roll(plane, DEPTH * x, 1)
            down = jnp.where(lane_group == x, plane, down)
            up = jnp.where(lane_group == (x + group - 1) % group, plane, up)
        low[...] = down
        high[...] = up

    def unpack(from_high, from_low, members_x, store):
        for x in members_x:
            mixed = jnp.where(
                lane_group == x,
                from_high,
                jnp.where(lane_group == (x + group - 1) % group, from_low, 0.0),
            )
            if x > 0:
                mixed = pltpu.roll(mixed, lanes - DEPTH * x, 1)
            store(x, mixed)

    def unpack_wide(got, j, target):
        for place, members_x in ((0, range(rows - DEPTH, rows)), (1, range(rows)), (2, range(DEPTH))):
            first = (DEPTH - rows, DEPTH, top)[place]

            def store(x, plane):
                target[j, first + x, :, lanes : 2 * lanes] = plane

            unpack(got[0, place, j], got[1, place, j], members_x, store)

    def column(ref, x):
        return ref[pl.ds(x, depth_z, stride=rows), :]

    for one in loads:
        one.wait()

    def planes(fn, least, most, batch):
        def several(first, count):
            stores = [fn(first + step) for step in range(count)]
            for store in stores:
                store()

        full, left_over = (most - least) // batch, (most - least) % batch
        if full == 1:
            several(least, batch)
        else:
            def turn(at, carry):
                several(least + at * batch, batch)
                return carry

            lax.fori_loop(0, full, turn, 0)
        if left_over:
            several(most - left_over, left_over)

    def own_coefs(x):
        before, diffusivity = column(prev_ref, x), column(diff_ref, x)
        cells = [column(sec_ref.at[j], x) for j in range(2)]
        coefs = [diffusivity * (1.0 + 0.5 * jnp.tanh(cells[j])) for j in range(2)]
        coef = diffusivity * (1.0 + 0.5 * jnp.tanh(before))
        slope = column(react_ref, x) * (1.0 - 3.0 * before * before)

        def store():
            for j in range(2):
                ext_a[j, x + DEPTH, :, 0:lanes] = cells[j]
                ext_a[2 + j, x + DEPTH, :, 0:lanes] = coefs[j]
            ext_b[0, x + DEPTH, :, 0:lanes] = coef
            ext_b[1, x + DEPTH, :, 0:lanes] = slope

        return store

    planes(own_coefs, 0, rows, 4)
    for j in range(4):
        pack(lambda x: ext_a[j, x + DEPTH, :, 0:lanes], pack_a.at[0, j], pack_a.at[1, j])
    for j in range(2):
        pack(lambda x: ext_b[j, x + DEPTH, :, 0:lanes], pack_b.at[0, j], pack_b.at[1, j])

    pl.semaphore_wait(barrier, members)

    used = [0]

    def copy(source, target, device):
        at = used[0]
        used[0] += 1
        return pltpu.make_async_remote_copy(
            src_ref=source,
            dst_ref=target,
            send_sem=send_sem.at[at],
            recv_sem=recv_sem.at[at],
            device_id=device,
            device_id_type=MESH,
        )

    wide = rows + 2 * DEPTH
    left, right = lax.rem(sx + sx_count - 1, sx_count), lax.rem(sx + 1, sx_count)
    below, above = lax.rem(sy + sy_count - 1, sy_count), lax.rem(sy + 1, sy_count)
    has_left, has_right = sx > 0, sx < sx_count - 1
    has_below, has_above = sy > 0, sy < sy_count - 1
    own = pl.ds(0, lanes)
    low_rows, high_rows = pl.ds(0, DEPTH), pl.ds(top, DEPTH)

    def slabs(low_source, high_source, target):
        return [
            (has_left, has_right, copy(low_source, target(high_rows), {"sx": left})),
            (has_right, has_left, copy(high_source, target(low_rows), {"sx": right})),
        ]

    def strips(packed, got, corners):
        result = []
        for side, device, out_ok, in_ok in (
            (0, below, has_below, has_above),
            (1, above, has_above, has_below),
        ):
            middle = got.at[side, 1] if corners else got.at[side]
            result.append((out_ok, in_ok, copy(packed.at[side], middle, {"sy": device})))
            if corners:
                result.append((
                    out_ok & has_left,
                    in_ok & has_right,
                    copy(
                        packed.at[side],
                        got.at[side, 2],
                        {"sx": left, "sy": device},
                    ),
                ))
                result.append((
                    out_ok & has_right,
                    in_ok & has_left,
                    copy(
                        packed.at[side],
                        got.at[side, 0],
                        {"sx": right, "sy": device},
                    ),
                ))
        return result

    def start(copies):
        for out_ok, in_ok, one in copies:
            pl.when(out_ok)(one.start)

    def receive(copies):
        for out_ok, in_ok, one in copies:
            pl.when(in_ok)(one.wait_recv)

    def release(copies):
        for out_ok, in_ok, one in copies:
            pl.when(out_ok)(one.wait_send)

    copies_a = strips(pack_a, got_a, False)
    edge = pl.ds(top, 1), pl.ds(DEPTH - 1, 1)
    copies_a.append((
        has_left,
        has_right,
        copy(
            ext_a.at[:, pl.ds(DEPTH, 1), :, own],
            ext_a.at[:, edge[0], :, own],
            {"sx": left},
        ),
    ))
    copies_a.append((
        has_right,
        has_left,
        copy(
            ext_a.at[:, pl.ds(top - 1, 1), :, own],
            ext_a.at[:, edge[1], :, own],
            {"sx": right},
        ),
    ))
    start(copies_a)
    copies_b = strips(pack_b, got_b, True)
    copies_b += slabs(
        ext_b.at[:, pl.ds(DEPTH, DEPTH), :, own],
        ext_b.at[:, pl.ds(top - DEPTH, DEPTH), :, own],
        lambda where: ext_b.at[:, where, :, own],
    )
    start(copies_b)

    receive(copies_a)

    for j in range(4):
        def put_a(x, plane):
            ext_a[j, x + DEPTH, :, lanes : 2 * lanes] = plane

        unpack(got_a[0, j], got_a[1, j], range(rows), put_a)

    q_own = [[pick(q_table[m][j], q_table[2 + m][2 + j]) for j in range(2)] for m in range(2)]
    q_far = [[pick(q_table[2 + m][j], q_table[m][2 + j]) for j in range(2)] for m in range(2)]
    c_own = [[pick(c_table[m][j], c_table[2 + m][2 + j]) for j in range(2)] for m in range(2)]
    c_far = [[pick(c_table[2 + m][j], c_table[m][2 + j]) for j in range(2)] for m in range(2)]

    def middle(plane):
        return plane[:, 0:lanes]

    z_at = lax.broadcasted_iota(jnp.int32, (depth_z, 2 * lanes), 0)
    has_next = (z_at < depth_z - 1, z_at > 0)

    def around_z(plane, member):
        mask = has_next[member][:, 0 : plane.shape[1]]
        return jnp.where(mask, near(plane, member), 0.0)

    def fluxes(x):
        flux, increment = [], []
        for j in range(2):
            cells, coefs = ext_a[j, x + DEPTH], ext_a[2 + j, x + DEPTH]
            here, coef_here = middle(cells), middle(coefs)
            total = jnp.zeros_like(here)
            for member in range(2):
                face = 0.5 * (coef_here + around_z(coef_here, member))
                total = total + face * (around_z(here, member) - here)
            for member in (2, 3):
                face = 0.5 * (coef_here + middle(near(coefs, member)))
                total = total + face * (middle(near(cells, member)) - here)
            for place in (x + DEPTH - 1, x + DEPTH + 1):
                face = 0.5 * (coef_here + ext_a[2 + j, place, :, 0:lanes])
                total = total + face * (ext_a[j, place, :, 0:lanes] - here)
            flux.append(total + column(react_ref, x) * here * (1.0 - here * here))
            increment.append(here - column(prev_ref, x))
        near_part = [
            q_own[m][0] * flux[0] + q_own[m][1] * flux[1]
            - c_own[m][0] * increment[0] - c_own[m][1] * increment[1]
            for m in range(2)
        ]
        far_part = [
            q_far[m][0] * flux[0] + q_far[m][1] * flux[1]
            - c_far[m][0] * increment[0] - c_far[m][1] * increment[1]
            for m in range(2)
        ]

        def store():
            for m in range(2):
                part[m, x] = near_part[m]
                part_out[m, x] = far_part[m]

        return store

    chunk = rows // 4
    swap = []
    for at in range(4):
        planes(fluxes, at * chunk, (at + 1) * chunk, chunk)
        piece = pl.ds(at * chunk, chunk)
        one = copy(part_out.at[:, piece], part_in.at[:, piece], {"section": 1 - half})
        one.start()
        swap.append(one)

    receive(copies_b)

    for j in range(2):
        unpack_wide(got_b, j, ext_b)

    real_part = pick(pairs[0][0] / step_size, pairs[1][0] / step_size)
    coupling = pick(pairs[0][1] / step_size, pairs[1][1] / step_size)
    lane_at = lax.broadcasted_iota(jnp.int32, (depth_z, 2 * lanes), 1)
    inside = (
        (lane_at < lanes)
        | ((lane_at < lanes + DEPTH) & has_above)
        | ((lane_at >= 2 * lanes - DEPTH) & has_below)
    )
    keep = inside.astype(jnp.float32)

    def x_faces(x):
        face = 0.5 * (ext_b[0, x] + ext_b[0, x + 1])

        def store():
            face_x[x] = face

        return store

    planes(x_faces, 0, wide - 1, 4)

    def operator(x):
        coefs = ext_b[0, x]
        diag = real_part - ext_b[1, x] + face_x[x - 1] + face_x[x]
        sides = []
        for member in range(2):
            face = 0.5 * (coefs + around_z(coefs, member))
            diag = diag + face
            sides.append(jnp.where(has_next[member], face, 0.0))
        for member in (2, 3):
            face = 0.5 * (coefs + near(coefs, member))
            diag = diag + face
            sides.append(face)
        inside_x = ((x >= DEPTH) | has_left) & ((x < top) | has_right)
        scale = keep / (diag * diag + coupling * coupling)
        scale = jnp.where(inside_x, scale, 0.0)

        def store():
            for member in range(4):
                faces[member, x] = sides[member]
            alpha[x] = diag * scale
            beta[x] = coupling * scale

        return store

    planes(operator, 1, wide - 1, 2)

    def first_scaled(x):
        rhs = [part[m, x] + part_in[m, x] for m in range(2)]
        a, b = middle(alpha[x + DEPTH]), middle(beta[x + DEPTH])

        def store():
            for m in range(2):
                basis[0, m, x] = rhs[m]
            hist[0][0, x + DEPTH, :, 0:lanes] = a * rhs[0] - b * rhs[1]
            hist[0][1, x + DEPTH, :, 0:lanes] = b * rhs[0] + a * rhs[1]

        return store

    copies_c = slabs(
        hist[0].at[:, pl.ds(DEPTH, DEPTH), :, own],
        hist[0].at[:, pl.ds(top - DEPTH, DEPTH), :, own],
        lambda where: hist[0].at[:, where, :, own],
    )
    for at in range(4):
        swap[at].wait_recv()
        planes(first_scaled, at * chunk, (at + 1) * chunk, chunk)
        if (at + 1) * chunk == DEPTH:
            start(copies_c[0:1])
        if (at + 1) * chunk == rows:
            start(copies_c[1:2])
    for j in range(2):
        pack(lambda x: hist[0][j, x + DEPTH, :, 0:lanes], pack_c.at[0, j], pack_c.at[1, j])
    more_c = strips(pack_c, got_c, True)
    start(more_c)
    copies_c = copies_c + more_c
    receive(copies_c)
    for j in range(2):
        unpack_wide(got_c, j, hist[0])

    for m in range(DEPTH - 1):
        def apply(x):
            around = []
            for field in range(2):
                cells = hist[m][field, x]
                total = face_x[x - 1] * hist[m][field, x - 1] + face_x[x] * hist[m][field, x + 1]
                for member in range(4):
                    total = total + faces[member, x] * near(cells, member)
                around.append(total)
            a, b = alpha[x], beta[x]
            scaled = [a * around[0] - b * around[1], b * around[0] + a * around[1]]

            def store():
                for field in range(2):
                    if m % 2 == 1:
                        powers[(m - 1) // 2][field, x] = middle(around[field])
                    hist[m + 1][field, x] = scaled[field]

            return store

        planes(apply, m + 1, wide - 1 - m, 4)

    index = [(i, j) for i in range(ITERS + 1) for j in range(i, ITERS + 1)]

    def last_apply(at, carry):
        totals = list(carry)
        ends = {}
        for step in range(4):
            at_x = 4 * at + step + DEPTH
            for field in range(2):
                cells = hist[DEPTH - 1][field, at_x]
                total = middle(face_x[at_x - 1]) * hist[DEPTH - 1][field, at_x - 1, :, 0:lanes]
                total = total + middle(face_x[at_x]) * hist[DEPTH - 1][field, at_x + 1, :, 0:lanes]
                for member in range(2):
                    total = total + middle(faces[member, at_x]) * near(middle(cells), member)
                for member in (2, 3):
                    total = total + middle(faces[member, at_x]) * middle(near(cells, member))
                ends[step, field] = total
        for step in range(4):
            for field in range(2):
                members_of = [basis[0, field, 4 * at + step]]
                members_of += [powers[k][field, 4 * at + step + DEPTH] for k in range(ITERS - 1)]
                members_of += [ends[step, field]]
                for pair, (i, j) in enumerate(index):
                    product = members_of[i] * members_of[j]
                    for r in range(0, depth_z, 8):
                        totals[pair] = totals[pair] + product[r : r + 8]
        return tuple(totals)

    zeros = tuple(jnp.zeros((8, lanes), jnp.float32) for pair in index)
    sums = lax.fori_loop(0, rows // 4, last_apply, zeros)
    square = jnp.concatenate(
        [jnp.sum(total, axis=0, keepdims=True) for total in sums]
        + [jnp.zeros((16 - len(index), lanes), jnp.float32)],
        axis=0,
    )
    diagonal = lax.broadcasted_iota(jnp.int32, (16, lanes), 0) == lax.broadcasted_iota(
        jnp.int32, (16, lanes), 1
    )
    square = jnp.where(diagonal, jnp.sum(square, axis=1, keepdims=True), 0.0)
    gram[0] = jnp.sum(square, axis=0, keepdims=True)

    def gram_copy(offset):
        return pltpu.make_async_remote_copy(
            src_ref=gram.at[0],
            dst_ref=gram.at[offset],
            send_sem=gram_send.at[offset],
            recv_sem=gram_recv.at[offset],
            device_id=member_at(offset),
            device_id_type=MESH,
        )

    def gram_start(offset, carry):
        gram_copy(offset).start()
        return carry

    def gram_take(offset, carry):
        gram_copy(offset).wait_recv()
        return carry

    def gram_release(offset, carry):
        gram_copy(offset).wait_send()
        return carry

    lax.fori_loop(1, members, gram_start, 0)
    release(copies_a)
    release(copies_b)
    release(copies_c)
    for one in swap:
        one.wait_send()
    lax.fori_loop(1, members, gram_take, 0)
    turn = [lax.rem(me - place + members, members) for place in range(members)]
    table = gram[turn[0]]
    for place in range(1, members):
        table = table + gram[turn[place]]
    table = jnp.where(diagonal, jnp.broadcast_to(table, (16, lanes)), 0.0)
    table = jnp.sum(table, axis=1, keepdims=True)
    entry = {}
    for at, (i, j) in enumerate(index):
        entry[i, j] = entry[j, i] = table[at : at + 1, :]

    weights = {0: jnp.ones((1, 1), jnp.float32)}
    gains = {}
    for sweep in range(ITERS):
        image = {}
        for j in range(sweep + 2):
            if j in weights and j - 1 in weights:
                image[j] = weights[j] - weights[j - 1]
            elif j in weights:
                image[j] = weights[j]
            else:
                image[j] = -weights[j - 1]
        against = {
            j: functools.reduce(jnp.add, [image[i] * entry[i, j] for i in image]) for j in image
        }
        numerator = functools.reduce(jnp.add, [against[j] * weights[j] for j in weights])
        denominator = functools.reduce(jnp.add, [against[j] * image[j] for j in image])
        step = numerator / (denominator + tiny_value)
        for j in weights:
            gains[j] = gains[j] + step * weights[j] if j in gains else step * weights[j]
        weights = {
            j: (weights[j] - step * image[j]) if j in weights else -step * image[j] for j in image
        }

    p_own = [[pick(p_table[j][m], p_table[2 + j][2 + m]) for m in range(2)] for j in range(2)]
    p_far = [[pick(p_table[2 + j][m], p_table[j][2 + m]) for m in range(2)] for j in range(2)]
    gain_at = [jnp.broadcast_to(gains[k], (depth_z, lanes)) for k in range(ITERS)]

    def correct(x):
        fix = []
        for field in range(2):
            total = None
            for k in range(ITERS):
                search = (
                    hist[2 * k][field, x + DEPTH, :, 0:lanes]
                    + hist[2 * k + 1][field, x + DEPTH, :, 0:lanes]
                )
                total = gain_at[k] * search if total is None else total + gain_at[k] * search
            fix.append(total)
        base = [ext_a[j, x + DEPTH, :, 0:lanes] for j in range(2)]

        def store():
            for j in range(2):
                corr_out[j, x] = p_far[j][0] * fix[0] + p_far[j][1] * fix[1]
                part[j, x] = base[j] + p_own[j][0] * fix[0] + p_own[j][1] * fix[1]

        return store

    final = []
    for at in range(4):
        planes(correct, at * chunk, (at + 1) * chunk, 4)
        piece = pl.ds(at * chunk, chunk)
        one = copy(corr_out.at[:, piece], corr_in.at[:, piece], {"section": 1 - half})
        one.start()
        final.append(one)
    for at in range(4):
        final[at].wait_recv()

        for x in range(at * chunk, (at + 1) * chunk):
            for j in range(2):
                out_ref[j, pl.ds(x, depth_z, stride=rows), :] = part[j, x] + corr_in[j, x]
    for one in final:
        one.wait_send()
    lax.fori_loop(1, members, gram_release, 0)


def solution(mesh):
    sx_count, sy_count = mesh.shape["sx"], mesh.shape["sy"]
    tableau, inverse, eigen_basis, basis_inverse, pairs = radau_tables()
    shift_table = table_product(basis_inverse, inverse)
    shift_table = [[v / step_size for v in row_values] for row_values in shift_table]
    tables = (basis_inverse, shift_table, eigen_basis, pairs)

    def body(previous, sections, diffusivity, reaction):
        depth_z, rows, lanes = previous.shape
        wide = rows + 2 * DEPTH
        f32 = jnp.float32
        vmem = pltpu.VMEM
        ext = (wide, depth_z, 2 * lanes)
        block = (2, rows, depth_z, lanes)
        flat = (depth_z * rows, lanes)
        members = sx_count * sy_count
        return pl.pallas_call(
            functools.partial(kernel, sx_count, sy_count, tables),
            out_shape=jax.ShapeDtypeStruct((2,) + flat, f32),
            in_specs=[pl.BlockSpec(memory_space=pltpu.HBM)] * 4,
            out_specs=pl.BlockSpec(memory_space=pltpu.VMEM),
            scratch_shapes=[
                vmem(flat, f32),
                vmem((2,) + flat, f32),
                vmem(flat, f32),
                vmem(flat, f32),
                vmem((4,) + ext, f32),
                vmem((2,) + ext, f32),
                vmem((4,) + ext, f32),
                vmem(ext, f32),
                vmem(ext, f32),
                vmem(ext, f32),
                *[vmem((2,) + ext, f32) for m in range(DEPTH)],
                *[vmem((2, wide, depth_z, lanes), f32) for m in range(ITERS - 1)],
                vmem((1,) + block, f32),
                vmem(block, f32),
                vmem(block, f32),
                vmem(block, f32),
                vmem(block, f32),
                vmem(block, f32),
                vmem((2, 4, depth_z, lanes), f32),
                vmem((2, 4, depth_z, lanes), f32),
                vmem((2, 2, depth_z, lanes), f32),
                vmem((2, 3, 2, depth_z, lanes), f32),
                vmem((2, 2, depth_z, lanes), f32),
                vmem((2, 3, 2, depth_z, lanes), f32),
                vmem((members, 1, lanes), f32),
                pltpu.SemaphoreType.DMA((4,)),
                pltpu.SemaphoreType.DMA((32,)),
                pltpu.SemaphoreType.DMA((32,)),
                pltpu.SemaphoreType.DMA((members,)),
                pltpu.SemaphoreType.DMA((members,)),
            ],
            compiler_params=pltpu.CompilerParams(
                collective_id=0, has_side_effects=True, vmem_limit_bytes=63 * 1024 * 1024
            ),
        )(
            previous.reshape(flat),
            sections.reshape((2,) + flat),
            diffusivity.reshape(flat),
            reaction.reshape(flat),
        ).reshape(sections.shape)

    in_specs = (
        P(None, "sx", "sy"),
        P("section", None, "sx", "sy"),
        P(None, "sx", "sy"),
        P(None, "sx", "sy"),
    )
    out_specs = P("section", None, "sx", "sy")
    return jax.shard_map(body, mesh=mesh, in_specs=in_specs, out_specs=out_specs, check_vma=False)
```

```python
import functools

import jax
import jax.numpy as jnp
from jax import lax
from jax.experimental import pallas as pl
from jax.experimental.pallas import tpu as pltpu
from jax.sharding import PartitionSpec as P

ITERS = 4
DEPTH = 2 * ITERS
MESH = pl.DeviceIdType.MESH

step_size = 1.0
tiny_value = 1e-06


def invert_table(matrix):
    order_n = len(matrix)
    augmented = [
        list(matrix[r]) + [1.0 if c == r else 0.0 for c in range(order_n)] for r in range(order_n)
    ]
    for col in range(order_n):
        pivot_row = max(range(col, order_n), key=lambda r: abs(augmented[r][col]))
        augmented[col], augmented[pivot_row] = (augmented[pivot_row], augmented[col])
        leading = augmented[col][col]
        augmented[col] = [v / leading for v in augmented[col]]
        for r in range(order_n):
            if r != col:
                factor = augmented[r][col]
                augmented[r] = [a - factor * b for a, b in zip(augmented[r], augmented[col])]
    return [row_values[order_n:] for row_values in augmented]


def table_product(left, right):
    return [
        [sum((left[i][k] * right[k][j] for k in range(len(right)))) for j in range(len(right[0]))]
        for i in range(len(left))
    ]


def pair_add(first, second):
    return (first[0] + second[0], first[1] + second[1])


def pair_sub(first, second):
    return (first[0] - second[0], first[1] - second[1])


def pair_mul(first, second):
    return (
        first[0] * second[0] - first[1] * second[1],
        first[0] * second[1] + first[1] * second[0],
    )


def pair_div(first, second):
    scale_sq = second[0] * second[0] + second[1] * second[1]
    return (
        (first[0] * second[0] + first[1] * second[1]) / scale_sq,
        (first[1] * second[0] - first[0] * second[1]) / scale_sq,
    )


def quartic_value(point):
    return (((210.0 * point - 480.0) * point + 360.0) * point - 96.0) * point + 6.0


def bisect_root(lower, upper):
    for count in range(200):
        middle = 0.5 * (lower + upper)
        if (quartic_value(lower) < 0.0) == (quartic_value(middle) < 0.0):
            lower = middle
        else:
            upper = middle
    return 0.5 * (lower + upper)


def radau_tables():
    abscissae = []
    grid_steps = 4000
    for m in range(grid_steps):
        lower = 0.999 * m / grid_steps
        upper = 0.999 * (m + 1) / grid_steps
        if (quartic_value(lower) < 0.0) != (quartic_value(upper) < 0.0):
            abscissae.append(bisect_root(lower, upper))
    abscissae.append(1.0)
    vander = [[abscissae[j] ** k for k in range(4)] for j in range(4)]
    moments = [[abscissae[i] ** (k + 1) / (k + 1) for k in range(4)] for i in range(4)]
    tableau = table_product(moments, invert_table(vander))
    inverse = invert_table(tableau)
    running = [list(row_values) for row_values in inverse]
    coeffs = []
    for k in range(1, 5):
        trace_value = sum((running[i][i] for i in range(4)))
        coeffs.append(-trace_value / k)
        shifted_table = [
            [running[i][j] + (coeffs[-1] if i == j else 0.0) for j in range(4)] for i in range(4)
        ]
        running = table_product(inverse, shifted_table)
    start_point = (0.4, 0.9)
    estimates = [(1.0, 0.0)]
    for k in range(3):
        estimates.append(pair_mul(estimates[-1], start_point))
    for count in range(500):
        for i in range(4):
            value = (1.0, 0.0)
            for coef_value in coeffs:
                value = pair_add(pair_mul(value, estimates[i]), (coef_value, 0.0))
            denom = (1.0, 0.0)
            for j in range(4):
                if j != i:
                    denom = pair_mul(denom, pair_sub(estimates[i], estimates[j]))
            estimates[i] = pair_sub(estimates[i], pair_div(value, denom))
    chosen = [m for m in range(4) if estimates[m][1] > 0.0]
    ranking = sorted(chosen, key=lambda m: -estimates[m][1])
    columns = []
    pairs = []
    for m in ranking:
        eigen_pair = estimates[m]
        system = [
            [
                (
                    inverse[i][j] - (eigen_pair[0] if i == j else 0.0),
                    -(eigen_pair[1] if i == j else 0.0),
                )
                for j in range(4)
            ]
            for i in range(3)
        ]
        rows_left = [
            [system[i][j] for j in range(3)] + [(-system[i][3][0], -system[i][3][1])]
            for i in range(3)
        ]
        for col in range(3):
            pivot_row = max(
                range(col, 3), key=lambda r: rows_left[r][col][0] ** 2 + rows_left[r][col][1] ** 2
            )
            rows_left[col], rows_left[pivot_row] = (rows_left[pivot_row], rows_left[col])
            leading = rows_left[col][col]
            rows_left[col] = [pair_div(v, leading) for v in rows_left[col]]
            for r in range(3):
                if r != col:
                    factor = rows_left[r][col]
                    rows_left[r] = [
                        pair_sub(a, pair_mul(factor, b))
                        for a, b in zip(rows_left[r], rows_left[col])
                    ]
        vector = [rows_left[i][3] for i in range(3)] + [(1.0, 0.0)]
        columns.append([v[0] for v in vector])
        columns.append([v[1] for v in vector])
        pairs.append((eigen_pair[0], eigen_pair[1]))
    eigen_basis = [[columns[j][i] for j in range(4)] for i in range(4)]
    basis_inverse = invert_table(eigen_basis)
    return (tableau, inverse, eigen_basis, basis_inverse, pairs)


def near(plane, member):
    if member == 0:
        return pltpu.roll(plane, plane.shape[0] - 1, 0)
    if member == 1:
        return pltpu.roll(plane, 1, 0)
    if member == 2:
        return pltpu.roll(plane, plane.shape[1] - 1, 1)
    return pltpu.roll(plane, 1, 1)


def kernel(
    sx_count, sy_count, tables,
    prev_any, sec_any, diff_any, react_any, out_ref,
    prev_ref, sec_ref, diff_ref, react_ref,
    ext_a, ext_b, faces, face_x, alpha, beta, *rest,
):
    hist, rest = rest[:DEPTH], rest[DEPTH:]
    powers, rest = rest[: ITERS - 1], rest[ITERS - 1 :]
    (
    basis, part, part_out, part_in, corr_out, corr_in,
    pack_a, got_a, pack_b, got_b, pack_c, got_c, gram, load_sem,
    send_sem, recv_sem, gram_send, gram_recv,
    ) = rest
    depth_z, lanes = ext_a.shape[2], prev_ref.shape[1]
    rows = prev_ref.shape[0] // depth_z
    top = DEPTH + rows
    group = rows
    sx, sy, half = lax.axis_index("sx"), lax.axis_index("sy"), lax.axis_index("section")
    q_table, c_table, p_table, pairs = tables

    def pick(first, second):
        return jnp.where(half == 0, jnp.float32(first), jnp.float32(second))

    barrier = pltpu.get_barrier_semaphore()
    members = sx_count * sy_count
    me = sx * sy_count + sy

    def member_at(offset):
        other = lax.rem(me + offset, members)
        return {"sx": other // sy_count, "sy": lax.rem(other, sy_count)}

    def greet(offset, carry):
        pl.semaphore_signal(barrier, inc=1, device_id=member_at(offset), device_id_type=MESH)
        return carry

    lax.fori_loop(1, members, greet, 0)
    pl.semaphore_signal(barrier, inc=1, device_id={"section": 1 - half}, device_id_type=MESH)

    loads = [
        pltpu.make_async_copy(source, target, load_sem.at[at])
        for at, (source, target) in enumerate((
            (sec_any, sec_ref), (diff_any, diff_ref), (prev_any, prev_ref), (react_any, react_ref),
        ))
    ]
    for one in loads:
        one.start()

    wide = rows + 2 * DEPTH
    left, right = lax.rem(sx + sx_count - 1, sx_count), lax.rem(sx + 1, sx_count)
    below, above = lax.rem(sy + sy_count - 1, sy_count), lax.rem(sy + 1, sy_count)
    has_left, has_right = sx > 0, sx < sx_count - 1
    has_below, has_above = sy > 0, sy < sy_count - 1

    def clear(missing, *views):
        def run():
            for view in views:
                view[...] = jnp.zeros(view.shape, jnp.float32)

        pl.when(jnp.logical_not(missing))(run)

    clear(has_left, ext_a.at[:, DEPTH - 1, :, 0:lanes], ext_b.at[:, 0:DEPTH, :, 0:lanes],
          hist[0].at[:, 0:DEPTH, :, 0:lanes])
    clear(has_right, ext_a.at[:, top, :, 0:lanes], ext_b.at[:, top:wide, :, 0:lanes],
          hist[0].at[:, top:wide, :, 0:lanes])
    for side, there in ((0, has_above), (1, has_below)):
        clear(there, got_a.at[side], got_b.at[side, 1], got_c.at[side, 1])
        clear(there & has_left, got_b.at[side, 0], got_c.at[side, 0])
        clear(there & has_right, got_b.at[side, 2], got_c.at[side, 2])

    lane_group = lax.broadcasted_iota(jnp.int32, (depth_z, lanes), 1) // DEPTH

    def pack(plane_of, low, high):
        down = jnp.zeros((depth_z, lanes), jnp.float32)
        up = jnp.zeros((depth_z, lanes), jnp.float32)
        for x in range(rows):
            plane = plane_of(x)
            if x > 0:
                plane = pltpu.roll(plane, DEPTH * x, 1)
            down = jnp.where(lane_group == x, plane, down)
            up = jnp.where(lane_group == (x + group - 1) % group, plane, up)
        low[...] = down
        high[...] = up

    def unpack(from_high, from_low, members_x, store):
        for x in members_x:
            mixed = jnp.where(
                lane_group == x,
                from_high,
                jnp.where(lane_group == (x + group - 1) % group, from_low, 0.0),
            )
            if x > 0:
                mixed = pltpu.roll(mixed, lanes - DEPTH * x, 1)
            store(x, mixed)

    def unpack_wide(got, j, target):
        for place, members_x in ((0, range(rows - DEPTH, rows)), (1, range(rows)), (2, range(DEPTH))):
            first = (DEPTH - rows, DEPTH, top)[place]

            def store(x, plane):
                target[j, first + x, :, lanes : 2 * lanes] = plane

            unpack(got[0, place, j], got[1, place, j], members_x, store)

    def column(ref, x):
        return ref[pl.ds(x, depth_z, stride=rows), :]

    def planes(fn, least, most, batch):
        def several(first, count):
            stores = [fn(first + step) for step in range(count)]
            for store in stores:
                store()

        full, left_over = (most - least) // batch, (most - least) % batch
        if full == 1:
            several(least, batch)
        else:
            def turn(at, carry):
                several(least + at * batch, batch)
                return carry

            lax.fori_loop(0, full, turn, 0)
        if left_over:
            several(most - left_over, left_over)

    def section_coefs(x):
        diffusivity = column(diff_ref, x)
        cells = [column(sec_ref.at[j], x) for j in range(2)]
        coefs = [diffusivity * (1.0 + 0.5 * jnp.tanh(cells[j])) for j in range(2)]

        def store():
            for j in range(2):
                ext_a[j, x + DEPTH, :, 0:lanes] = cells[j]
                ext_a[2 + j, x + DEPTH, :, 0:lanes] = coefs[j]

        return store

    def frozen_coefs(x):
        before = column(prev_ref, x)
        coef = column(diff_ref, x) * (1.0 + 0.5 * jnp.tanh(before))
        slope = column(react_ref, x) * (1.0 - 3.0 * before * before)

        def store():
            ext_b[0, x + DEPTH, :, 0:lanes] = coef
            ext_b[1, x + DEPTH, :, 0:lanes] = slope

        return store

    for one in loads[:2]:
        one.wait()
    planes(section_coefs, 0, rows, 4)
    for j in range(4):
        pack(lambda x: ext_a[j, x + DEPTH, :, 0:lanes], pack_a.at[0, j], pack_a.at[1, j])

    pl.semaphore_wait(barrier, members)

    used = [0]

    def copy(source, target, device):
        at = used[0]
        used[0] += 1
        return pltpu.make_async_remote_copy(
            src_ref=source,
            dst_ref=target,
            send_sem=send_sem.at[at],
            recv_sem=recv_sem.at[at],
            device_id=device,
            device_id_type=MESH,
        )

    own = pl.ds(0, lanes)
    low_rows, high_rows = pl.ds(0, DEPTH), pl.ds(top, DEPTH)

    def slabs(low_source, high_source, target):
        return [
            (has_left, has_right, copy(low_source, target(high_rows), {"sx": left})),
            (has_right, has_left, copy(high_source, target(low_rows), {"sx": right})),
        ]

    def strips(packed, got, corners):
        result = []
        for side, device, out_ok, in_ok in (
            (0, below, has_below, has_above),
            (1, above, has_above, has_below),
        ):
            middle = got.at[side, 1] if corners else got.at[side]
            result.append((out_ok, in_ok, copy(packed.at[side], middle, {"sy": device})))
            if corners:
                result.append((
                    out_ok & has_left,
                    in_ok & has_right,
                    copy(
                        packed.at[side],
                        got.at[side, 2],
                        {"sx": left, "sy": device},
                    ),
                ))
                result.append((
                    out_ok & has_right,
                    in_ok & has_left,
                    copy(
                        packed.at[side],
                        got.at[side, 0],
                        {"sx": right, "sy": device},
                    ),
                ))
        return result

    def start(copies):
        for out_ok, in_ok, one in copies:
            pl.when(out_ok)(one.start)

    def receive(copies):
        for out_ok, in_ok, one in copies:
            pl.when(in_ok)(one.wait_recv)

    def release(copies):
        for out_ok, in_ok, one in copies:
            pl.when(out_ok)(one.wait_send)

    copies_a = strips(pack_a, got_a, False)
    edge = pl.ds(top, 1), pl.ds(DEPTH - 1, 1)
    copies_a.append((
        has_left,
        has_right,
        copy(
            ext_a.at[:, pl.ds(DEPTH, 1), :, own],
            ext_a.at[:, edge[0], :, own],
            {"sx": left},
        ),
    ))
    copies_a.append((
        has_right,
        has_left,
        copy(
            ext_a.at[:, pl.ds(top - 1, 1), :, own],
            ext_a.at[:, edge[1], :, own],
            {"sx": right},
        ),
    ))
    start(copies_a)
    for one in loads[2:]:
        one.wait()
    planes(frozen_coefs, 0, rows, 4)
    for j in range(2):
        pack(lambda x: ext_b[j, x + DEPTH, :, 0:lanes], pack_b.at[0, j], pack_b.at[1, j])
    copies_b = strips(pack_b, got_b, True)
    copies_b += slabs(
        ext_b.at[:, pl.ds(DEPTH, DEPTH), :, own],
        ext_b.at[:, pl.ds(top - DEPTH, DEPTH), :, own],
        lambda where: ext_b.at[:, where, :, own],
    )
    start(copies_b)

    receive(copies_a)

    for j in range(4):
        def put_a(x, plane):
            ext_a[j, x + DEPTH, :, lanes : 2 * lanes] = plane

        unpack(got_a[0, j], got_a[1, j], range(rows), put_a)

    q_own = [[pick(q_table[m][j], q_table[2 + m][2 + j]) for j in range(2)] for m in range(2)]
    q_far = [[pick(q_table[2 + m][j], q_table[m][2 + j]) for j in range(2)] for m in range(2)]
    c_own = [[pick(c_table[m][j], c_table[2 + m][2 + j]) for j in range(2)] for m in range(2)]
    c_far = [[pick(c_table[2 + m][j], c_table[m][2 + j]) for j in range(2)] for m in range(2)]

    def middle(plane):
        return plane[:, 0:lanes]

    z_at = lax.broadcasted_iota(jnp.int32, (depth_z, 2 * lanes), 0)
    has_next = (z_at < depth_z - 1, z_at > 0)

    def around_z(plane, member):
        mask = has_next[member][:, 0 : plane.shape[1]]
        return jnp.where(mask, near(plane, member), 0.0)

    def fluxes(x):
        flux, increment = [], []
        for j in range(2):
            cells, coefs = ext_a[j, x + DEPTH], ext_a[2 + j, x + DEPTH]
            here, coef_here = middle(cells), middle(coefs)
            total = jnp.zeros_like(here)
            for member in range(2):
                face = 0.5 * (coef_here + around_z(coef_here, member))
                total = total + face * (around_z(here, member) - here)
            for member in (2, 3):
                face = 0.5 * (coef_here + middle(near(coefs, member)))
                total = total + face * (middle(near(cells, member)) - here)
            for place in (x + DEPTH - 1, x + DEPTH + 1):
                face = 0.5 * (coef_here + ext_a[2 + j, place, :, 0:lanes])
                total = total + face * (ext_a[j, place, :, 0:lanes] - here)
            flux.append(total + column(react_ref, x) * here * (1.0 - here * here))
            increment.append(here - column(prev_ref, x))
        near_part = [
            q_own[m][0] * flux[0] + q_own[m][1] * flux[1]
            - c_own[m][0] * increment[0] - c_own[m][1] * increment[1]
            for m in range(2)
        ]
        far_part = [
            q_far[m][0] * flux[0] + q_far[m][1] * flux[1]
            - c_far[m][0] * increment[0] - c_far[m][1] * increment[1]
            for m in range(2)
        ]

        def store():
            for m in range(2):
                part[m, x] = near_part[m]
                part_out[m, x] = far_part[m]

        return store

    chunk = rows // 4
    swap = []
    for at in range(4):
        planes(fluxes, at * chunk, (at + 1) * chunk, chunk)
        piece = pl.ds(at * chunk, chunk)
        one = copy(part_out.at[:, piece], part_in.at[:, piece], {"section": 1 - half})
        one.start()
        swap.append(one)

    receive(copies_b)

    for j in range(2):
        unpack_wide(got_b, j, ext_b)

    real_part = pick(pairs[0][0] / step_size, pairs[1][0] / step_size)
    coupling = pick(pairs[0][1] / step_size, pairs[1][1] / step_size)
    lane_at = lax.broadcasted_iota(jnp.int32, (depth_z, 2 * lanes), 1)
    inside = (
        (lane_at < lanes)
        | ((lane_at < lanes + DEPTH) & has_above)
        | ((lane_at >= 2 * lanes - DEPTH) & has_below)
    )
    keep = inside.astype(jnp.float32)

    def x_faces(x):
        face = 0.5 * (ext_b[0, x] + ext_b[0, x + 1])

        def store():
            face_x[x] = face

        return store

    planes(x_faces, 0, wide - 1, 4)

    def operator(x):
        coefs = ext_b[0, x]
        diag = real_part - ext_b[1, x] + face_x[x - 1] + face_x[x]
        sides = []
        for member in range(2):
            face = 0.5 * (coefs + around_z(coefs, member))
            diag = diag + face
            sides.append(jnp.where(has_next[member], face, 0.0))
        for member in (2, 3):
            face = 0.5 * (coefs + near(coefs, member))
            diag = diag + face
            sides.append(face)
        inside_x = ((x >= DEPTH) | has_left) & ((x < top) | has_right)
        scale = keep / (diag * diag + coupling * coupling)
        scale = jnp.where(inside_x, scale, 0.0)

        def store():
            for member in range(4):
                faces[member, x] = sides[member]
            alpha[x] = diag * scale
            beta[x] = coupling * scale

        return store

    planes(operator, 1, wide - 1, 2)

    def first_scaled(x):
        rhs = [part[m, x] + part_in[m, x] for m in range(2)]
        a, b = middle(alpha[x + DEPTH]), middle(beta[x + DEPTH])

        def store():
            for m in range(2):
                basis[0, m, x] = rhs[m]
            hist[0][0, x + DEPTH, :, 0:lanes] = a * rhs[0] - b * rhs[1]
            hist[0][1, x + DEPTH, :, 0:lanes] = b * rhs[0] + a * rhs[1]

        return store

    copies_c = []
    for at in range(4):
        swap[at].wait_recv()
        planes(first_scaled, at * chunk, (at + 1) * chunk, chunk)
        low = (at + 1) * chunk <= DEPTH
        one = copy(
            hist[0].at[:, pl.ds(DEPTH + at * chunk, chunk), :, own],
            hist[0].at[:, pl.ds(at * chunk + (top if low else DEPTH - rows), chunk), :, own],
            {"sx": left if low else right},
        )
        copies_c.append((has_left, has_right, one) if low else (has_right, has_left, one))
        start(copies_c[-1:])
    for j in range(2):
        pack(lambda x: hist[0][j, x + DEPTH, :, 0:lanes], pack_c.at[0, j], pack_c.at[1, j])
    more_c = strips(pack_c, got_c, True)
    start(more_c)
    copies_c = copies_c + more_c
    receive(copies_c)
    for j in range(2):
        unpack_wide(got_c, j, hist[0])

    for m in range(DEPTH - 1):
        def apply(x):
            around = []
            for field in range(2):
                cells = hist[m][field, x]
                total = face_x[x - 1] * hist[m][field, x - 1] + face_x[x] * hist[m][field, x + 1]
                for member in range(4):
                    total = total + faces[member, x] * near(cells, member)
                around.append(total)
            a, b = alpha[x], beta[x]
            scaled = [a * around[0] - b * around[1], b * around[0] + a * around[1]]

            def store():
                for field in range(2):
                    if m % 2 == 1:
                        powers[(m - 1) // 2][field, x] = middle(around[field])
                    hist[m + 1][field, x] = scaled[field]

            return store

        planes(apply, m + 1, wide - 1 - m, 4)

    index = [(i, j) for i in range(ITERS + 1) for j in range(i, ITERS + 1)]

    def last_apply(at, carry):
        totals = list(carry)
        ends = {}
        for step in range(4):
            at_x = 4 * at + step + DEPTH
            for field in range(2):
                cells = hist[DEPTH - 1][field, at_x]
                total = middle(face_x[at_x - 1]) * hist[DEPTH - 1][field, at_x - 1, :, 0:lanes]
                total = total + middle(face_x[at_x]) * hist[DEPTH - 1][field, at_x + 1, :, 0:lanes]
                for member in range(2):
                    total = total + middle(faces[member, at_x]) * near(middle(cells), member)
                for member in (2, 3):
                    total = total + middle(faces[member, at_x]) * middle(near(cells, member))
                ends[step, field] = total
        for step in range(4):
            for field in range(2):
                members_of = [basis[0, field, 4 * at + step]]
                members_of += [powers[k][field, 4 * at + step + DEPTH] for k in range(ITERS - 1)]
                members_of += [ends[step, field]]
                for pair, (i, j) in enumerate(index):
                    product = members_of[i] * members_of[j]
                    for r in range(0, depth_z, 8):
                        totals[pair] = totals[pair] + product[r : r + 8]
        return tuple(totals)

    zeros = tuple(jnp.zeros((8, lanes), jnp.float32) for pair in index)
    sums = lax.fori_loop(0, rows // 4, last_apply, zeros)
    square = jnp.concatenate(
        [jnp.sum(total, axis=0, keepdims=True) for total in sums]
        + [jnp.zeros((16 - len(index), lanes), jnp.float32)],
        axis=0,
    )
    diagonal = lax.broadcasted_iota(jnp.int32, (16, lanes), 0) == lax.broadcasted_iota(
        jnp.int32, (16, lanes), 1
    )
    square = jnp.where(diagonal, jnp.sum(square, axis=1, keepdims=True), 0.0)
    gram[0] = jnp.sum(square, axis=0, keepdims=True)

    def gram_copy(offset):
        return pltpu.make_async_remote_copy(
            src_ref=gram.at[0],
            dst_ref=gram.at[offset],
            send_sem=gram_send.at[offset],
            recv_sem=gram_recv.at[offset],
            device_id=member_at(offset),
            device_id_type=MESH,
        )

    def gram_start(offset, carry):
        gram_copy(offset).start()
        return carry

    def gram_take(offset, carry):
        gram_copy(offset).wait_recv()
        return carry

    def gram_release(offset, carry):
        gram_copy(offset).wait_send()
        return carry

    lax.fori_loop(1, members, gram_start, 0)
    release(copies_a)
    release(copies_b)
    release(copies_c)
    for one in swap:
        one.wait_send()
    lax.fori_loop(1, members, gram_take, 0)
    turn = [lax.rem(me - place + members, members) for place in range(members)]
    table = gram[turn[0]]
    for place in range(1, members):
        table = table + gram[turn[place]]
    table = jnp.where(diagonal, jnp.broadcast_to(table, (16, lanes)), 0.0)
    table = jnp.sum(table, axis=1, keepdims=True)
    entry = {}
    for at, (i, j) in enumerate(index):
        entry[i, j] = entry[j, i] = table[at : at + 1, :]

    weights = {0: jnp.ones((1, 1), jnp.float32)}
    gains = {}
    for sweep in range(ITERS):
        image = {}
        for j in range(sweep + 2):
            if j in weights and j - 1 in weights:
                image[j] = weights[j] - weights[j - 1]
            elif j in weights:
                image[j] = weights[j]
            else:
                image[j] = -weights[j - 1]
        against = {
            j: functools.reduce(jnp.add, [image[i] * entry[i, j] for i in image]) for j in image
        }
        numerator = functools.reduce(jnp.add, [against[j] * weights[j] for j in weights])
        denominator = functools.reduce(jnp.add, [against[j] * image[j] for j in image])
        step = numerator / (denominator + tiny_value)
        for j in weights:
            gains[j] = gains[j] + step * weights[j] if j in gains else step * weights[j]
        weights = {
            j: (weights[j] - step * image[j]) if j in weights else -step * image[j] for j in image
        }

    p_own = [[pick(p_table[j][m], p_table[2 + j][2 + m]) for m in range(2)] for j in range(2)]
    p_far = [[pick(p_table[2 + j][m], p_table[j][2 + m]) for m in range(2)] for j in range(2)]
    gain_at = [jnp.broadcast_to(gains[k], (depth_z, lanes)) for k in range(ITERS)]

    def correct(x):
        fix = []
        for field in range(2):
            total = None
            for k in range(ITERS):
                search = (
                    hist[2 * k][field, x + DEPTH, :, 0:lanes]
                    + hist[2 * k + 1][field, x + DEPTH, :, 0:lanes]
                )
                total = gain_at[k] * search if total is None else total + gain_at[k] * search
            fix.append(total)
        base = [ext_a[j, x + DEPTH, :, 0:lanes] for j in range(2)]

        def store():
            for j in range(2):
                corr_out[j, x] = p_far[j][0] * fix[0] + p_far[j][1] * fix[1]
                part[j, x] = base[j] + p_own[j][0] * fix[0] + p_own[j][1] * fix[1]

        return store

    final = []
    for at in range(4):
        planes(correct, at * chunk, (at + 1) * chunk, 4)
        piece = pl.ds(at * chunk, chunk)
        one = copy(corr_out.at[:, piece], corr_in.at[:, piece], {"section": 1 - half})
        one.start()
        final.append(one)
    for at in range(4):
        final[at].wait_recv()

        for x in range(at * chunk, (at + 1) * chunk):
            for j in range(2):
                out_ref[j, pl.ds(x, depth_z, stride=rows), :] = part[j, x] + corr_in[j, x]
    for one in final:
        one.wait_send()
    lax.fori_loop(1, members, gram_release, 0)


def solution(mesh):
    sx_count, sy_count = mesh.shape["sx"], mesh.shape["sy"]
    tableau, inverse, eigen_basis, basis_inverse, pairs = radau_tables()
    shift_table = table_product(basis_inverse, inverse)
    shift_table = [[v / step_size for v in row_values] for row_values in shift_table]
    tables = (basis_inverse, shift_table, eigen_basis, pairs)

    def body(previous, sections, diffusivity, reaction):
        depth_z, rows, lanes = previous.shape
        wide = rows + 2 * DEPTH
        f32 = jnp.float32
        vmem = pltpu.VMEM
        ext = (wide, depth_z, 2 * lanes)
        block = (2, rows, depth_z, lanes)
        flat = (depth_z * rows, lanes)
        members = sx_count * sy_count
        return pl.pallas_call(
            functools.partial(kernel, sx_count, sy_count, tables),
            out_shape=jax.ShapeDtypeStruct((2,) + flat, f32),
            in_specs=[pl.BlockSpec(memory_space=pltpu.HBM)] * 4,
            out_specs=pl.BlockSpec(memory_space=pltpu.VMEM),
            scratch_shapes=[
                vmem(flat, f32),
                vmem((2,) + flat, f32),
                vmem(flat, f32),
                vmem(flat, f32),
                vmem((4,) + ext, f32),
                vmem((2,) + ext, f32),
                vmem((4,) + ext, f32),
                vmem(ext, f32),
                vmem(ext, f32),
                vmem(ext, f32),
                *[vmem((2,) + ext, f32) for m in range(DEPTH)],
                *[vmem((2, wide, depth_z, lanes), f32) for m in range(ITERS - 1)],
                vmem((1,) + block, f32),
                vmem(block, f32),
                vmem(block, f32),
                vmem(block, f32),
                vmem(block, f32),
                vmem(block, f32),
                vmem((2, 4, depth_z, lanes), f32),
                vmem((2, 4, depth_z, lanes), f32),
                vmem((2, 2, depth_z, lanes), f32),
                vmem((2, 3, 2, depth_z, lanes), f32),
                vmem((2, 2, depth_z, lanes), f32),
                vmem((2, 3, 2, depth_z, lanes), f32),
                vmem((members, 1, lanes), f32),
                pltpu.SemaphoreType.DMA((4,)),
                pltpu.SemaphoreType.DMA((40,)),
                pltpu.SemaphoreType.DMA((40,)),
                pltpu.SemaphoreType.DMA((members,)),
                pltpu.SemaphoreType.DMA((members,)),
            ],
            compiler_params=pltpu.CompilerParams(
                collective_id=0, has_side_effects=True, vmem_limit_bytes=63 * 1024 * 1024
            ),
        )(
            previous.reshape(flat),
            sections.reshape((2,) + flat),
            diffusivity.reshape(flat),
            reaction.reshape(flat),
        ).reshape(sections.shape)

    in_specs = (
        P(None, "sx", "sy"),
        P("section", None, "sx", "sy"),
        P(None, "sx", "sy"),
        P(None, "sx", "sy"),
    )
    out_specs = P("section", None, "sx", "sy")
    return jax.shard_map(body, mesh=mesh, in_specs=in_specs, out_specs=out_specs, check_vma=False)
```

```python
import functools

import jax
import jax.numpy as jnp
from jax import lax
from jax.experimental import pallas as pl
from jax.experimental.pallas import tpu as pltpu
from jax.sharding import PartitionSpec as P

ITERS = 4
DEPTH = 2 * ITERS
MESH = pl.DeviceIdType.MESH

step_size = 1.0
tiny_value = 1e-06


def invert_table(matrix):
    order_n = len(matrix)
    augmented = [
        list(matrix[r]) + [1.0 if c == r else 0.0 for c in range(order_n)] for r in range(order_n)
    ]
    for col in range(order_n):
        pivot_row = max(range(col, order_n), key=lambda r: abs(augmented[r][col]))
        augmented[col], augmented[pivot_row] = (augmented[pivot_row], augmented[col])
        leading = augmented[col][col]
        augmented[col] = [v / leading for v in augmented[col]]
        for r in range(order_n):
            if r != col:
                factor = augmented[r][col]
                augmented[r] = [a - factor * b for a, b in zip(augmented[r], augmented[col])]
    return [row_values[order_n:] for row_values in augmented]


def table_product(left, right):
    return [
        [sum((left[i][k] * right[k][j] for k in range(len(right)))) for j in range(len(right[0]))]
        for i in range(len(left))
    ]


def pair_add(first, second):
    return (first[0] + second[0], first[1] + second[1])


def pair_sub(first, second):
    return (first[0] - second[0], first[1] - second[1])


def pair_mul(first, second):
    return (
        first[0] * second[0] - first[1] * second[1],
        first[0] * second[1] + first[1] * second[0],
    )


def pair_div(first, second):
    scale_sq = second[0] * second[0] + second[1] * second[1]
    return (
        (first[0] * second[0] + first[1] * second[1]) / scale_sq,
        (first[1] * second[0] - first[0] * second[1]) / scale_sq,
    )


def quartic_value(point):
    return (((210.0 * point - 480.0) * point + 360.0) * point - 96.0) * point + 6.0


def bisect_root(lower, upper):
    for count in range(200):
        middle = 0.5 * (lower + upper)
        if (quartic_value(lower) < 0.0) == (quartic_value(middle) < 0.0):
            lower = middle
        else:
            upper = middle
    return 0.5 * (lower + upper)


def radau_tables():
    abscissae = []
    grid_steps = 4000
    for m in range(grid_steps):
        lower = 0.999 * m / grid_steps
        upper = 0.999 * (m + 1) / grid_steps
        if (quartic_value(lower) < 0.0) != (quartic_value(upper) < 0.0):
            abscissae.append(bisect_root(lower, upper))
    abscissae.append(1.0)
    vander = [[abscissae[j] ** k for k in range(4)] for j in range(4)]
    moments = [[abscissae[i] ** (k + 1) / (k + 1) for k in range(4)] for i in range(4)]
    tableau = table_product(moments, invert_table(vander))
    inverse = invert_table(tableau)
    running = [list(row_values) for row_values in inverse]
    coeffs = []
    for k in range(1, 5):
        trace_value = sum((running[i][i] for i in range(4)))
        coeffs.append(-trace_value / k)
        shifted_table = [
            [running[i][j] + (coeffs[-1] if i == j else 0.0) for j in range(4)] for i in range(4)
        ]
        running = table_product(inverse, shifted_table)
    start_point = (0.4, 0.9)
    estimates = [(1.0, 0.0)]
    for k in range(3):
        estimates.append(pair_mul(estimates[-1], start_point))
    for count in range(500):
        for i in range(4):
            value = (1.0, 0.0)
            for coef_value in coeffs:
                value = pair_add(pair_mul(value, estimates[i]), (coef_value, 0.0))
            denom = (1.0, 0.0)
            for j in range(4):
                if j != i:
                    denom = pair_mul(denom, pair_sub(estimates[i], estimates[j]))
            estimates[i] = pair_sub(estimates[i], pair_div(value, denom))
    chosen = [m for m in range(4) if estimates[m][1] > 0.0]
    ranking = sorted(chosen, key=lambda m: -estimates[m][1])
    columns = []
    pairs = []
    for m in ranking:
        eigen_pair = estimates[m]
        system = [
            [
                (
                    inverse[i][j] - (eigen_pair[0] if i == j else 0.0),
                    -(eigen_pair[1] if i == j else 0.0),
                )
                for j in range(4)
            ]
            for i in range(3)
        ]
        rows_left = [
            [system[i][j] for j in range(3)] + [(-system[i][3][0], -system[i][3][1])]
            for i in range(3)
        ]
        for col in range(3):
            pivot_row = max(
                range(col, 3), key=lambda r: rows_left[r][col][0] ** 2 + rows_left[r][col][1] ** 2
            )
            rows_left[col], rows_left[pivot_row] = (rows_left[pivot_row], rows_left[col])
            leading = rows_left[col][col]
            rows_left[col] = [pair_div(v, leading) for v in rows_left[col]]
            for r in range(3):
                if r != col:
                    factor = rows_left[r][col]
                    rows_left[r] = [
                        pair_sub(a, pair_mul(factor, b))
                        for a, b in zip(rows_left[r], rows_left[col])
                    ]
        vector = [rows_left[i][3] for i in range(3)] + [(1.0, 0.0)]
        columns.append([v[0] for v in vector])
        columns.append([v[1] for v in vector])
        pairs.append((eigen_pair[0], eigen_pair[1]))
    eigen_basis = [[columns[j][i] for j in range(4)] for i in range(4)]
    basis_inverse = invert_table(eigen_basis)
    return (tableau, inverse, eigen_basis, basis_inverse, pairs)


def near(plane, member):
    if member == 0:
        return pltpu.roll(plane, plane.shape[0] - 1, 0)
    if member == 1:
        return pltpu.roll(plane, 1, 0)
    if member == 2:
        return pltpu.roll(plane, plane.shape[1] - 1, 1)
    return pltpu.roll(plane, 1, 1)


def kernel(
    sx_count, sy_count, tables,
    prev_any, sec_any, diff_any, react_any, out_ref,
    prev_ref, sec_ref, diff_ref, react_ref,
    ext_a, ext_b, faces, face_x, alpha, beta, *rest,
):
    hist, rest = rest[:DEPTH], rest[DEPTH:]
    powers, rest = rest[: ITERS - 1], rest[ITERS - 1 :]
    (
    basis, part, part_out, part_in, corr_out, corr_in,
    pack_a, got_a, pack_b, got_b, pack_c, got_c, gram, load_sem,
    send_sem, recv_sem, gram_send, gram_recv,
    ) = rest
    depth_z, lanes = ext_a.shape[2], prev_ref.shape[1]
    rows = prev_ref.shape[0] // depth_z
    top = DEPTH + rows
    group = rows
    sx, sy, half = lax.axis_index("sx"), lax.axis_index("sy"), lax.axis_index("section")
    q_table, c_table, p_table, pairs = tables

    def pick(first, second):
        return jnp.where(half == 0, jnp.float32(first), jnp.float32(second))

    barrier = pltpu.get_barrier_semaphore()
    members = sx_count * sy_count
    me = sx * sy_count + sy

    def member_at(offset):
        other = lax.rem(me + offset, members)
        return {"sx": other // sy_count, "sy": lax.rem(other, sy_count)}

    def greet(offset, carry):
        pl.semaphore_signal(barrier, inc=1, device_id=member_at(offset), device_id_type=MESH)
        return carry

    lax.fori_loop(1, members, greet, 0)
    pl.semaphore_signal(barrier, inc=1, device_id={"section": 1 - half}, device_id_type=MESH)

    loads = [
        pltpu.make_async_copy(source, target, load_sem.at[at])
        for at, (source, target) in enumerate((
            (sec_any, sec_ref), (diff_any, diff_ref), (prev_any, prev_ref), (react_any, react_ref),
        ))
    ]
    for one in loads:
        one.start()

    wide = rows + 2 * DEPTH
    left, right = lax.rem(sx + sx_count - 1, sx_count), lax.rem(sx + 1, sx_count)
    below, above = lax.rem(sy + sy_count - 1, sy_count), lax.rem(sy + 1, sy_count)
    has_left, has_right = sx > 0, sx < sx_count - 1
    has_below, has_above = sy > 0, sy < sy_count - 1

    def clear(missing, *views):
        def run():
            for view in views:
                view[...] = jnp.zeros(view.shape, jnp.float32)

        pl.when(jnp.logical_not(missing))(run)

    clear(has_left, ext_a.at[:, DEPTH - 1, :, 0:lanes], ext_b.at[:, 0:DEPTH, :, 0:lanes],
          hist[0].at[:, 0:DEPTH, :, 0:lanes])
    clear(has_right, ext_a.at[:, top, :, 0:lanes], ext_b.at[:, top:wide, :, 0:lanes],
          hist[0].at[:, top:wide, :, 0:lanes])
    for side, there in ((0, has_above), (1, has_below)):
        clear(there, got_a.at[side], got_b.at[side, 1], got_c.at[side, 1])
        clear(there & has_left, got_b.at[side, 0], got_c.at[side, 0])
        clear(there & has_right, got_b.at[side, 2], got_c.at[side, 2])

    lane_group = lax.broadcasted_iota(jnp.int32, (depth_z, lanes), 1) // DEPTH

    def pack(plane_of, low, high):
        down = jnp.zeros((depth_z, lanes), jnp.float32)
        up = jnp.zeros((depth_z, lanes), jnp.float32)
        for x in range(rows):
            plane = plane_of(x)
            if x > 0:
                plane = pltpu.roll(plane, DEPTH * x, 1)
            down = jnp.where(lane_group == x, plane, down)
            up = jnp.where(lane_group == (x + group - 1) % group, plane, up)
        low[...] = down
        high[...] = up

    def unpack(from_high, from_low, members_x, store):
        for x in members_x:
            mixed = jnp.where(
                lane_group == x,
                from_high,
                jnp.where(lane_group == (x + group - 1) % group, from_low, 0.0),
            )
            if x > 0:
                mixed = pltpu.roll(mixed, lanes - DEPTH * x, 1)
            store(x, mixed)

    def unpack_wide(got, j, target):
        for place, members_x in ((0, range(rows - DEPTH, rows)), (1, range(rows)), (2, range(DEPTH))):
            first = (DEPTH - rows, DEPTH, top)[place]

            def store(x, plane):
                target[j, first + x, :, lanes : 2 * lanes] = plane

            unpack(got[0, place, j], got[1, place, j], members_x, store)

    def column(ref, x):
        return ref[pl.ds(x, depth_z, stride=rows), :]

    def planes(fn, least, most, batch):
        def several(first, count):
            stores = [fn(first + step) for step in range(count)]
            for store in stores:
                store()

        full, left_over = (most - least) // batch, (most - least) % batch
        if full == 1:
            several(least, batch)
        else:
            def turn(at, carry):
                several(least + at * batch, batch)
                return carry

            lax.fori_loop(0, full, turn, 0)
        if left_over:
            several(most - left_over, left_over)

    def section_coefs(x):
        diffusivity = column(diff_ref, x)
        cells = [column(sec_ref.at[j], x) for j in range(2)]
        coefs = [diffusivity * (1.0 + 0.5 * jnp.tanh(cells[j])) for j in range(2)]

        def store():
            for j in range(2):
                ext_a[j, x + DEPTH, :, 0:lanes] = cells[j]
                ext_a[2 + j, x + DEPTH, :, 0:lanes] = coefs[j]

        return store

    def frozen_coefs(x):
        before = column(prev_ref, x)
        coef = column(diff_ref, x) * (1.0 + 0.5 * jnp.tanh(before))
        slope = column(react_ref, x) * (1.0 - 3.0 * before * before)

        def store():
            ext_b[0, x + DEPTH, :, 0:lanes] = coef
            ext_b[1, x + DEPTH, :, 0:lanes] = slope

        return store

    for one in loads[:2]:
        one.wait()
    planes(section_coefs, 0, rows, 4)
    for j in range(4):
        pack(lambda x: ext_a[j, x + DEPTH, :, 0:lanes], pack_a.at[0, j], pack_a.at[1, j])

    pl.semaphore_wait(barrier, members)

    used = [0]

    def copy(source, target, device):
        at = used[0]
        used[0] += 1
        return pltpu.make_async_remote_copy(
            src_ref=source,
            dst_ref=target,
            send_sem=send_sem.at[at],
            recv_sem=recv_sem.at[at],
            device_id=device,
            device_id_type=MESH,
        )

    own = pl.ds(0, lanes)
    low_rows, high_rows = pl.ds(0, DEPTH), pl.ds(top, DEPTH)

    def slabs(low_source, high_source, target):
        return [
            (has_left, has_right, copy(low_source, target(high_rows), {"sx": left})),
            (has_right, has_left, copy(high_source, target(low_rows), {"sx": right})),
        ]

    def strips(packed, got, corners):
        result = []
        for side, device, out_ok, in_ok in (
            (0, below, has_below, has_above),
            (1, above, has_above, has_below),
        ):
            middle = got.at[side, 1] if corners else got.at[side]
            result.append((out_ok, in_ok, copy(packed.at[side], middle, {"sy": device})))
            if corners:
                result.append((
                    out_ok & has_left,
                    in_ok & has_right,
                    copy(
                        packed.at[side],
                        got.at[side, 2],
                        {"sx": left, "sy": device},
                    ),
                ))
                result.append((
                    out_ok & has_right,
                    in_ok & has_left,
                    copy(
                        packed.at[side],
                        got.at[side, 0],
                        {"sx": right, "sy": device},
                    ),
                ))
        return result

    def start(copies):
        for out_ok, in_ok, one in copies:
            pl.when(out_ok)(one.start)

    def receive(copies):
        for out_ok, in_ok, one in copies:
            pl.when(in_ok)(one.wait_recv)

    def release(copies):
        for out_ok, in_ok, one in copies:
            pl.when(out_ok)(one.wait_send)

    copies_a = strips(pack_a, got_a, False)
    edge = pl.ds(top, 1), pl.ds(DEPTH - 1, 1)
    copies_a.append((
        has_left,
        has_right,
        copy(
            ext_a.at[:, pl.ds(DEPTH, 1), :, own],
            ext_a.at[:, edge[0], :, own],
            {"sx": left},
        ),
    ))
    copies_a.append((
        has_right,
        has_left,
        copy(
            ext_a.at[:, pl.ds(top - 1, 1), :, own],
            ext_a.at[:, edge[1], :, own],
            {"sx": right},
        ),
    ))
    start(copies_a)
    for one in loads[2:]:
        one.wait()
    planes(frozen_coefs, 0, rows, 4)
    for j in range(2):
        pack(lambda x: ext_b[j, x + DEPTH, :, 0:lanes], pack_b.at[0, j], pack_b.at[1, j])
    copies_b = strips(pack_b, got_b, True)
    copies_b += slabs(
        ext_b.at[:, pl.ds(DEPTH, DEPTH), :, own],
        ext_b.at[:, pl.ds(top - DEPTH, DEPTH), :, own],
        lambda where: ext_b.at[:, where, :, own],
    )
    start(copies_b)

    receive(copies_a)

    q_own = [[pick(q_table[m][j], q_table[2 + m][2 + j]) for j in range(2)] for m in range(2)]
    q_far = [[pick(q_table[2 + m][j], q_table[m][2 + j]) for j in range(2)] for m in range(2)]
    c_own = [[pick(c_table[m][j], c_table[2 + m][2 + j]) for j in range(2)] for m in range(2)]
    c_far = [[pick(c_table[2 + m][j], c_table[m][2 + j]) for j in range(2)] for m in range(2)]

    def middle(plane):
        return plane[:, 0:lanes]

    z_at = lax.broadcasted_iota(jnp.int32, (depth_z, 2 * lanes), 0)
    has_next = (z_at < depth_z - 1, z_at > 0)

    def around_z(plane, member):
        mask = has_next[member][:, 0 : plane.shape[1]]
        return jnp.where(mask, near(plane, member), 0.0)

    def fluxes(x):
        flux, increment = [], []
        for j in range(2):
            cells, coefs = ext_a[j, x + DEPTH], ext_a[2 + j, x + DEPTH]
            here, coef_here = middle(cells), middle(coefs)
            total = jnp.zeros_like(here)
            for member in range(2):
                face = 0.5 * (coef_here + around_z(coef_here, member))
                total = total + face * (around_z(here, member) - here)
            for member in (2, 3):
                face = 0.5 * (coef_here + middle(near(coefs, member)))
                total = total + face * (middle(near(cells, member)) - here)
            for place in (x + DEPTH - 1, x + DEPTH + 1):
                face = 0.5 * (coef_here + ext_a[2 + j, place, :, 0:lanes])
                total = total + face * (ext_a[j, place, :, 0:lanes] - here)
            flux.append(total + column(react_ref, x) * here * (1.0 - here * here))
            increment.append(here - column(prev_ref, x))
        near_part = [
            q_own[m][0] * flux[0] + q_own[m][1] * flux[1]
            - c_own[m][0] * increment[0] - c_own[m][1] * increment[1]
            for m in range(2)
        ]
        far_part = [
            q_far[m][0] * flux[0] + q_far[m][1] * flux[1]
            - c_far[m][0] * increment[0] - c_far[m][1] * increment[1]
            for m in range(2)
        ]

        def store():
            for m in range(2):
                part[m, x] = near_part[m]
                part_out[m, x] = far_part[m]

        return store

    chunk = rows // 4
    swap = []
    for at in range(4):
        for j in range(4):
            def put_a(x, plane):
                ext_a[j, x + DEPTH, :, lanes : 2 * lanes] = plane

            unpack(got_a[0, j], got_a[1, j], range(at * chunk, (at + 1) * chunk), put_a)
        planes(fluxes, at * chunk, (at + 1) * chunk, chunk)
        piece = pl.ds(at * chunk, chunk)
        one = copy(part_out.at[:, piece], part_in.at[:, piece], {"section": 1 - half})
        one.start()
        swap.append(one)

    receive(copies_b)

    for j in range(2):
        unpack_wide(got_b, j, ext_b)

    real_part = pick(pairs[0][0] / step_size, pairs[1][0] / step_size)
    coupling = pick(pairs[0][1] / step_size, pairs[1][1] / step_size)
    lane_at = lax.broadcasted_iota(jnp.int32, (depth_z, 2 * lanes), 1)
    inside = (
        (lane_at < lanes)
        | ((lane_at < lanes + DEPTH) & has_above)
        | ((lane_at >= 2 * lanes - DEPTH) & has_below)
    )
    keep = inside.astype(jnp.float32)

    def x_faces(x):
        face = 0.5 * (ext_b[0, x] + ext_b[0, x + 1])

        def store():
            face_x[x] = face

        return store

    planes(x_faces, 0, wide - 1, 4)

    def operator(x):
        coefs = ext_b[0, x]
        diag = real_part - ext_b[1, x] + face_x[x - 1] + face_x[x]
        sides = []
        for member in range(2):
            face = 0.5 * (coefs + around_z(coefs, member))
            diag = diag + face
            sides.append(jnp.where(has_next[member], face, 0.0))
        for member in (2, 3):
            face = 0.5 * (coefs + near(coefs, member))
            diag = diag + face
            sides.append(face)
        inside_x = ((x >= DEPTH) | has_left) & ((x < top) | has_right)
        scale = keep / (diag * diag + coupling * coupling)
        scale = jnp.where(inside_x, scale, 0.0)

        def store():
            for member in range(4):
                faces[member, x] = sides[member]
            alpha[x] = diag * scale
            beta[x] = coupling * scale

        return store

    planes(operator, 1, wide - 1, 2)

    def first_scaled(x):
        rhs = [part[m, x] + part_in[m, x] for m in range(2)]
        a, b = middle(alpha[x + DEPTH]), middle(beta[x + DEPTH])

        def store():
            for m in range(2):
                basis[0, m, x] = rhs[m]
            hist[0][0, x + DEPTH, :, 0:lanes] = a * rhs[0] - b * rhs[1]
            hist[0][1, x + DEPTH, :, 0:lanes] = b * rhs[0] + a * rhs[1]

        return store

    copies_c = []
    for at in range(4):
        swap[at].wait_recv()
        planes(first_scaled, at * chunk, (at + 1) * chunk, chunk)
        low = (at + 1) * chunk <= DEPTH
        one = copy(
            hist[0].at[:, pl.ds(DEPTH + at * chunk, chunk), :, own],
            hist[0].at[:, pl.ds(at * chunk + (top if low else DEPTH - rows), chunk), :, own],
            {"sx": left if low else right},
        )
        copies_c.append((has_left, has_right, one) if low else (has_right, has_left, one))
        start(copies_c[-1:])
    for j in range(2):
        pack(lambda x: hist[0][j, x + DEPTH, :, 0:lanes], pack_c.at[0, j], pack_c.at[1, j])
    more_c = strips(pack_c, got_c, True)
    start(more_c)
    copies_c = copies_c + more_c
    receive(copies_c)
    for j in range(2):
        unpack_wide(got_c, j, hist[0])

    for m in range(DEPTH - 1):
        def apply(x):
            around = []
            for field in range(2):
                cells = hist[m][field, x]
                total = face_x[x - 1] * hist[m][field, x - 1] + face_x[x] * hist[m][field, x + 1]
                for member in range(4):
                    total = total + faces[member, x] * near(cells, member)
                around.append(total)
            a, b = alpha[x], beta[x]
            scaled = [a * around[0] - b * around[1], b * around[0] + a * around[1]]

            def store():
                for field in range(2):
                    if m % 2 == 1:
                        powers[(m - 1) // 2][field, x] = middle(around[field])
                    hist[m + 1][field, x] = scaled[field]

            return store

        planes(apply, m + 1, wide - 1 - m, 4)

    index = [(i, j) for i in range(ITERS + 1) for j in range(i, ITERS + 1)]

    def last_apply(at, carry):
        totals = list(carry)
        ends = {}
        for step in range(4):
            at_x = 4 * at + step + DEPTH
            for field in range(2):
                cells = hist[DEPTH - 1][field, at_x]
                total = middle(face_x[at_x - 1]) * hist[DEPTH - 1][field, at_x - 1, :, 0:lanes]
                total = total + middle(face_x[at_x]) * hist[DEPTH - 1][field, at_x + 1, :, 0:lanes]
                for member in range(2):
                    total = total + middle(faces[member, at_x]) * near(middle(cells), member)
                for member in (2, 3):
                    total = total + middle(faces[member, at_x]) * middle(near(cells, member))
                ends[step, field] = total
        for step in range(4):
            for field in range(2):
                members_of = [basis[0, field, 4 * at + step]]
                members_of += [powers[k][field, 4 * at + step + DEPTH] for k in range(ITERS - 1)]
                members_of += [ends[step, field]]
                for pair, (i, j) in enumerate(index):
                    product = members_of[i] * members_of[j]
                    for r in range(0, depth_z, 8):
                        totals[pair] = totals[pair] + product[r : r + 8]
        return tuple(totals)

    zeros = tuple(jnp.zeros((8, lanes), jnp.float32) for pair in index)
    sums = lax.fori_loop(0, rows // 4, last_apply, zeros)
    square = jnp.concatenate(
        [jnp.sum(total, axis=0, keepdims=True) for total in sums]
        + [jnp.zeros((16 - len(index), lanes), jnp.float32)],
        axis=0,
    )
    diagonal = lax.broadcasted_iota(jnp.int32, (16, lanes), 0) == lax.broadcasted_iota(
        jnp.int32, (16, lanes), 1
    )
    square = jnp.where(diagonal, jnp.sum(square, axis=1, keepdims=True), 0.0)
    gram[0] = jnp.sum(square, axis=0, keepdims=True)

    def gram_copy(offset):
        return pltpu.make_async_remote_copy(
            src_ref=gram.at[0],
            dst_ref=gram.at[offset],
            send_sem=gram_send.at[offset],
            recv_sem=gram_recv.at[offset],
            device_id=member_at(offset),
            device_id_type=MESH,
        )

    def gram_start(offset, carry):
        gram_copy(offset).start()
        return carry

    def gram_take(offset, carry):
        gram_copy(offset).wait_recv()
        return carry

    def gram_release(offset, carry):
        gram_copy(offset).wait_send()
        return carry

    lax.fori_loop(1, members, gram_start, 0)
    release(copies_a)
    release(copies_b)
    release(copies_c)
    for one in swap:
        one.wait_send()
    lax.fori_loop(1, members, gram_take, 0)
    turn = [lax.rem(me - place + members, members) for place in range(members)]
    table = gram[turn[0]]
    for place in range(1, members):
        table = table + gram[turn[place]]
    table = jnp.where(diagonal, jnp.broadcast_to(table, (16, lanes)), 0.0)
    table = jnp.sum(table, axis=1, keepdims=True)
    entry = {}
    for at, (i, j) in enumerate(index):
        entry[i, j] = entry[j, i] = table[at : at + 1, :]

    weights = {0: jnp.ones((1, 1), jnp.float32)}
    gains = {}
    for sweep in range(ITERS):
        image = {}
        for j in range(sweep + 2):
            if j in weights and j - 1 in weights:
                image[j] = weights[j] - weights[j - 1]
            elif j in weights:
                image[j] = weights[j]
            else:
                image[j] = -weights[j - 1]
        against = {
            j: functools.reduce(jnp.add, [image[i] * entry[i, j] for i in image]) for j in image
        }
        numerator = functools.reduce(jnp.add, [against[j] * weights[j] for j in weights])
        denominator = functools.reduce(jnp.add, [against[j] * image[j] for j in image])
        step = numerator / (denominator + tiny_value)
        for j in weights:
            gains[j] = gains[j] + step * weights[j] if j in gains else step * weights[j]
        weights = {
            j: (weights[j] - step * image[j]) if j in weights else -step * image[j] for j in image
        }

    p_own = [[pick(p_table[j][m], p_table[2 + j][2 + m]) for m in range(2)] for j in range(2)]
    p_far = [[pick(p_table[2 + j][m], p_table[j][2 + m]) for m in range(2)] for j in range(2)]
    gain_at = [jnp.broadcast_to(gains[k], (depth_z, lanes)) for k in range(ITERS)]

    def correct(x):
        fix = []
        for field in range(2):
            total = None
            for k in range(ITERS):
                search = (
                    hist[2 * k][field, x + DEPTH, :, 0:lanes]
                    + hist[2 * k + 1][field, x + DEPTH, :, 0:lanes]
                )
                total = gain_at[k] * search if total is None else total + gain_at[k] * search
            fix.append(total)
        base = [ext_a[j, x + DEPTH, :, 0:lanes] for j in range(2)]

        def store():
            for j in range(2):
                corr_out[j, x] = p_far[j][0] * fix[0] + p_far[j][1] * fix[1]
                part[j, x] = base[j] + p_own[j][0] * fix[0] + p_own[j][1] * fix[1]

        return store

    final = []
    for at in range(4):
        planes(correct, at * chunk, (at + 1) * chunk, 4)
        piece = pl.ds(at * chunk, chunk)
        one = copy(corr_out.at[:, piece], corr_in.at[:, piece], {"section": 1 - half})
        one.start()
        final.append(one)
    for at in range(4):
        final[at].wait_recv()

        for x in range(at * chunk, (at + 1) * chunk):
            for j in range(2):
                out_ref[j, pl.ds(x, depth_z, stride=rows), :] = part[j, x] + corr_in[j, x]
    for one in final:
        one.wait_send()
    lax.fori_loop(1, members, gram_release, 0)


def solution(mesh):
    sx_count, sy_count = mesh.shape["sx"], mesh.shape["sy"]
    tableau, inverse, eigen_basis, basis_inverse, pairs = radau_tables()
    shift_table = table_product(basis_inverse, inverse)
    shift_table = [[v / step_size for v in row_values] for row_values in shift_table]
    tables = (basis_inverse, shift_table, eigen_basis, pairs)

    def body(previous, sections, diffusivity, reaction):
        depth_z, rows, lanes = previous.shape
        wide = rows + 2 * DEPTH
        f32 = jnp.float32
        vmem = pltpu.VMEM
        ext = (wide, depth_z, 2 * lanes)
        block = (2, rows, depth_z, lanes)
        flat = (depth_z * rows, lanes)
        members = sx_count * sy_count
        return pl.pallas_call(
            functools.partial(kernel, sx_count, sy_count, tables),
            out_shape=jax.ShapeDtypeStruct((2,) + flat, f32),
            in_specs=[pl.BlockSpec(memory_space=pltpu.HBM)] * 4,
            out_specs=pl.BlockSpec(memory_space=pltpu.VMEM),
            scratch_shapes=[
                vmem(flat, f32),
                vmem((2,) + flat, f32),
                vmem(flat, f32),
                vmem(flat, f32),
                vmem((4,) + ext, f32),
                vmem((2,) + ext, f32),
                vmem((4,) + ext, f32),
                vmem(ext, f32),
                vmem(ext, f32),
                vmem(ext, f32),
                *[vmem((2,) + ext, f32) for m in range(DEPTH)],
                *[vmem((2, wide, depth_z, lanes), f32) for m in range(ITERS - 1)],
                vmem((1,) + block, f32),
                vmem(block, f32),
                vmem(block, f32),
                vmem(block, f32),
                vmem(block, f32),
                vmem(block, f32),
                vmem((2, 4, depth_z, lanes), f32),
                vmem((2, 4, depth_z, lanes), f32),
                vmem((2, 2, depth_z, lanes), f32),
                vmem((2, 3, 2, depth_z, lanes), f32),
                vmem((2, 2, depth_z, lanes), f32),
                vmem((2, 3, 2, depth_z, lanes), f32),
                vmem((members, 1, lanes), f32),
                pltpu.SemaphoreType.DMA((4,)),
                pltpu.SemaphoreType.DMA((40,)),
                pltpu.SemaphoreType.DMA((40,)),
                pltpu.SemaphoreType.DMA((members,)),
                pltpu.SemaphoreType.DMA((members,)),
            ],
            compiler_params=pltpu.CompilerParams(
                collective_id=0, has_side_effects=True, vmem_limit_bytes=48 * 1024 * 1024
            ),
        )(
            *(
                pltpu.with_memory_space_constraint(cells, pltpu.HBM)
                for cells in (
                    previous.reshape(flat),
                    sections.reshape((2,) + flat),
                    diffusivity.reshape(flat),
                    reaction.reshape(flat),
                )
            )
        ).reshape(sections.shape)

    in_specs = (
        P(None, "sx", "sy"),
        P("section", None, "sx", "sy"),
        P(None, "sx", "sy"),
        P(None, "sx", "sy"),
    )
    out_specs = P("section", None, "sx", "sy")
    return jax.shard_map(body, mesh=mesh, in_specs=in_specs, out_specs=out_specs, check_vma=False)
```

```python
import functools

import jax
import jax.numpy as jnp
from jax import lax
from jax.experimental import pallas as pl
from jax.experimental.pallas import tpu as pltpu
from jax.sharding import PartitionSpec as P

ITERS = 4
DEPTH = 2 * ITERS
MESH = pl.DeviceIdType.MESH

step_size = 1.0
tiny_value = 1e-06


def invert_table(matrix):
    order_n = len(matrix)
    augmented = [
        list(matrix[r]) + [1.0 if c == r else 0.0 for c in range(order_n)] for r in range(order_n)
    ]
    for col in range(order_n):
        pivot_row = max(range(col, order_n), key=lambda r: abs(augmented[r][col]))
        augmented[col], augmented[pivot_row] = (augmented[pivot_row], augmented[col])
        leading = augmented[col][col]
        augmented[col] = [v / leading for v in augmented[col]]
        for r in range(order_n):
            if r != col:
                factor = augmented[r][col]
                augmented[r] = [a - factor * b for a, b in zip(augmented[r], augmented[col])]
    return [row_values[order_n:] for row_values in augmented]


def table_product(left, right):
    return [
        [sum((left[i][k] * right[k][j] for k in range(len(right)))) for j in range(len(right[0]))]
        for i in range(len(left))
    ]


def pair_add(first, second):
    return (first[0] + second[0], first[1] + second[1])


def pair_sub(first, second):
    return (first[0] - second[0], first[1] - second[1])


def pair_mul(first, second):
    return (
        first[0] * second[0] - first[1] * second[1],
        first[0] * second[1] + first[1] * second[0],
    )


def pair_div(first, second):
    scale_sq = second[0] * second[0] + second[1] * second[1]
    return (
        (first[0] * second[0] + first[1] * second[1]) / scale_sq,
        (first[1] * second[0] - first[0] * second[1]) / scale_sq,
    )


def quartic_value(point):
    return (((210.0 * point - 480.0) * point + 360.0) * point - 96.0) * point + 6.0


def bisect_root(lower, upper):
    for count in range(200):
        middle = 0.5 * (lower + upper)
        if (quartic_value(lower) < 0.0) == (quartic_value(middle) < 0.0):
            lower = middle
        else:
            upper = middle
    return 0.5 * (lower + upper)


def radau_tables():
    abscissae = []
    grid_steps = 4000
    for m in range(grid_steps):
        lower = 0.999 * m / grid_steps
        upper = 0.999 * (m + 1) / grid_steps
        if (quartic_value(lower) < 0.0) != (quartic_value(upper) < 0.0):
            abscissae.append(bisect_root(lower, upper))
    abscissae.append(1.0)
    vander = [[abscissae[j] ** k for k in range(4)] for j in range(4)]
    moments = [[abscissae[i] ** (k + 1) / (k + 1) for k in range(4)] for i in range(4)]
    tableau = table_product(moments, invert_table(vander))
    inverse = invert_table(tableau)
    running = [list(row_values) for row_values in inverse]
    coeffs = []
    for k in range(1, 5):
        trace_value = sum((running[i][i] for i in range(4)))
        coeffs.append(-trace_value / k)
        shifted_table = [
            [running[i][j] + (coeffs[-1] if i == j else 0.0) for j in range(4)] for i in range(4)
        ]
        running = table_product(inverse, shifted_table)
    start_point = (0.4, 0.9)
    estimates = [(1.0, 0.0)]
    for k in range(3):
        estimates.append(pair_mul(estimates[-1], start_point))
    for count in range(500):
        for i in range(4):
            value = (1.0, 0.0)
            for coef_value in coeffs:
                value = pair_add(pair_mul(value, estimates[i]), (coef_value, 0.0))
            denom = (1.0, 0.0)
            for j in range(4):
                if j != i:
                    denom = pair_mul(denom, pair_sub(estimates[i], estimates[j]))
            estimates[i] = pair_sub(estimates[i], pair_div(value, denom))
    chosen = [m for m in range(4) if estimates[m][1] > 0.0]
    ranking = sorted(chosen, key=lambda m: -estimates[m][1])
    columns = []
    pairs = []
    for m in ranking:
        eigen_pair = estimates[m]
        system = [
            [
                (
                    inverse[i][j] - (eigen_pair[0] if i == j else 0.0),
                    -(eigen_pair[1] if i == j else 0.0),
                )
                for j in range(4)
            ]
            for i in range(3)
        ]
        rows_left = [
            [system[i][j] for j in range(3)] + [(-system[i][3][0], -system[i][3][1])]
            for i in range(3)
        ]
        for col in range(3):
            pivot_row = max(
                range(col, 3), key=lambda r: rows_left[r][col][0] ** 2 + rows_left[r][col][1] ** 2
            )
            rows_left[col], rows_left[pivot_row] = (rows_left[pivot_row], rows_left[col])
            leading = rows_left[col][col]
            rows_left[col] = [pair_div(v, leading) for v in rows_left[col]]
            for r in range(3):
                if r != col:
                    factor = rows_left[r][col]
                    rows_left[r] = [
                        pair_sub(a, pair_mul(factor, b))
                        for a, b in zip(rows_left[r], rows_left[col])
                    ]
        vector = [rows_left[i][3] for i in range(3)] + [(1.0, 0.0)]
        columns.append([v[0] for v in vector])
        columns.append([v[1] for v in vector])
        pairs.append((eigen_pair[0], eigen_pair[1]))
    eigen_basis = [[columns[j][i] for j in range(4)] for i in range(4)]
    basis_inverse = invert_table(eigen_basis)
    return (tableau, inverse, eigen_basis, basis_inverse, pairs)


def near(plane, member):
    if member == 0:
        return pltpu.roll(plane, plane.shape[0] - 1, 0)
    if member == 1:
        return pltpu.roll(plane, 1, 0)
    if member == 2:
        return pltpu.roll(plane, plane.shape[1] - 1, 1)
    return pltpu.roll(plane, 1, 1)


def kernel(
    sx_count, sy_count, tables,
    prev_any, sec_any, diff_any, react_any, out_ref,
    prev_ref, sec_ref, diff_ref, react_ref,
    ext_a, ext_b, faces, face_x, alpha, beta, *rest,
):
    hist, rest = rest[:DEPTH], rest[DEPTH:]
    powers, rest = rest[: ITERS - 1], rest[ITERS - 1 :]
    (
    basis, part, part_out, part_in, corr_out, corr_in,
    pack_a, got_a, pack_b, got_b, pack_c, got_c, gram, load_sem,
    send_sem, recv_sem, gram_send, gram_recv,
    ) = rest
    depth_z, lanes = ext_a.shape[2], prev_ref.shape[1]
    rows = prev_ref.shape[0] // depth_z
    top = DEPTH + rows
    group = rows
    sx, sy, half = lax.axis_index("sx"), lax.axis_index("sy"), lax.axis_index("section")
    q_table, c_table, p_table, pairs = tables

    def pick(first, second):
        return jnp.where(half == 0, jnp.float32(first), jnp.float32(second))

    barrier = pltpu.get_barrier_semaphore()
    members = sx_count * sy_count
    me = sx * sy_count + sy

    def member_at(offset):
        other = lax.rem(me + offset, members)
        return {"sx": other // sy_count, "sy": lax.rem(other, sy_count)}

    def greet(offset, carry):
        pl.semaphore_signal(barrier, inc=1, device_id=member_at(offset), device_id_type=MESH)
        return carry

    lax.fori_loop(1, members, greet, 0)
    pl.semaphore_signal(barrier, inc=1, device_id={"section": 1 - half}, device_id_type=MESH)

    loads = [
        pltpu.make_async_copy(source, target, load_sem.at[at])
        for at, (source, target) in enumerate((
            (sec_any, sec_ref), (diff_any, diff_ref), (prev_any, prev_ref), (react_any, react_ref),
        ))
    ]
    for one in loads:
        one.start()

    wide = rows + 2 * DEPTH
    left, right = lax.rem(sx + sx_count - 1, sx_count), lax.rem(sx + 1, sx_count)
    below, above = lax.rem(sy + sy_count - 1, sy_count), lax.rem(sy + 1, sy_count)
    has_left, has_right = sx > 0, sx < sx_count - 1
    has_below, has_above = sy > 0, sy < sy_count - 1

    def clear(missing, *views):
        def run():
            for view in views:
                view[...] = jnp.zeros(view.shape, jnp.float32)

        pl.when(jnp.logical_not(missing))(run)

    clear(has_left, ext_a.at[:, DEPTH - 1, :, 0:lanes], ext_b.at[:, 0:DEPTH, :, 0:lanes],
          hist[0].at[:, 0:DEPTH, :, 0:lanes])
    clear(has_right, ext_a.at[:, top, :, 0:lanes], ext_b.at[:, top:wide, :, 0:lanes],
          hist[0].at[:, top:wide, :, 0:lanes])
    for side, there in ((0, has_above), (1, has_below)):
        clear(there, got_a.at[side], got_b.at[side, 1], got_c.at[side, 1])
        clear(there & has_left, got_b.at[side, 0], got_c.at[side, 0])
        clear(there & has_right, got_b.at[side, 2], got_c.at[side, 2])

    lane_group = lax.broadcasted_iota(jnp.int32, (depth_z, lanes), 1) // DEPTH

    def pack(plane_of, low, high):
        down = jnp.zeros((depth_z, lanes), jnp.float32)
        up = jnp.zeros((depth_z, lanes), jnp.float32)
        for x in range(rows):
            plane = plane_of(x)
            if x > 0:
                plane = pltpu.roll(plane, DEPTH * x, 1)
            down = jnp.where(lane_group == x, plane, down)
            up = jnp.where(lane_group == (x + group - 1) % group, plane, up)
        low[...] = down
        high[...] = up

    def unpack(from_high, from_low, members_x, store):
        for x in members_x:
            mixed = jnp.where(
                lane_group == x,
                from_high,
                jnp.where(lane_group == (x + group - 1) % group, from_low, 0.0),
            )
            if x > 0:
                mixed = pltpu.roll(mixed, lanes - DEPTH * x, 1)
            store(x, mixed)

    def unpack_wide(got, j, target):
        for place, members_x in ((0, range(rows - DEPTH, rows)), (1, range(rows)), (2, range(DEPTH))):
            first = (DEPTH - rows, DEPTH, top)[place]

            def store(x, plane):
                target[j, first + x, :, lanes : 2 * lanes] = plane

            unpack(got[0, place, j], got[1, place, j], members_x, store)

    def column(ref, x):
        return ref[pl.ds(x, depth_z, stride=rows), :]

    def planes(fn, least, most, batch):
        def several(first, count):
            stores = [fn(first + step) for step in range(count)]
            for store in stores:
                store()

        full, left_over = (most - least) // batch, (most - least) % batch
        if full == 1:
            several(least, batch)
        else:
            def turn(at, carry):
                several(least + at * batch, batch)
                return carry

            lax.fori_loop(0, full, turn, 0)
        if left_over:
            several(most - left_over, left_over)

    def section_coefs(x):
        diffusivity = column(diff_ref, x)
        cells = [column(sec_ref.at[j], x) for j in range(2)]
        coefs = [diffusivity * (1.0 + 0.5 * jnp.tanh(cells[j])) for j in range(2)]

        def store():
            for j in range(2):
                ext_a[j, x + DEPTH, :, 0:lanes] = cells[j]
                ext_a[2 + j, x + DEPTH, :, 0:lanes] = coefs[j]

        return store

    def frozen_coefs(x):
        before = column(prev_ref, x)
        coef = column(diff_ref, x) * (1.0 + 0.5 * jnp.tanh(before))
        slope = column(react_ref, x) * (1.0 - 3.0 * before * before)

        def store():
            ext_b[0, x + DEPTH, :, 0:lanes] = coef
            ext_b[1, x + DEPTH, :, 0:lanes] = slope

        return store

    for one in loads[:2]:
        one.wait()
    planes(section_coefs, 0, rows, 4)
    for j in range(4):
        pack(lambda x: ext_a[j, x + DEPTH, :, 0:lanes], pack_a.at[0, j], pack_a.at[1, j])

    pl.semaphore_wait(barrier, members)

    used = [0]

    def copy(source, target, device):
        at = used[0]
        used[0] += 1
        return pltpu.make_async_remote_copy(
            src_ref=source,
            dst_ref=target,
            send_sem=send_sem.at[at],
            recv_sem=recv_sem.at[at],
            device_id=device,
            device_id_type=MESH,
        )

    own = pl.ds(0, lanes)
    low_rows, high_rows = pl.ds(0, DEPTH), pl.ds(top, DEPTH)

    def slabs(low_source, high_source, target):
        return [
            (has_left, has_right, copy(low_source, target(high_rows), {"sx": left})),
            (has_right, has_left, copy(high_source, target(low_rows), {"sx": right})),
        ]

    def strips(packed, got, corners):
        result = []
        for side, device, out_ok, in_ok in (
            (0, below, has_below, has_above),
            (1, above, has_above, has_below),
        ):
            middle = got.at[side, 1] if corners else got.at[side]
            result.append((out_ok, in_ok, copy(packed.at[side], middle, {"sy": device})))
            if corners:
                result.append((
                    out_ok & has_left,
                    in_ok & has_right,
                    copy(
                        packed.at[side],
                        got.at[side, 2],
                        {"sx": left, "sy": device},
                    ),
                ))
                result.append((
                    out_ok & has_right,
                    in_ok & has_left,
                    copy(
                        packed.at[side],
                        got.at[side, 0],
                        {"sx": right, "sy": device},
                    ),
                ))
        return result

    def start(copies):
        for out_ok, in_ok, one in copies:
            pl.when(out_ok)(one.start)

    def receive(copies):
        for out_ok, in_ok, one in copies:
            pl.when(in_ok)(one.wait_recv)

    def release(copies):
        for out_ok, in_ok, one in copies:
            pl.when(out_ok)(one.wait_send)

    copies_a = strips(pack_a, got_a, False)
    edge = pl.ds(top, 1), pl.ds(DEPTH - 1, 1)
    copies_a.append((
        has_left,
        has_right,
        copy(
            ext_a.at[:, pl.ds(DEPTH, 1), :, own],
            ext_a.at[:, edge[0], :, own],
            {"sx": left},
        ),
    ))
    copies_a.append((
        has_right,
        has_left,
        copy(
            ext_a.at[:, pl.ds(top - 1, 1), :, own],
            ext_a.at[:, edge[1], :, own],
            {"sx": right},
        ),
    ))
    start(copies_a)
    for one in loads[2:]:
        one.wait()
    planes(frozen_coefs, 0, rows, 4)
    for j in range(2):
        pack(lambda x: ext_b[j, x + DEPTH, :, 0:lanes], pack_b.at[0, j], pack_b.at[1, j])
    copies_b = strips(pack_b, got_b, True)
    copies_b += slabs(
        ext_b.at[:, pl.ds(DEPTH, DEPTH), :, own],
        ext_b.at[:, pl.ds(top - DEPTH, DEPTH), :, own],
        lambda where: ext_b.at[:, where, :, own],
    )
    start(copies_b)

    receive(copies_a)

    q_own = [[pick(q_table[m][j], q_table[2 + m][2 + j]) for j in range(2)] for m in range(2)]
    q_far = [[pick(q_table[2 + m][j], q_table[m][2 + j]) for j in range(2)] for m in range(2)]
    c_own = [[pick(c_table[m][j], c_table[2 + m][2 + j]) for j in range(2)] for m in range(2)]
    c_far = [[pick(c_table[2 + m][j], c_table[m][2 + j]) for j in range(2)] for m in range(2)]

    def middle(plane):
        return plane[:, 0:lanes]

    z_at = lax.broadcasted_iota(jnp.int32, (depth_z, 2 * lanes), 0)
    has_next = (z_at < depth_z - 1, z_at > 0)

    def around_z(plane, member):
        mask = has_next[member][:, 0 : plane.shape[1]]
        return jnp.where(mask, near(plane, member), 0.0)

    def fluxes(x):
        flux, increment = [], []
        for j in range(2):
            cells, coefs = ext_a[j, x + DEPTH], ext_a[2 + j, x + DEPTH]
            here, coef_here = middle(cells), middle(coefs)
            total = jnp.zeros_like(here)
            for member in range(2):
                face = 0.5 * (coef_here + around_z(coef_here, member))
                total = total + face * (around_z(here, member) - here)
            for member in (2, 3):
                face = 0.5 * (coef_here + middle(near(coefs, member)))
                total = total + face * (middle(near(cells, member)) - here)
            for place in (x + DEPTH - 1, x + DEPTH + 1):
                face = 0.5 * (coef_here + ext_a[2 + j, place, :, 0:lanes])
                total = total + face * (ext_a[j, place, :, 0:lanes] - here)
            flux.append(total + column(react_ref, x) * here * (1.0 - here * here))
            increment.append(here - column(prev_ref, x))
        near_part = [
            q_own[m][0] * flux[0] + q_own[m][1] * flux[1]
            - c_own[m][0] * increment[0] - c_own[m][1] * increment[1]
            for m in range(2)
        ]
        far_part = [
            q_far[m][0] * flux[0] + q_far[m][1] * flux[1]
            - c_far[m][0] * increment[0] - c_far[m][1] * increment[1]
            for m in range(2)
        ]

        def store():
            for m in range(2):
                part[m, x] = near_part[m]
                part_out[m, x] = far_part[m]

        return store

    chunk = rows // 4
    swap = []
    for at in range(4):
        for j in range(4):
            def put_a(x, plane):
                ext_a[j, x + DEPTH, :, lanes : 2 * lanes] = plane

            unpack(got_a[0, j], got_a[1, j], range(at * chunk, (at + 1) * chunk), put_a)
        planes(fluxes, at * chunk, (at + 1) * chunk, chunk)
        piece = pl.ds(at * chunk, chunk)
        one = copy(part_out.at[:, piece], part_in.at[:, piece], {"section": 1 - half})
        one.start()
        swap.append(one)

    receive(copies_b)

    for j in range(2):
        unpack_wide(got_b, j, ext_b)

    real_part = pick(pairs[0][0] / step_size, pairs[1][0] / step_size)
    coupling = pick(pairs[0][1] / step_size, pairs[1][1] / step_size)
    lane_at = lax.broadcasted_iota(jnp.int32, (depth_z, 2 * lanes), 1)
    inside = (
        (lane_at < lanes)
        | ((lane_at < lanes + DEPTH) & has_above)
        | ((lane_at >= 2 * lanes - DEPTH) & has_below)
    )
    keep = inside.astype(jnp.float32)

    def x_faces(x):
        face = 0.5 * (ext_b[0, x] + ext_b[0, x + 1])

        def store():
            face_x[x] = face

        return store

    planes(x_faces, 0, wide - 1, 4)

    def operator(x):
        coefs = ext_b[0, x]
        diag = real_part - ext_b[1, x] + face_x[x - 1] + face_x[x]
        sides = []
        for member in range(2):
            face = 0.5 * (coefs + around_z(coefs, member))
            diag = diag + face
            sides.append(jnp.where(has_next[member], face, 0.0))
        for member in (2, 3):
            face = 0.5 * (coefs + near(coefs, member))
            diag = diag + face
            sides.append(face)
        inside_x = ((x >= DEPTH) | has_left) & ((x < top) | has_right)
        scale = keep / (diag * diag + coupling * coupling)
        scale = jnp.where(inside_x, scale, 0.0)

        def store():
            for member in range(4):
                faces[member, x] = sides[member]
            alpha[x] = diag * scale
            beta[x] = coupling * scale

        return store

    planes(operator, 1, wide - 1, 2)

    def first_scaled(x):
        rhs = [part[m, x] + part_in[m, x] for m in range(2)]
        a, b = middle(alpha[x + DEPTH]), middle(beta[x + DEPTH])

        def store():
            for m in range(2):
                basis[0, m, x] = rhs[m]
            hist[0][0, x + DEPTH, :, 0:lanes] = a * rhs[0] - b * rhs[1]
            hist[0][1, x + DEPTH, :, 0:lanes] = b * rhs[0] + a * rhs[1]

        return store

    copies_c = []
    for at in range(4):
        swap[at].wait_recv()
        planes(first_scaled, at * chunk, (at + 1) * chunk, chunk)
        low = (at + 1) * chunk <= DEPTH
        one = copy(
            hist[0].at[:, pl.ds(DEPTH + at * chunk, chunk), :, own],
            hist[0].at[:, pl.ds(at * chunk + (top if low else DEPTH - rows), chunk), :, own],
            {"sx": left if low else right},
        )
        copies_c.append((has_left, has_right, one) if low else (has_right, has_left, one))
        start(copies_c[-1:])
    for j in range(2):
        pack(lambda x: hist[0][j, x + DEPTH, :, 0:lanes], pack_c.at[0, j], pack_c.at[1, j])
    more_c = strips(pack_c, got_c, True)
    start(more_c)
    copies_c = copies_c + more_c
    receive(copies_c)
    for j in range(2):
        unpack_wide(got_c, j, hist[0])

    for m in range(DEPTH - 1):
        def apply(x):
            around = []
            for field in range(2):
                cells = hist[m][field, x]
                total = face_x[x - 1] * hist[m][field, x - 1] + face_x[x] * hist[m][field, x + 1]
                for member in range(4):
                    total = total + faces[member, x] * near(cells, member)
                around.append(total)
            a, b = alpha[x], beta[x]
            scaled = [a * around[0] - b * around[1], b * around[0] + a * around[1]]

            def store():
                for field in range(2):
                    if m % 2 == 1:
                        powers[(m - 1) // 2][field, x] = middle(around[field])
                    hist[m + 1][field, x] = scaled[field]

            return store

        planes(apply, m + 1, wide - 1 - m, 6)

    index = [(i, j) for i in range(ITERS + 1) for j in range(i, ITERS + 1)]

    def last_apply(at, carry):
        totals = list(carry)
        ends = {}
        for step in range(4):
            at_x = 4 * at + step + DEPTH
            for field in range(2):
                cells = hist[DEPTH - 1][field, at_x]
                total = middle(face_x[at_x - 1]) * hist[DEPTH - 1][field, at_x - 1, :, 0:lanes]
                total = total + middle(face_x[at_x]) * hist[DEPTH - 1][field, at_x + 1, :, 0:lanes]
                for member in range(2):
                    total = total + middle(faces[member, at_x]) * near(middle(cells), member)
                for member in (2, 3):
                    total = total + middle(faces[member, at_x]) * middle(near(cells, member))
                ends[step, field] = total
        for step in range(4):
            for field in range(2):
                members_of = [basis[0, field, 4 * at + step]]
                members_of += [powers[k][field, 4 * at + step + DEPTH] for k in range(ITERS - 1)]
                members_of += [ends[step, field]]
                for pair, (i, j) in enumerate(index):
                    product = members_of[i] * members_of[j]
                    for r in range(0, depth_z, 8):
                        totals[pair] = totals[pair] + product[r : r + 8]
        return tuple(totals)

    zeros = tuple(jnp.zeros((8, lanes), jnp.float32) for pair in index)
    sums = lax.fori_loop(0, rows // 4, last_apply, zeros)
    square = jnp.concatenate(
        [jnp.sum(total, axis=0, keepdims=True) for total in sums]
        + [jnp.zeros((16 - len(index), lanes), jnp.float32)],
        axis=0,
    )
    diagonal = lax.broadcasted_iota(jnp.int32, (16, lanes), 0) == lax.broadcasted_iota(
        jnp.int32, (16, lanes), 1
    )
    square = jnp.where(diagonal, jnp.sum(square, axis=1, keepdims=True), 0.0)
    gram[0] = jnp.sum(square, axis=0, keepdims=True)

    def gram_copy(offset):
        return pltpu.make_async_remote_copy(
            src_ref=gram.at[0],
            dst_ref=gram.at[offset],
            send_sem=gram_send.at[offset],
            recv_sem=gram_recv.at[offset],
            device_id=member_at(offset),
            device_id_type=MESH,
        )

    def gram_start(offset, carry):
        gram_copy(offset).start()
        return carry

    def gram_take(offset, carry):
        gram_copy(offset).wait_recv()
        return carry

    def gram_release(offset, carry):
        gram_copy(offset).wait_send()
        return carry

    lax.fori_loop(1, members, gram_start, 0)
    release(copies_a)
    release(copies_b)
    release(copies_c)
    for one in swap:
        one.wait_send()
    lax.fori_loop(1, members, gram_take, 0)
    turn = [lax.rem(me - place + members, members) for place in range(members)]
    table = gram[turn[0]]
    for place in range(1, members):
        table = table + gram[turn[place]]
    table = jnp.where(diagonal, jnp.broadcast_to(table, (16, lanes)), 0.0)
    table = jnp.sum(table, axis=1, keepdims=True)
    entry = {}
    for at, (i, j) in enumerate(index):
        entry[i, j] = entry[j, i] = table[at : at + 1, :]

    weights = {0: jnp.ones((1, 1), jnp.float32)}
    gains = {}
    for sweep in range(ITERS):
        image = {}
        for j in range(sweep + 2):
            if j in weights and j - 1 in weights:
                image[j] = weights[j] - weights[j - 1]
            elif j in weights:
                image[j] = weights[j]
            else:
                image[j] = -weights[j - 1]
        against = {
            j: functools.reduce(jnp.add, [image[i] * entry[i, j] for i in image]) for j in image
        }
        numerator = functools.reduce(jnp.add, [against[j] * weights[j] for j in weights])
        denominator = functools.reduce(jnp.add, [against[j] * image[j] for j in image])
        step = numerator / (denominator + tiny_value)
        for j in weights:
            gains[j] = gains[j] + step * weights[j] if j in gains else step * weights[j]
        weights = {
            j: (weights[j] - step * image[j]) if j in weights else -step * image[j] for j in image
        }

    p_own = [[pick(p_table[j][m], p_table[2 + j][2 + m]) for m in range(2)] for j in range(2)]
    p_far = [[pick(p_table[2 + j][m], p_table[j][2 + m]) for m in range(2)] for j in range(2)]
    gain_at = [jnp.broadcast_to(gains[k], (depth_z, lanes)) for k in range(ITERS)]

    def correct(x):
        fix = []
        for field in range(2):
            total = None
            for k in range(ITERS):
                search = (
                    hist[2 * k][field, x + DEPTH, :, 0:lanes]
                    + hist[2 * k + 1][field, x + DEPTH, :, 0:lanes]
                )
                total = gain_at[k] * search if total is None else total + gain_at[k] * search
            fix.append(total)
        base = [ext_a[j, x + DEPTH, :, 0:lanes] for j in range(2)]

        def store():
            for j in range(2):
                corr_out[j, x] = p_far[j][0] * fix[0] + p_far[j][1] * fix[1]
                part[j, x] = base[j] + p_own[j][0] * fix[0] + p_own[j][1] * fix[1]

        return store

    final = []
    for at in range(4):
        planes(correct, at * chunk, (at + 1) * chunk, 4)
        piece = pl.ds(at * chunk, chunk)
        one = copy(corr_out.at[:, piece], corr_in.at[:, piece], {"section": 1 - half})
        one.start()
        final.append(one)
    for at in range(4):
        final[at].wait_recv()

        for x in range(at * chunk, (at + 1) * chunk):
            for j in range(2):
                out_ref[j, pl.ds(x, depth_z, stride=rows), :] = part[j, x] + corr_in[j, x]
    for one in final:
        one.wait_send()
    lax.fori_loop(1, members, gram_release, 0)


def solution(mesh):
    sx_count, sy_count = mesh.shape["sx"], mesh.shape["sy"]
    tableau, inverse, eigen_basis, basis_inverse, pairs = radau_tables()
    shift_table = table_product(basis_inverse, inverse)
    shift_table = [[v / step_size for v in row_values] for row_values in shift_table]
    tables = (basis_inverse, shift_table, eigen_basis, pairs)

    def body(previous, sections, diffusivity, reaction):
        depth_z, rows, lanes = previous.shape
        wide = rows + 2 * DEPTH
        f32 = jnp.float32
        vmem = pltpu.VMEM
        ext = (wide, depth_z, 2 * lanes)
        block = (2, rows, depth_z, lanes)
        flat = (depth_z * rows, lanes)
        members = sx_count * sy_count
        return pl.pallas_call(
            functools.partial(kernel, sx_count, sy_count, tables),
            out_shape=jax.ShapeDtypeStruct((2,) + flat, f32),
            in_specs=[pl.BlockSpec(memory_space=pltpu.HBM)] * 4,
            out_specs=pl.BlockSpec(memory_space=pltpu.VMEM),
            scratch_shapes=[
                vmem(flat, f32),
                vmem((2,) + flat, f32),
                vmem(flat, f32),
                vmem(flat, f32),
                vmem((4,) + ext, f32),
                vmem((2,) + ext, f32),
                vmem((4,) + ext, f32),
                vmem(ext, f32),
                vmem(ext, f32),
                vmem(ext, f32),
                *[vmem((2,) + ext, f32) for m in range(DEPTH)],
                *[vmem((2, wide, depth_z, lanes), f32) for m in range(ITERS - 1)],
                vmem((1,) + block, f32),
                vmem(block, f32),
                vmem(block, f32),
                vmem(block, f32),
                vmem(block, f32),
                vmem(block, f32),
                vmem((2, 4, depth_z, lanes), f32),
                vmem((2, 4, depth_z, lanes), f32),
                vmem((2, 2, depth_z, lanes), f32),
                vmem((2, 3, 2, depth_z, lanes), f32),
                vmem((2, 2, depth_z, lanes), f32),
                vmem((2, 3, 2, depth_z, lanes), f32),
                vmem((members, 1, lanes), f32),
                pltpu.SemaphoreType.DMA((4,)),
                pltpu.SemaphoreType.DMA((40,)),
                pltpu.SemaphoreType.DMA((40,)),
                pltpu.SemaphoreType.DMA((members,)),
                pltpu.SemaphoreType.DMA((members,)),
            ],
            compiler_params=pltpu.CompilerParams(
                collective_id=0, has_side_effects=True, vmem_limit_bytes=48 * 1024 * 1024
            ),
        )(
            *(
                pltpu.with_memory_space_constraint(cells, pltpu.HBM)
                for cells in (
                    previous.reshape(flat),
                    sections.reshape((2,) + flat),
                    diffusivity.reshape(flat),
                    reaction.reshape(flat),
                )
            )
        ).reshape(sections.shape)

    in_specs = (
        P(None, "sx", "sy"),
        P("section", None, "sx", "sy"),
        P(None, "sx", "sy"),
        P(None, "sx", "sy"),
    )
    out_specs = P("section", None, "sx", "sy")
    return jax.shard_map(body, mesh=mesh, in_specs=in_specs, out_specs=out_specs, check_vma=False)
```
